32 devices in a mesh: batch: 4 (over y, x), seq: 4 (over z), mp: 2 (over core).
Axes of the slice: x: 2, y: 2, z: 4, core: 2. Of those that a mesh axis runs over, the one named last changes fastest.
Arguments:
- tokens_in: bfloat16 [24, 1024, 768], P(('batch', 'mp'), 'seq'), may hold values from -6 to 6
- prefix: int32 [24], P(('batch', 'mp')), may hold values from 0 to 1023
- mask_bits: int32 [24, 1024], P(('batch', 'mp'), 'seq'), may hold values 0 or 1
- timestep: int32 [24], P(('batch', 'mp')), may hold values from 0 to 999
- mask_embed: bfloat16 [768], replicated, may hold values from -6 to 6
- w_ada: bfloat16 [128, 4608], replicated, may hold values from -0.5 to 0.5
- b_ada: bfloat16 [4608], replicated, may hold values from 0.5 to 1.5
- gain1: bfloat16 [768], replicated, may hold values from 0.5 to 1.5
- query_key_value_weight: bfloat16 [768, 2304], replicated, may hold values from -0.109375 to 0.109375
- attention_out_weight: bfloat16 [768, 768], replicated, may hold values from -1.25 to 1.25
- gain2: bfloat16 [768], replicated, may hold values from 0.5 to 1.5
- first_up_weight: bfloat16 [768, 3072], P(None, 'mp'), may hold values from -0.21875 to 0.21875
- first_hidden_bias: bfloat16 [3072], P('mp'), may hold values from -3 to 3
- second_down_weight: bfloat16 [3072, 768], P('mp'), may hold values from -0.109375 to 0.109375
- second_output_bias: bfloat16 [768], replicated, may hold values from -3 to 3
- cotangent: bfloat16 [24, 1024, 768], P(('batch', 'mp'), 'seq'), may hold values from -6 to 6
Outputs:
- mixed: bfloat16 [24, 1024, 768], P(('batch', 'mp'), 'seq')
- input_grad: float32 [24, 1024, 768], P(('batch', 'mp'), 'seq')
- grad_mask_embed: float32 [768], P(('batch', 'seq', 'mp'))
- grad_w_ada: float32 [128, 4608], P(None, ('batch', 'seq', 'mp'))
- grad_b_ada: float32 [4608], P(('batch', 'seq', 'mp'))
- grad_gain1: float32 [768], P(('batch', 'seq', 'mp'))
- grad_w_qkv: float32 [768, 2304], P(('batch', 'seq', 'mp'))
- grad_w_out: float32 [768, 768], P(('batch', 'seq', 'mp'))
- grad_gain2: float32 [768], P(('batch', 'seq', 'mp'))
- grad_w_fc1: float32 [768, 3072], P(('batch', 'seq'), 'mp')
- grad_b_fc1: float32 [3072], P('mp')
- grad_w_fc2: float32 [3072, 768], P('mp', ('batch', 'seq'))
- grad_b_fc2: float32 [768], P(('batch', 'seq', 'mp'))
The draws below stay inside these ranges and needn't reach their ends.
All inputs are finite; a program needn't handle non-finite values. No bound on the sum of `mask_bits` on one device may be relied on, other than what follows from the above.
Results may differ from the reference program's by a relative error of at most 0.012.
Values may be sent and summed in bfloat16 or wider, within the bound.
No kernel may reach another device: no remote copies, remote signals or barrier semaphores. Data moves between devices by JAX's collectives and lax.ppermute only.
A program may use at most 256 MiB of HBM per device.

```python
import math
import jax
import jax.numpy as jnp
from jax import lax

HEADS = 12
HEAD = 64
D = 768
FF = 3072
COND = 128
LEN = 1024
SEQS = 24


def with_ends(entries, rng, low, high):
    extent = entries.shape
    place = [jax.random.randint(jax.random.fold_in(rng, axis), (), 0, extent[axis]) for axis in range(len(extent))]
    entries = entries.at[tuple(place)].set(low)
    longest = extent.index(max(extent))
    place[longest] = (place[longest] + 1) % extent[longest]
    return entries.at[tuple(place)].set(high)


def strengthened(result, own_key, source, target, blocks, factor):
    owner, partner = [(jnp.arange(result.shape[position]) // (result.shape[position] // blocks)).reshape([-1 if axis == position else 1 for axis in range(result.ndim)]) for position in (source, target)]
    chosen = jax.random.permutation(own_key, blocks)[partner]
    strong = (owner == chosen) | (owner == (partner + blocks // 2) % blocks)
    return jnp.where(strong, factor * result, result)


def block_levels(own_key, extent, cuts, low, top_value):
    def one(axis_at, blocks):
        heights = jax.random.uniform(jax.random.fold_in(jax.random.fold_in(own_key, 6), axis_at), (blocks,), jnp.float32, low / len(cuts), top_value / len(cuts))
        return jnp.repeat(jnp.exp(heights), extent[axis_at] // blocks).reshape((-1,) + (1,) * (len(extent) - axis_at - 1))

    loudness = one(*cuts[0])
    for cut in cuts[1:]:
        loudness = loudness * one(*cut)
    return loudness


def bell_draw(own_key, extent, scale, limit, cuts=(), kind=jnp.bfloat16):
    level = block_levels(own_key, extent, cuts, -0.22, 0.18) if cuts else 1.0
    drawn = jax.random.normal(own_key, extent, jnp.float32) * scale * level
    return jnp.minimum(jnp.maximum(drawn, -limit), limit).astype(kind)


def bell_draw_with(rng, shape, scale, most, cuts, heavy, held_as=jnp.bfloat16):
    values = scale * jax.random.normal(rng, shape, jnp.float32)
    if cuts:
        values = values * block_levels(rng, shape, cuts, -0.22, 0.18)
    return jnp.clip(strengthened(values, jax.random.fold_in(rng, 3), *heavy), -most, most).astype(held_as)


def setup_inputs(seed: int = 0) -> dict:
    key_list = jax.random.split(jax.random.key(seed), 17)
    return {
        "tokens_in": bell_draw(key_list[0], (SEQS, LEN, D), 1.0, 6.0, ((0, 8), (1, 4))),
        "prefix": with_ends(jax.random.randint(key_list[1], (SEQS,), 0, LEN), jax.random.fold_in(key_list[1], 1), 0, LEN - 1).astype(jnp.int32),
        "mask_bits": with_ends((jax.random.randint(key_list[2], (SEQS, LEN), 0, 2) < 1).astype(jnp.int32), jax.random.fold_in(key_list[2], 1), 0, 1),
        "timestep": with_ends(jax.random.randint(key_list[3], (SEQS,), 0, 1000), jax.random.fold_in(key_list[3], 1), 0, 999).astype(jnp.int32),
        "mask_embed": bell_draw(key_list[4], (D,), 1.0, 6.0),
        "w_ada": bell_draw(key_list[5], (COND, 6 * D), COND ** -0.5, 0.5),
        "b_ada": jnp.clip(jax.random.uniform(key_list[6], (6 * D,), jnp.float32, 0.5, 1.5), 0.5, 1.5).astype(jnp.bfloat16),
        "gain1": jnp.clip(1.0 + 0.1 * jax.random.normal(key_list[7], (D,), jnp.float32), 0.5, 1.5).astype(jnp.bfloat16),
        "query_key_value_weight": bell_draw(key_list[8], (D, 3 * D), (4 * D) ** -0.5, 0.109375),
        "attention_out_weight": bell_draw(key_list[9], (D, D), (D // 32) ** -0.5, 1.25),
        "gain2": jnp.clip(1.0 + 0.1 * jax.random.normal(key_list[10], (D,), jnp.float32), 0.5, 1.5).astype(jnp.bfloat16),
        "first_up_weight": bell_draw(key_list[11], (D, FF), D ** -0.5, 0.21875, ((1, 2),)),
        "first_hidden_bias": bell_draw(key_list[12], (FF,), 0.5, 3.0, ((0, 2),)),
        "second_down_weight": bell_draw(key_list[13], (FF, D), FF ** -0.5, 0.109375, ((0, 2),)),
        "second_output_bias": bell_draw(key_list[14], (D,), 0.5, 3.0),
        "cotangent": bell_draw_with(key_list[15], (SEQS, LEN, D), 1.0, 6.0, ((0, 8), (1, 4)), (0, 2, 8, 2.0)),
    }


@jax.custom_vjp
def low(v):
    return lax.optimization_barrier(v.astype(jnp.bfloat16)).astype(jnp.float32)

@jax.custom_vjp
def lower_backward(v):
    return v

def low_keep(v):
    return (low(v), None)

def low_pass(kept, grad):
    return (grad,)

def back_keep(v):
    return (v, None)

def back_low(kept, grad):
    return (low(grad),)
low.defvjp(low_keep, low_pass)
lower_backward.defvjp(back_keep, back_low)
highest_precision = lax.Precision.HIGHEST

def time_features(timestep, width):
    half = width // 2
    freqs = jnp.exp(-math.log(10000.0) * jnp.arange(half, dtype=jnp.float32) / half)
    angles = timestep.astype(jnp.float32)[:, None] * freqs[None, :]
    return jnp.concatenate([jnp.cos(angles), jnp.sin(angles)], axis=-1)

def norm_modulate(field, gain, shift, scale):
    center = field - lax.optimization_barrier(jnp.mean(field, axis=-1, keepdims=True))
    spread = lax.optimization_barrier(jnp.mean(center * center, axis=-1, keepdims=True))
    normed = center * lax.rsqrt(spread + 1e-05) * gain
    return normed * (1.0 + scale[:, None, :]) + shift[:, None, :]

def rotate(heads_in, positions):
    half = heads_in.shape[-1] // 2
    inverse = jnp.exp(-math.log(10000.0) * jnp.arange(half, dtype=jnp.float32) / half)
    angles = positions[:, None] * inverse[None, :]
    cosine = jnp.concatenate([jnp.cos(angles), jnp.cos(angles)], axis=-1)[None, :, None, :]
    sine = jnp.concatenate([jnp.sin(angles), jnp.sin(angles)], axis=-1)[None, :, None, :]
    turned = jnp.concatenate([-heads_in[..., half:], heads_in[..., :half]], axis=-1)
    return heads_in * cosine + turned * sine

def block_forward(tokens, masked, cond, params):
    embed, w_ada, b_ada, gain1, query_key_value_weight, attention_out_weight, gain2, first_up_weight, first_hidden_bias, second_down_weight, second_output_bias = params
    group = tokens.shape[0]
    field = jnp.where(masked[..., None], embed, tokens)
    modul = jnp.dot(low(cond), w_ada, precision=highest_precision) + b_ada
    shift1, scale1, gate1, shift2, scale2, gate2 = jnp.split(modul, 6, axis=-1)
    first_normalized = low(norm_modulate(field, gain1, shift1, scale1))
    projected_rows = lower_backward(jnp.einsum('cno,ox->cnx', first_normalized, query_key_value_weight, precision=highest_precision))
    projected_rows = projected_rows.reshape(group, LEN, 3, HEADS, HEAD)
    positions = jnp.arange(LEN, dtype=jnp.float32)
    queries = low(rotate(projected_rows[:, :, 0], positions))
    keys = low(rotate(projected_rows[:, :, 1], positions))
    values = low(projected_rows[:, :, 2])
    scores = lower_backward(jnp.einsum('sqhe,skhe->shqk', queries, keys, precision=highest_precision) * HEAD ** (-0.5))
    probs = low(jax.nn.softmax(scores, axis=-1))
    attended_rows = jnp.einsum('shqk,skhe->sqhe', probs, values, precision=highest_precision).reshape(group, LEN, HEADS * HEAD)
    attended_rows = low(lower_backward(attended_rows))
    attention_result = lower_backward(jnp.einsum('cno,ox->cnx', attended_rows, attention_out_weight, precision=highest_precision))
    field1 = field + gate1[:, None, :] * attention_result
    second_normalized = low(norm_modulate(field1, gain2, shift2, scale2))
    residual_before = lower_backward(jnp.einsum('eur,rj->euj', second_normalized, first_up_weight, precision=highest_precision) + first_hidden_bias)
    hidden_activations = low(jax.nn.gelu(residual_before))
    perceptron_output = lower_backward(jnp.einsum('pnb,bh->pnh', hidden_activations, second_down_weight, precision=highest_precision) + second_output_bias)
    return field1 + gate2[:, None, :] * perceptron_output

def reference(tokens_in, prefix, mask_bits, timestep, mask_embed, w_ada, b_ada, gain1, query_key_value_weight, attention_out_weight, gain2, first_up_weight, first_hidden_bias, second_down_weight, second_output_bias, cotangent):
    floats = lambda a: a.astype(jnp.float32)
    params = tuple((floats(a) for a in (mask_embed, w_ada, b_ada, gain1, query_key_value_weight, attention_out_weight, gain2, first_up_weight, first_hidden_bias, second_down_weight, second_output_bias)))
    group = 2
    count = SEQS // group
    places = jnp.arange(LEN, dtype=jnp.int32)
    masked = (places[None, :] >= prefix[:, None]) & (mask_bits == 1)
    cond = jax.nn.silu(time_features(timestep, COND))

    def split_groups(a):
        return a.reshape((count, group) + a.shape[1:])

    def forward(tokens, weights):
        step = jax.checkpoint(lambda item: block_forward(item[0], item[1], item[2], weights))
        outputs = lax.map(step, (split_groups(tokens), split_groups(masked), split_groups(cond)))
        return outputs.reshape(SEQS, LEN, HEADS * HEAD)
    output, backward = jax.vjp(forward, floats(tokens_in), params)
    grad_tokens, grads = backward(floats(cotangent))
    g_embed, g_w_ada, g_b_ada, g_gain1, g_w_qkv, g_w_out, g_gain2, g_w_fc1, g_b_fc1, g_w_fc2, g_b_fc2 = grads
    return (output.astype(jnp.bfloat16), grad_tokens, g_embed, g_w_ada, g_b_ada, g_gain1, g_w_qkv, g_w_out, g_gain2, g_w_fc1, g_b_fc1, g_w_fc2, g_b_fc2)
```

```python
import functools
import math

import jax
import jax.numpy as jnp
from jax import lax
from jax.experimental import pallas as pl
from jax.experimental.pallas import tpu as pltpu
from jax.sharding import PartitionSpec as P

HEAD = 64
PAIR = 2 * HEAD
CHUNK = 256
LOG2E = math.log2(math.e)
LN2 = math.log(2.0)
BF = jnp.bfloat16
FL = jnp.float32
VMEM = 56 * 1024 * 1024
SWAP = [(0, 1), (1, 0)]


def mm(left, right):
    return lax.dot_general(left, right, (((1,), (0,)), ((), ())), preferred_element_type=FL)


def mm_nt(left, right):
    return lax.dot_general(left, right, (((1,), (1,)), ((), ())), preferred_element_type=FL)


def mm_tn(left, right):
    return lax.dot_general(left, right, (((0,), (0,)), ((), ())), preferred_element_type=FL)


def time_features(timestep, width):
    half = width // 2
    freqs = jnp.exp(-math.log(10000.0) * jnp.arange(half, dtype=FL) / half)
    angles = timestep.astype(FL)[:, None] * freqs[None, :]
    return jnp.concatenate([jnp.cos(angles), jnp.sin(angles)], axis=-1)


def unit(field):
    center = field - jnp.mean(field, axis=-1, keepdims=True)
    scale = lax.rsqrt(jnp.mean(center * center, axis=-1, keepdims=True) + 1e-05)
    return center * scale, scale


def unit_back(grad, normal, scale):
    return scale * (
        grad
        - jnp.mean(grad, axis=-1, keepdims=True)
        - normal * jnp.mean(grad * normal, axis=-1, keepdims=True)
    )


def turn(tile, cosine, sine):
    lane = lax.broadcasted_iota(jnp.int32, tile.shape, 1)
    ahead = pltpu.roll(tile, PAIR - HEAD // 2, 1)
    behind = pltpu.roll(tile, HEAD // 2, 1)
    other = jnp.where(lane % HEAD < HEAD // 2, ahead, behind)
    return tile * cosine + other * sine


def qkv_kernel(x_ref, w_ref, cos_ref, sin_ref, *refs):
    q_ref, k_ref, v_ref = refs[-3:]
    own = q_ref.shape[1]
    out = mm(x_ref[...], w_ref[...])
    cosine, sine = cos_ref[...], sin_ref[...]
    for at in range(0, own, PAIR):
        here = slice(at, at + PAIR)
        q_ref[:, here] = (turn(out[:, here], cosine, sine) * (LOG2E * HEAD ** (-0.5))).astype(BF)
        k_ref[:, here] = turn(out[:, own + at : own + at + PAIR], cosine, sine).astype(BF)
    v_ref[...] = out[:, 2 * own :].astype(BF)


def qkv_call(x, weight, cosine, sine, part, earlier):
    rows, width = x.shape
    own = weight.shape[1] // 3
    steps = rows // CHUNK
    shape = jax.ShapeDtypeStruct((2 * rows, own), BF)
    place = lambda g: (g + part * steps, 0)
    extra = [] if earlier is None else list(earlier)
    return pl.pallas_call(
        qkv_kernel,
        grid=(steps,),
        in_specs=[
            pl.BlockSpec((CHUNK, width), lambda g: (g, 0)),
            pl.BlockSpec(weight.shape, lambda g: (0, 0)),
            pl.BlockSpec((CHUNK, PAIR), place),
            pl.BlockSpec((CHUNK, PAIR), place),
        ]
        + [pl.BlockSpec(memory_space=pl.ANY)] * len(extra),
        out_specs=[pl.BlockSpec((CHUNK, own), place)] * 3,
        out_shape=[shape] * 3,
        input_output_aliases={4 + i: i for i in range(len(extra))},
        compiler_params=pltpu.CompilerParams(vmem_limit_bytes=VMEM),
        cost_estimate=pl.CostEstimate(
            flops=2 * rows * width * 3 * own, bytes_accessed=2 * (rows * width + weight.size + 3 * rows * own), transcendentals=0
        ),
        name="qkv",
    )(x, weight, cosine, sine, *extra)


def head_lanes(shape, head):
    lane = lax.broadcasted_iota(jnp.int32, shape, 1)
    return (lane >= head * HEAD) & (lane < (head + 1) * HEAD)


def attend_kernel(q_ref, k_ref, v_ref, out_ref, lse_ref, vt_ref):
    @pl.when(pl.program_id(1) == 0)
    def _():
        turned = v_ref[...].astype(FL).T.astype(BF)
        ones = jnp.ones((16, turned.shape[1]), BF)
        vt_ref[0] = jnp.concatenate([turned[:HEAD], ones], axis=0)
        vt_ref[1] = jnp.concatenate([turned[HEAD:], ones], axis=0)

    queries = q_ref[...]
    keys = k_ref[...]
    results = []
    for head in range(2):
        mine = jnp.where(head_lanes(queries.shape, head), queries, jnp.zeros_like(queries))
        scores = mm_nt(keys, mine)
        top = jnp.max(scores, axis=0, keepdims=True)
        raised = jnp.exp2(scores - top).astype(BF)
        both = mm(vt_ref[head], raised)
        total = both[HEAD : HEAD + 1]
        results.append(both[:HEAD] / total)
        lse_ref[0, head : head + 1, :] = top + jnp.log2(total)
    out_ref[...] = jnp.concatenate(results, axis=0).T.astype(BF)


def attend_call(q, k, v, stride):
    length, width = k.shape
    steps = length // CHUNK // stride
    rows = steps * CHUNK
    pairs = width // PAIR
    return pl.pallas_call(
        attend_kernel,
        grid=(pairs, steps),
        in_specs=[
            pl.BlockSpec((CHUNK, PAIR), lambda p, g: (g * stride, p)),
            pl.BlockSpec((length, PAIR), lambda p, g: (0, p)),
            pl.BlockSpec((length, PAIR), lambda p, g: (0, p)),
        ],
        out_specs=[
            pl.BlockSpec((CHUNK, PAIR), lambda p, g: (g, p)),
            pl.BlockSpec((1, 8, CHUNK), lambda p, g: (p, 0, g)),
        ],
        out_shape=[
            jax.ShapeDtypeStruct((rows, width), BF),
            jax.ShapeDtypeStruct((pairs, 8, rows), FL),
        ],
        scratch_shapes=[pltpu.VMEM((2, HEAD + 16, length), BF)],
        compiler_params=pltpu.CompilerParams(vmem_limit_bytes=VMEM),
        cost_estimate=pl.CostEstimate(
            flops=16 * rows * length * width, bytes_accessed=4 * (rows + length) * width, transcendentals=0
        ),
        name="attend",
    )(q, k, v)


def attend_back_kernel(
    stride, q_ref, k_ref, v_ref, att_ref, grad_ref, lse_ref, cosq_ref, sinq_ref, cos_ref, sin_ref, out_ref, kt_ref, dk_ref, dv_ref
):
    pair, step = pl.program_id(0), pl.program_id(1)
    length = k_ref.shape[0]
    own = out_ref.shape[1] // 3

    @pl.when(step == 0)
    def _():
        kt_ref[...] = k_ref[...].astype(FL).T.astype(BF)
        dk_ref[...] = jnp.zeros_like(dk_ref)
        dv_ref[...] = jnp.zeros_like(dv_ref)

    queries, keys, values, grads = q_ref[...], k_ref[...], v_ref[...], grad_ref[...]
    product = (att_ref[...].astype(FL) * grads.astype(FL)).T
    parts, dk, dv = [], dk_ref[...], dv_ref[...]
    for head in range(2):
        lanes = head_lanes(queries.shape, head)
        mine = jnp.where(lanes, queries, jnp.zeros_like(queries))
        grad = jnp.where(lanes, grads, jnp.zeros_like(grads))
        delta = jnp.sum(product[head * HEAD : (head + 1) * HEAD], axis=0, keepdims=True)
        probs = jnp.exp2(mm_nt(keys, mine) - lse_ref[0, head : head + 1, :])
        dv = dv + mm(probs.astype(BF), grad)
        scores = (probs * (mm_nt(values, grad) - delta)).astype(BF)
        dk = dk + mm(scores, mine)
        parts.append(mm(kt_ref[head * HEAD : (head + 1) * HEAD], scores))
    dk_ref[...] = dk
    dv_ref[...] = dv
    dq = jnp.concatenate(parts, axis=0).T * (HEAD ** (-0.5))
    row = pl.ds(pl.multiple_of(step * stride * CHUNK, CHUNK), CHUNK)
    column = pl.multiple_of(pair * PAIR, PAIR)
    out_ref[row, pl.ds(column, PAIR)] = turn(dq, cosq_ref[...], -sinq_ref[...]).astype(BF)
    if stride > 1:
        rest = pl.ds(pl.multiple_of(step * stride * CHUNK + CHUNK, CHUNK), (stride - 1) * CHUNK)
        out_ref[rest, pl.ds(column, PAIR)] = jnp.zeros(((stride - 1) * CHUNK, PAIR), BF)

    @pl.when(step == pl.num_programs(1) - 1)
    def _():
        turned = turn(dk_ref[...] * LN2, cos_ref[...], -sin_ref[...])
        out_ref[:, pl.ds(pl.multiple_of(own + column, PAIR), PAIR)] = turned.astype(BF)
        out_ref[:, pl.ds(pl.multiple_of(2 * own + column, PAIR), PAIR)] = dv_ref[...].astype(BF)


def attend_back_call(q, k, v, att, grad, lse, cosine, sine, stride):
    length, width = k.shape
    steps = length // CHUNK // stride
    rows = steps * CHUNK
    pairs = width // PAIR
    chunk = lambda p, g: (g, p)
    whole = lambda p, g: (0, p)
    fixed = lambda p, g: (0, 0)
    return pl.pallas_call(
        functools.partial(attend_back_kernel, stride),
        grid=(pairs, steps),
        in_specs=[
            pl.BlockSpec((CHUNK, PAIR), lambda p, g: (g * stride, p)),
            pl.BlockSpec((length, PAIR), whole),
            pl.BlockSpec((length, PAIR), whole),
            pl.BlockSpec((CHUNK, PAIR), chunk),
            pl.BlockSpec((CHUNK, PAIR), chunk),
            pl.BlockSpec((1, 8, CHUNK), lambda p, g: (p, 0, g)),
            pl.BlockSpec((CHUNK, PAIR), lambda p, g: (g * stride, 0)),
            pl.BlockSpec((CHUNK, PAIR), lambda p, g: (g * stride, 0)),
            pl.BlockSpec((length, PAIR), fixed),
            pl.BlockSpec((length, PAIR), fixed),
        ],
        out_specs=pl.BlockSpec((length, 3 * width), fixed),
        out_shape=jax.ShapeDtypeStruct((length, 3 * width), BF),
        scratch_shapes=[
            pltpu.VMEM((PAIR, length), BF),
            pltpu.VMEM((length, PAIR), FL),
            pltpu.VMEM((length, PAIR), FL),
        ],
        compiler_params=pltpu.CompilerParams(vmem_limit_bytes=VMEM),
        cost_estimate=pl.CostEstimate(
            flops=40 * rows * length * width, bytes_accessed=8 * (rows + length) * width, transcendentals=0
        ),
        name="attend_back",
    )(q, k, v, att, grad, lse, cosine, sine, cosine, sine)


def bits_of(axis):
    return (lax.axis_size(axis) - 1).bit_length()


def partner(axis, bit):
    return [(at, at ^ (1 << bit)) for at in range(lax.axis_size(axis))]


def one_of(array, at, axis):
    return lax.dynamic_index_in_dim(array, at, axis, keepdims=False)


def scatter_sum(array, order):
    batch_bits, seq_bits = bits_of("batch"), bits_of("seq")
    names = [("batch", bit) for bit in reversed(range(batch_bits))]
    names += [("seq", bit) for bit in reversed(range(seq_bits))]
    rows = array.shape[0] >> len(names)
    total = array.reshape([2] * len(names) + [rows, array.shape[1]])
    steps = [("batch", bit) for bit in (range(batch_bits) if order else reversed(range(batch_bits)))]
    steps += [("seq", bit) for bit in range(seq_bits)]
    for axis, bit in steps:
        at = names.index((axis, bit))
        mine = (lax.axis_index(axis) >> bit) & 1
        sent = one_of(total, 1 - mine, at).astype(BF)
        kept = one_of(total, mine, at)
        total = kept + lax.ppermute(sent, axis, partner(axis, bit)).astype(FL)
        names.pop(at)
    return total


def sum_everywhere(array):
    for axis in ("batch", "seq"):
        for bit in range(bits_of(axis)):
            array = array + lax.ppermute(array, axis, partner(axis, bit))
    return array


def routes(second, turned):
    pairs = []
    for q in range(4):
        for c in range(2):
            group = 1 - c if second else c
            chip = 2 * group + (q // 2 + turned) % 2
            pairs.append((q * 2 + c, chip * 2 + q % 2))
    return pairs


def send(block, second, turned):
    return lax.ppermute(block, ("seq", "mp"), routes(second, turned))


def send_home(block, second, turned):
    return lax.ppermute(block, ("seq", "mp"), [(to, at) for at, to in routes(second, turned)])


def per_device(
    tokens_in,
    prefix,
    mask_bits,
    timestep,
    mask_embed,
    w_ada,
    b_ada,
    gain1,
    query_key_value_weight,
    attention_out_weight,
    gain2,
    first_up_weight,
    first_hidden_bias,
    second_down_weight,
    second_output_bias,
    cotangent,
):
    seqs, span, width = tokens_in.shape
    own = width // 2
    half_rows = seqs * span
    z, c = lax.axis_index("seq"), lax.axis_index("mp")
    upper, side = z // 2, z % 2
    devices = lax.axis_size("batch") * lax.axis_size("seq") * lax.axis_size("mp")

    places = jnp.arange(span, dtype=jnp.int32) + z * span
    masked = ((places[None, :] >= prefix[:, None]) & (mask_bits == 1))[:, :, None]
    home = jnp.where(masked, mask_embed, tokens_in)

    def depart(blocks):
        return (
            send(one_of(blocks, upper, 0), False, 0),
            send(one_of(blocks, 1 - upper, 0), False, 1),
            send(blocks[2], True, 0),
        )

    def back_home(blocks):
        first = send_home(blocks[0], False, 0)
        second = send_home(blocks[1], False, 1)
        third = send_home(blocks[2], True, 0)
        low, high = jnp.where(upper == 0, first, second), jnp.where(upper == 0, second, first)
        return jnp.stack([low, high, third])

    block_a0, block_a1, block_b0 = depart(home)
    block_b1 = send(home[2], True, 1)
    grad_out = jnp.stack(depart(cotangent)).astype(FL)

    other_time = lax.ppermute(timestep, "mp", SWAP)
    time_a = one_of(jnp.where(c == upper, timestep, other_time), side, 0)
    time_b = jnp.where(c == upper, other_time, timestep)[2]
    cond = jax.nn.silu(time_features(jnp.stack([time_a, time_b]), w_ada.shape[0])).astype(BF)
    modul = jnp.dot(cond, w_ada, preferred_element_type=FL) + b_ada.astype(FL)
    shift1, scale1, gate1, shift2, scale2, gate2 = jnp.split(modul, 6, axis=-1)
    gain_one, gain_two = gain1.astype(FL), gain2.astype(FL)

    def per_block(rows):
        return jnp.stack([rows[0], rows[0], rows[1]])[:, None, :]

    w_heads = jnp.concatenate(
        [
            lax.dynamic_slice_in_dim(query_key_value_weight, at * width + c * own, own, 1)
            for at in range(3)
        ],
        axis=1,
    )
    w_out = jnp.concatenate(
        [
            lax.dynamic_slice_in_dim(attention_out_weight, c * own, own, 0),
            lax.dynamic_slice_in_dim(attention_out_weight, (1 - c) * own, own, 0),
        ],
        axis=0,
    )
    quarter = jnp.stack([2 * side + c, 2 * (1 - side) + c, 2 * side + 1 - c, 2 * (1 - side) + 1 - c])
    positions = (quarter[:, None] * span + jnp.arange(span)[None, :]).reshape(-1).astype(FL)
    half = HEAD // 2
    inverse = jnp.exp(-math.log(10000.0) * jnp.arange(half, dtype=FL) / half)
    angles = positions[:, None] * inverse[None, :]
    cosine = jnp.tile(jnp.cos(angles), (1, 4))
    sine = jnp.tile(jnp.concatenate([-jnp.sin(angles), jnp.sin(angles)], axis=1), (1, 2))

    def first_norm(blocks, at):
        normal, scale = unit(blocks.astype(FL))
        normed = normal * gain_one * (1.0 + scale1[at]) + shift1[at]
        return normed.astype(BF).reshape(-1, width)

    def project(blocks, at):
        mine = first_norm(blocks, at)
        other = lax.ppermute(mine, "mp", SWAP)
        results = qkv_call(mine, w_heads, cosine, sine, 0, None)
        return jnp.concatenate([mine, other], axis=0), qkv_call(other, w_heads, cosine, sine, 1, results)

    normed_a, (q_a, k_a, v_a) = project(jnp.stack([block_a0, block_a1]), 0)
    att_a, lse_a = attend_call(q_a, k_a, v_a, 1)
    normed_b, (q_b, k_b, v_b) = project(jnp.stack([block_b0, block_b1]), 1)
    att_b, lse_b = attend_call(q_b, k_b, v_b, 2)

    rows_a, rows_b = 2 * span, span
    att_mine = jnp.concatenate([att_a[:rows_a], att_b[:rows_b]], axis=0)
    att_other = lax.ppermute(
        jnp.concatenate([att_a[rows_a:], att_b[rows_b:]], axis=0), "mp", SWAP
    )
    attended = jnp.concatenate([att_mine, att_other], axis=1)
    attention_result = mm(attended, w_out).reshape(seqs, span, width)
    field = jnp.stack([block_a0, block_a1, block_b0]).astype(FL)
    field1 = field + per_block(gate1) * attention_result

    unit2, spread2 = unit(field1)
    normed2 = (
        (unit2 * gain_two * (1.0 + per_block(scale2)) + per_block(shift2))
        .astype(BF)
        .reshape(half_rows, width)
    )
    normed2_other = lax.ppermute(normed2, "mp", SWAP)
    grad_mlp = (per_block(gate2) * grad_out).astype(BF).reshape(half_rows, width)
    grad_mlp_other = lax.ppermute(grad_mlp, "mp", SWAP)
    bias1 = first_hidden_bias.astype(FL)

    def up(rows):
        before = mm(rows, first_up_weight) + bias1
        return before, jax.nn.gelu(before).astype(BF)

    before_other, hidden_other = up(normed2_other)
    term_other = lax.ppermute(mm(hidden_other, second_down_weight).astype(BF), "mp", SWAP)
    before, hidden = up(normed2)
    mlp_out = mm(hidden, second_down_weight) + term_other.astype(FL) + second_output_bias.astype(FL)
    mlp_out = mlp_out.reshape(seqs, span, width)
    mixed = (field1 + per_block(gate2) * mlp_out).astype(BF)
    output = back_home(mixed)

    grad_gate2 = jnp.sum(grad_out * mlp_out, axis=1)
    grad_b2 = jnp.sum(grad_mlp.astype(FL), axis=0)

    def up_back(rows, before):
        grad_hidden = mm_nt(rows, second_down_weight)
        return jax.vjp(jax.nn.gelu, before)[1](grad_hidden)[0].astype(BF)

    grad_before_other = up_back(grad_mlp_other, before_other)
    normed2_term = lax.ppermute(mm_nt(grad_before_other, first_up_weight).astype(BF), "mp", SWAP)
    grad_before = up_back(grad_mlp, before)
    grad_normed2 = (mm_nt(grad_before, first_up_weight) + normed2_term.astype(FL)).reshape(
        seqs, span, width
    )
    grad_w1 = mm_tn(normed2, grad_before) + mm_tn(normed2_other, grad_before_other)
    grad_w2 = mm_tn(grad_mlp, hidden) + mm_tn(grad_mlp_other, hidden_other)
    grad_b1 = jnp.sum(grad_before.astype(FL), axis=0) + jnp.sum(grad_before_other.astype(FL), axis=0)
    grad_w1 = scatter_sum(grad_w1, False)
    grad_w2 = scatter_sum(grad_w2, True).T
    grad_b1 = sum_everywhere(grad_b1)

    weighted = jnp.sum(grad_normed2 * unit2, axis=1)
    grad_shift2 = jnp.sum(grad_normed2, axis=1)
    grad_field1 = grad_out + unit_back(
        grad_normed2 * (1.0 + per_block(scale2)) * gain_two, unit2, spread2
    )
    grad_gate1 = jnp.sum(grad_field1 * attention_result, axis=1)
    grad_attn = (per_block(gate1) * grad_field1).astype(BF).reshape(half_rows, width)
    grad_att = mm_nt(grad_attn, w_out).astype(BF)
    grad_att_other = lax.ppermute(grad_att[:, own:], "mp", SWAP)
    grad_w_out = mm_tn(attended, grad_attn)
    grad_w_out = grad_w_out[:own] + lax.ppermute(grad_w_out[own:].astype(BF), "mp", SWAP).astype(FL)
    grad_w_out = scatter_sum(grad_w_out, False)

    grad_att_a = jnp.concatenate([grad_att[:rows_a, :own], grad_att_other[:rows_a]], axis=0)
    grad_att_b = jnp.concatenate([grad_att[rows_a:, :own], grad_att_other[rows_a:]], axis=0)
    grad_proj_b = attend_back_call(q_b, k_b, v_b, att_b, grad_att_b, lse_b, cosine, sine, 2)
    grad_proj_a = attend_back_call(q_a, k_a, v_a, att_a, grad_att_a, lse_a, cosine, sine, 1)

    def project_back(grad_proj):
        other = mm_nt(grad_proj[rows_a:], w_heads).astype(BF)
        other = lax.ppermute(other, "mp", SWAP)
        return mm_nt(grad_proj[:rows_a], w_heads) + other.astype(FL)

    normed1_b = project_back(grad_proj_b)
    beside = lax.ppermute(normed1_b[rows_b:].astype(BF), "seq", partner("seq", 0))
    normed1_b = normed1_b[:rows_b] + beside.astype(FL)
    normed1_a = project_back(grad_proj_a)
    grad_normed1 = jnp.concatenate([normed1_a, normed1_b], axis=0).reshape(seqs, span, width)
    grad_w_qkv = scatter_sum(mm_tn(normed_b, grad_proj_b) + mm_tn(normed_a, grad_proj_a), True)

    unit1, spread1 = unit(field)
    weighted1 = jnp.sum(grad_normed1 * unit1, axis=1)
    grad_shift1 = jnp.sum(grad_normed1, axis=1)
    grad_field = grad_field1 + unit_back(
        grad_normed1 * (1.0 + per_block(scale1)) * gain_one, unit1, spread1
    )
    grad_home = back_home(grad_field.astype(BF)).astype(FL)
    grad_tokens = jnp.where(masked, 0.0, grad_home)
    grad_embed = jnp.sum(jnp.where(masked, grad_home, 0.0), axis=(0, 1))

    def per_sequence(rows):
        return jnp.stack([rows[0] + rows[1], rows[2]])

    weighted, weighted1 = per_sequence(weighted), per_sequence(weighted1)
    grad_modul = jnp.concatenate(
        [
            per_sequence(grad_shift1),
            weighted1 * gain_one,
            per_sequence(grad_gate1),
            per_sequence(grad_shift2),
            weighted * gain_two,
            per_sequence(grad_gate2),
        ],
        axis=-1,
    )
    grad_gain1 = jnp.sum(weighted1 * (1.0 + scale1), axis=0)
    grad_gain2 = jnp.sum(weighted * (1.0 + scale2), axis=0)
    ada = grad_modul.shape[1] // devices
    part = width // devices
    small = jnp.concatenate(
        [
            grad_modul.reshape(2, devices, ada).transpose(1, 0, 2).reshape(devices, 2 * ada),
            jnp.stack([grad_embed, grad_gain1, grad_gain2, grad_b2])
            .reshape(4, devices, part)
            .transpose(1, 0, 2)
            .reshape(devices, 4 * part),
            jnp.broadcast_to(cond.astype(FL).reshape(1, -1), (devices, cond.size)),
        ],
        axis=1,
    )
    small = lax.all_to_all(small, ("batch", "seq", "mp"), 0, 0, tiled=True)
    all_modul = small[:, : 2 * ada].reshape(2 * devices, ada)
    vectors = jnp.sum(small[:, 2 * ada : 2 * ada + 4 * part].reshape(devices, 4, part), axis=0)
    all_cond = small[:, 2 * ada + 4 * part :].reshape(2 * devices, -1)
    g_w_ada = lax.dot_general(
        all_cond, all_modul, (((0,), (0,)), ((), ())), precision=lax.Precision.HIGHEST
    )
    g_b_ada = jnp.sum(all_modul, axis=0)

    rows = grad_w_qkv.shape[0] // 2
    mine = lax.dynamic_slice_in_dim(grad_w_qkv, c * rows, rows, 0)
    other = lax.dynamic_slice_in_dim(grad_w_qkv, (1 - c) * rows, rows, 0)
    other = lax.ppermute(other.astype(BF), "mp", SWAP).astype(FL)
    low = jnp.where(c == 0, mine, other).reshape(rows, 3, own)
    high = jnp.where(c == 0, other, mine).reshape(rows, 3, own)
    g_w_qkv = jnp.concatenate([low, high], axis=2).reshape(rows, 3 * width)
    chips = devices // 2
    moves = [(2 * at + core, chips * core + at) for at in range(chips) for core in range(2)]
    g_w_out = lax.ppermute(grad_w_out.astype(BF), ("batch", "seq", "mp"), moves).astype(FL)
    return (
        output,
        grad_tokens,
        vectors[0],
        g_w_ada,
        g_b_ada,
        vectors[1],
        g_w_qkv,
        g_w_out,
        vectors[2],
        grad_w1,
        grad_b1,
        grad_w2,
        vectors[3],
    )


def solution(mesh):
    in_specs = (
        P(("batch", "mp"), "seq", None),
        P(("batch", "mp")),
        P(("batch", "mp"), "seq"),
        P(("batch", "mp")),
        P(),
        P(),
        P(),
        P(),
        P(),
        P(),
        P(),
        P(None, "mp"),
        P("mp"),
        P("mp", None),
        P(),
        P(("batch", "mp"), "seq", None),
    )
    out_specs = (
        P(("batch", "mp"), "seq", None),
        P(("batch", "mp"), "seq", None),
        P(("batch", "seq", "mp")),
        P(None, ("batch", "seq", "mp")),
        P(("batch", "seq", "mp")),
        P(("batch", "seq", "mp")),
        P(("batch", "seq", "mp"), None),
        P(("batch", "seq", "mp"), None),
        P(("batch", "seq", "mp")),
        P(("batch", "seq"), "mp"),
        P("mp"),
        P("mp", ("batch", "seq")),
        P(("batch", "seq", "mp")),
    )
    return jax.shard_map(
        per_device, mesh=mesh, in_specs=in_specs, out_specs=out_specs, check_vma=False
    )
```

```python
import functools
import math

import jax
import jax.numpy as jnp
from jax import lax
from jax.experimental import pallas as pl
from jax.experimental.pallas import tpu as pltpu
from jax.sharding import PartitionSpec as P

HEAD = 64
PAIR = 2 * HEAD
CHUNK = 256
LOG2E = math.log2(math.e)
LN2 = math.log(2.0)
BF = jnp.bfloat16
FL = jnp.float32
SWAP = [(0, 1), (1, 0)]


def mm(left, right):
    return lax.dot_general(left, right, (((1,), (0,)), ((), ())), preferred_element_type=FL)


def mm_nt(left, right):
    return lax.dot_general(left, right, (((1,), (1,)), ((), ())), preferred_element_type=FL)


def mm_tn(left, right):
    return lax.dot_general(left, right, (((0,), (0,)), ((), ())), preferred_element_type=FL)


def time_features(timestep, width):
    half = width // 2
    freqs = jnp.exp(-math.log(10000.0) * jnp.arange(half, dtype=FL) / half)
    angles = timestep.astype(FL)[:, None] * freqs[None, :]
    return jnp.concatenate([jnp.cos(angles), jnp.sin(angles)], axis=-1)


def unit(field):
    center = field - jnp.mean(field, axis=-1, keepdims=True)
    scale = lax.rsqrt(jnp.mean(center * center, axis=-1, keepdims=True) + 1e-05)
    return center * scale, scale


def unit_back(grad, normal, scale):
    return scale * (
        grad
        - jnp.mean(grad, axis=-1, keepdims=True)
        - normal * jnp.mean(grad * normal, axis=-1, keepdims=True)
    )


def row_sum(array):
    return jnp.sum(array, axis=0, keepdims=True)


def call(kernel, name, grid, ins, outs, flops, megabytes, aliases=None, scratch=()):
    arrays = [entry[0] for entry in ins]
    in_specs = [
        pl.BlockSpec(memory_space=pl.ANY) if entry[1] is None else pl.BlockSpec(entry[1], entry[2])
        for entry in ins
    ]
    moved = sum(a.size * a.dtype.itemsize for a in arrays)
    moved += sum(math.prod(o[0]) * jnp.dtype(o[1]).itemsize for o in outs)
    return pl.pallas_call(
        kernel,
        grid=grid,
        in_specs=in_specs,
        out_specs=[pl.BlockSpec(o[2], o[3]) for o in outs],
        out_shape=[jax.ShapeDtypeStruct(o[0], o[1]) for o in outs],
        scratch_shapes=list(scratch),
        input_output_aliases=aliases or {},
        compiler_params=pltpu.CompilerParams(vmem_limit_bytes=megabytes * 1024 * 1024),
        cost_estimate=pl.CostEstimate(flops=flops, bytes_accessed=moved, transcendentals=0),
        name=name,
    )(*arrays)


def still(*indices):
    return lambda *grid: indices


def pick(values):
    step = pl.program_id(0)
    chosen = values[-1][...]
    for at in reversed(range(len(values) - 1)):
        chosen = jnp.where(step == at, values[at][...], chosen)
    return chosen


def norm1_kernel(x0_ref, x1_ref, mod_ref, gain_ref, out_ref):
    for at, ref in enumerate((x0_ref, x1_ref)):
        normal, _ = unit(ref[...].astype(FL))
        normed = normal * gain_ref[...] * (1.0 + mod_ref[0, 1:2]) + mod_ref[0, 0:1]
        out_ref[at * CHUNK : (at + 1) * CHUNK] = normed.astype(BF)


def norm1_call(x0, x1, modul, gain, seq):
    width = gain.shape[1]
    block = (CHUNK, width)
    return call(
        norm1_kernel,
        "norm1",
        (1,),
        [
            (x0, block, still(0, 0)),
            (x1, block, still(0, 0)),
            (modul, (1, 6, width), still(seq, 0, 0)),
            (gain, (1, width), still(0, 0)),
        ],
        [((2 * CHUNK, width), BF, (2 * CHUNK, width), still(0, 0))],
        10 * 2 * CHUNK * width,
        16,
    )[0]


def turn(tile, cosine, sine):
    lane = lax.broadcasted_iota(jnp.int32, tile.shape, 1)
    ahead = pltpu.roll(tile, PAIR - HEAD // 2, 1)
    behind = pltpu.roll(tile, HEAD // 2, 1)
    other = jnp.where(lane % HEAD < HEAD // 2, ahead, behind)
    return tile * cosine + other * sine


def qkv_kernel(x_ref, w_ref, cos_ref, sin_ref, *refs):
    copy_ref, q_ref, k_ref, v_ref = refs[-4:]
    own = q_ref.shape[1]
    x = x_ref[...]
    copy_ref[...] = x
    out = mm(x, w_ref[...])
    cosine, sine = cos_ref[...], sin_ref[...]
    for at in range(0, own, PAIR):
        here = slice(at, at + PAIR)
        q_ref[:, here] = (turn(out[:, here], cosine, sine) * (LOG2E * HEAD ** (-0.5))).astype(BF)
        k_ref[:, here] = turn(out[:, own + at : own + at + PAIR], cosine, sine).astype(BF)
    v_ref[...] = out[:, 2 * own :].astype(BF)


def qkv_call(x, weight, cosine, sine, part, earlier):
    rows, width = x.shape
    own = weight.shape[1] // 3
    steps = rows // CHUNK
    place = lambda g: (g + part * steps, 0)
    extra = [] if earlier is None else list(earlier)
    return call(
        qkv_kernel,
        "qkv",
        (steps,),
        [
            (x, (CHUNK, width), lambda g: (g, 0)),
            (weight, weight.shape, still(0, 0)),
            (cosine, (CHUNK, PAIR), place),
            (sine, (CHUNK, PAIR), place),
        ]
        + [(array, None, None) for array in extra],
        [((2 * rows, width), BF, (CHUNK, width), place)]
        + [((2 * rows, own), BF, (CHUNK, own), place)] * 3,
        2 * rows * width * 3 * own,
        24,
        {4 + i: i for i in range(len(extra))},
    )


def head_lanes(shape, head):
    lane = lax.broadcasted_iota(jnp.int32, shape, 1)
    return (lane >= head * HEAD) & (lane < (head + 1) * HEAD)


def taken(ref, stride):
    chunks = [ref[at : at + CHUNK] for at in range(0, ref.shape[0], stride * CHUNK)]
    return jnp.concatenate(chunks, axis=0)


def attend_kernel(stride, q_ref, k_ref, v_ref, own_ref, other_ref, lse_ref):
    queries = taken(q_ref, stride)
    keys = k_ref[...]
    turned = v_ref[...].astype(FL).T.astype(BF)
    ones = jnp.ones((16, turned.shape[1]), BF)
    results = []
    for head in range(2):
        mine = jnp.where(head_lanes(queries.shape, head), queries, jnp.zeros_like(queries))
        scores = mm_nt(keys, mine)
        top = jnp.max(scores, axis=0, keepdims=True)
        raised = jnp.exp2(scores - top).astype(BF)
        values = jnp.concatenate([turned[head * HEAD : (head + 1) * HEAD], ones], axis=0)
        both = mm(values, raised)
        total = both[HEAD : HEAD + 1]
        results.append(both[:HEAD] / total)
        lse_ref[0, head : head + 1, :] = top + jnp.log2(total)
    out = jnp.concatenate(results, axis=0).T.astype(BF)
    rows = own_ref.shape[0]
    own_ref[...] = out[:rows]
    other_ref[...] = out[rows:]


def attend_call(q, k, v, stride):
    length, width = k.shape
    rows = length // stride
    pairs = width // PAIR
    whole = ((length, PAIR), lambda p: (0, p))
    return call(
        functools.partial(attend_kernel, stride),
        "attend",
        (pairs,),
        [(q, *whole), (k, *whole), (v, *whole)],
        [((rows // 2, width), BF, (rows // 2, PAIR), lambda p: (0, p))] * 2
        + [((pairs, 8, rows), FL, (1, 8, rows), lambda p: (p, 0, 0))],
        8 * rows * length * width,
        40,
    )


def out_kernel(own_ref, got_ref, *refs):
    fields, (mod_ref, gain_ref, w_ref, att_ref, res_ref, normed_ref) = refs[:-6], refs[-6:]
    attended = jnp.concatenate([own_ref[...], got_ref[...]], axis=1)
    att_ref[...] = attended
    result = mm(attended, w_ref[...])
    res_ref[...] = result
    field = pick(fields).astype(FL) + mod_ref[0, 2:3] * result
    normal, _ = unit(field)
    normed = normal * gain_ref[...] * (1.0 + mod_ref[0, 4:5]) + mod_ref[0, 3:4]
    normed_ref[...] = normed.astype(BF)


def out_call(own, got, fields, modul, gain, weight, seq):
    rows, width = own.shape[0], gain.shape[1]
    part = (CHUNK, width // 2)
    block = (CHUNK, width)
    row = lambda g: (g, 0)
    return call(
        out_kernel,
        "out_norm2",
        (rows // CHUNK,),
        [(own, part, row), (got, part, row)]
        + [(field, block, still(0, 0)) for field in fields]
        + [
            (modul, (1, 6, width), still(seq, 0, 0)),
            (gain, (1, width), still(0, 0)),
            (weight, weight.shape, still(0, 0)),
        ],
        [((rows, width), BF, block, row), ((rows, width), FL, block, row), ((rows, width), BF, block, row)],
        2 * rows * width * width,
        24,
    )


def mlp_kernel(
    x_ref, xo_ref, c_ref, co_ref, mod_ref, w1_ref, b1_ref, w2_ref,
    copy_ref, grad_ref, hidden_ref, before_ref, out_ref, back_ref, away_ref, bsum_ref, gsum_ref,
):
    step = pl.program_id(0)
    first = step == 0
    owns = step < pl.num_programs(0) // 2
    x = jnp.where(owns, x_ref[...], xo_ref[...])
    copy_ref[...] = x
    grad = jnp.where(owns, c_ref[...], co_ref[...])
    grad = (mod_ref[0, 5:6] * grad.astype(FL)).astype(BF)
    grad_ref[...] = grad
    units = w1_ref.shape[1]
    size = units // 3
    root = math.sqrt(2.0 / math.pi)
    total, back = None, None
    for at in range(0, units, size):
        here = slice(at, at + size)
        before = mm(x, w1_ref[:, here]) + b1_ref[:, here]
        square = before * before
        inner = jnp.tanh(before * (root + (root * 0.044715) * square))
        half = 0.5 * (1.0 + inner)
        hidden = (before * half).astype(BF)
        slope = half + (0.5 * before) * (1.0 - inner * inner) * (root + (3.0 * root * 0.044715) * square)
        grad_before = (mm_nt(grad, w2_ref[here]) * slope).astype(BF)
        hidden_ref[:, here] = hidden
        before_ref[:, here] = grad_before
        add = row_sum(grad_before.astype(FL))
        bsum_ref[:, here] = jnp.where(first, add, bsum_ref[:, here] + add)
        term = mm(hidden, w2_ref[here])
        total = term if total is None else total + term
        term = mm_nt(grad_before, w1_ref[:, here])
        back = term if back is None else back + term

    @pl.when(owns)
    def _():
        out_ref[...] = total
        back_ref[...] = back
        add = row_sum(grad.astype(FL))
        gsum_ref[...] = jnp.where(first, add, gsum_ref[...] + add)

    @pl.when(jnp.logical_not(owns))
    def _():
        away_ref[0] = total.astype(BF)
        away_ref[1] = back.astype(BF)


def mlp_call(x, x_other, grads, grads_other, modul, w1, b1, w2, seq):
    rows, width = x.shape
    units = w1.shape[1]
    steps = rows // CHUNK
    block = (CHUNK, width)
    row = lambda g: (g, 0)
    early = lambda g: (jnp.minimum(g, steps - 1), 0)
    late = lambda g: (jnp.maximum(g - steps, 0), 0)
    return call(
        mlp_kernel,
        "mlp",
        (2 * steps,),
        [
            (x, block, early),
            (x_other, block, late),
            (grads, block, early),
            (grads_other, block, late),
            (modul, (1, 6, width), still(seq, 0, 0)),
            (w1, w1.shape, still(0, 0)),
            (b1, b1.shape, still(0, 0)),
            (w2, w2.shape, still(0, 0)),
        ],
        [((2 * rows, width), BF, block, row)] * 2
        + [((2 * rows, units), BF, (CHUNK, units), row)] * 2
        + [((rows, width), FL, block, early)] * 2
        + [((2, rows, width), BF, (2, CHUNK, width), lambda g: (0, jnp.maximum(g - steps, 0), 0))]
        + [((1, units), FL, (1, units), still(0, 0)), ((1, width), FL, (1, width), still(0, 0))],
        16 * rows * width * units,
        40,
    )


def norm2_back_kernel(own_ref, got_ref, bown_ref, bgot_ref, res_ref, c_ref, *refs):
    blocks = (len(refs) - 9) // 2
    fields, refs = refs[:blocks], refs[blocks:]
    mod_ref, gain_ref, b2_ref, w_ref = refs[:4]
    outs, (field_ref, attn_ref, mine_ref, other_ref, sum_ref) = refs[4:-5], refs[-5:]
    step = pl.program_id(0)
    mod = lambda at: mod_ref[0, at : at + 1]
    grad_out = c_ref[...].astype(FL)
    result = res_ref[...]
    field = pick(fields).astype(FL) + mod(2) * result
    out = own_ref[...] + got_ref[0].astype(FL) + b2_ref[...]
    mixed = (field + mod(5) * out).astype(BF)
    for at, ref in enumerate(outs):

        @pl.when(step == at)
        def _():
            ref[...] = mixed

    grad = bown_ref[...] + bgot_ref[0].astype(FL)
    normal, scale = unit(field)
    grad_field = grad_out + unit_back(grad * (1.0 + mod(4)) * gain_ref[...], normal, scale)
    field_ref[...] = grad_field
    grad_attn = (mod(2) * grad_field).astype(BF)
    attn_ref[...] = grad_attn
    back = mm_nt(grad_attn, w_ref[...]).astype(BF)
    own = mine_ref.shape[1]
    mine_ref[...] = back[:, :own]
    other_ref[...] = back[:, own:]
    sums = [grad_out * out, grad, grad * normal, grad_field * result]
    sums = [row_sum(array) for array in sums] + [jnp.zeros((4, grad.shape[1]), FL)]
    sum_ref[0] = jnp.concatenate(sums, axis=0)


def norm2_back_call(own, back_own, got, result, fields, grads, modul, gain, bias, weight, seq):
    rows, width = result.shape
    steps = rows // CHUNK
    block, half = (CHUNK, width), (CHUNK, width // 2)
    row = lambda g: (g, 0)
    return call(
        norm2_back_kernel,
        "norm2_back",
        (steps,),
        [
            (own, block, row),
            (got, (1, CHUNK, width), lambda g: (0, g, 0)),
            (back_own, block, row),
            (got, (1, CHUNK, width), lambda g: (1, g, 0)),
            (result, block, row),
            (grads, block, row),
        ]
        + [(array, block, still(0, 0)) for array in fields]
        + [
            (modul, (1, 6, width), still(seq, 0, 0)),
            (gain, (1, width), still(0, 0)),
            (bias, (1, width), still(0, 0)),
            (weight, weight.shape, still(0, 0)),
        ],
        [(block, BF, block, still(0, 0))] * steps
        + [((rows, width), FL, block, row), ((rows, width), BF, block, row)]
        + [((rows, width // 2), BF, half, row)] * 2
        + [((steps, 8, width), FL, (1, 8, width), lambda g: (g, 0, 0))],
        2 * rows * width * width,
        32,
    )


def attend_back_kernel(
    stride, q_ref, k_ref, v_ref, own_ref, other_ref, gown_ref, gother_ref, lse_ref, cos_ref, sin_ref, out_ref
):
    pair = pl.program_id(0)
    own = out_ref.shape[1] // 3
    queries, keys, values = taken(q_ref, stride), k_ref[...], v_ref[...]
    att = jnp.concatenate([own_ref[...], other_ref[...]], axis=0)
    grads = jnp.concatenate([gown_ref[...], gother_ref[...]], axis=0)
    turned = keys.astype(FL).T.astype(BF)
    product = (att.astype(FL) * grads.astype(FL)).T
    parts, dk, dv = [], None, None
    for head in range(2):
        lanes = head_lanes(queries.shape, head)
        mine = jnp.where(lanes, queries, jnp.zeros_like(queries))
        grad = jnp.where(lanes, grads, jnp.zeros_like(grads))
        delta = jnp.sum(product[head * HEAD : (head + 1) * HEAD], axis=0, keepdims=True)
        probs = jnp.exp2(mm_nt(keys, mine) - lse_ref[0, head : head + 1, :])
        term = mm(probs.astype(BF), grad)
        dv = term if dv is None else dv + term
        scores = (probs * (mm_nt(values, grad) - delta)).astype(BF)
        term = mm(scores, mine)
        dk = term if dk is None else dk + term
        parts.append(mm(turned[head * HEAD : (head + 1) * HEAD], scores))
    dq = jnp.concatenate(parts, axis=0).T * (HEAD ** (-0.5))
    column = pl.multiple_of(pair * PAIR, PAIR)
    here = pl.ds(column, PAIR)
    cosine, sine = cos_ref[...], -sin_ref[...]
    turned = turn(dq, taken(cos_ref, stride), -taken(sin_ref, stride)).astype(BF)
    for at in range(dq.shape[0] // CHUNK):
        start = at * stride * CHUNK
        out_ref[start : start + CHUNK, here] = turned[at * CHUNK : (at + 1) * CHUNK]
        if stride > 1:
            empty = jnp.zeros(((stride - 1) * CHUNK, PAIR), BF)
            out_ref[start + CHUNK : start + stride * CHUNK, here] = empty
    turned = turn(dk * LN2, cosine, sine).astype(BF)
    out_ref[:, pl.ds(pl.multiple_of(own + column, PAIR), PAIR)] = turned
    out_ref[:, pl.ds(pl.multiple_of(2 * own + column, PAIR), PAIR)] = dv.astype(BF)


def attend_back_call(q, k, v, att, grads, lse, cosine, sine, stride):
    length, width = k.shape
    rows = length // stride
    pairs = width // PAIR
    whole = ((length, PAIR), lambda p: (0, p))
    fixed = ((length, PAIR), still(0, 0))
    return call(
        functools.partial(attend_back_kernel, stride),
        "attend_back",
        (pairs,),
        [(q, *whole), (k, *whole), (v, *whole)]
        + [(array, (rows // 2, PAIR), lambda p: (0, p)) for array in (*att, *grads)]
        + [(lse, (1, 8, rows), lambda p: (p, 0, 0)), (cosine, *fixed), (sine, *fixed)],
        [((length, 3 * width), BF, (length, 3 * width), still(0, 0))],
        20 * rows * length * width,
        52,
    )[0]


def project_kernel(x_ref, w_ref, out_ref):
    out_ref[...] = mm_nt(x_ref[...], w_ref[...]).astype(BF)


def project_call(grad, weight):
    length, columns = grad.shape
    rows, width = length // 2, weight.shape[0]
    return call(
        project_kernel,
        "project_other",
        (2,),
        [(grad, (CHUNK, columns), lambda g: (g + 2, 0)), (weight, weight.shape, still(0, 0))],
        [((rows, width), BF, (CHUNK, width), lambda g: (g, 0))],
        2 * rows * columns * width,
        20,
    )[0]


def project_own_kernel(x_ref, w_ref, got_ref, own_ref, beside_ref):
    out = mm_nt(x_ref[...], w_ref[...]) + got_ref[...].astype(FL)
    own_ref[...] = out[:CHUNK]
    beside_ref[...] = out[CHUNK:].astype(BF)


def project_own_call(grad, weight, got):
    columns, width = grad.shape[1], weight.shape[0]
    block = (CHUNK, width)
    return call(
        project_own_kernel,
        "project_own",
        (1,),
        [
            (grad, (2 * CHUNK, columns), still(0, 0)),
            (weight, weight.shape, still(0, 0)),
            (got, (2 * CHUNK, width), still(0, 0)),
        ],
        [(block, FL, block, still(0, 0)), (block, BF, block, still(0, 0))],
        4 * CHUNK * columns * width,
        20,
    )


def norm1_back(grad, field, grad_field1, mask, mod_ref, gain_ref):
    normal, scale = unit(field.astype(FL))
    grad_field = grad_field1 + unit_back(
        grad * (1.0 + mod_ref[0, 1:2]) * gain_ref[...], normal, scale
    )
    rounded = grad_field.astype(BF)
    embed = mm(mask[:, :CHUNK], rounded)
    sums = jnp.concatenate(
        [row_sum(grad), row_sum(grad * normal), embed[:1], jnp.zeros((5, grad.shape[1]), FL)], axis=0
    )
    return rounded, sums


def norm1_back_a_kernel(x_ref, w_ref, got_ref, f0, f1, k0, k1, g_ref, mod_ref, gain_ref, o0, o1, sum_ref):
    step = pl.program_id(0)
    grad = mm_nt(x_ref[...], w_ref[...]) + got_ref[...].astype(FL)
    rounded, sums = norm1_back(grad, pick((f0, f1)), g_ref[...], pick((k0, k1)), mod_ref, gain_ref)
    for at, ref in enumerate((o0, o1)):

        @pl.when(step == at)
        def _():
            ref[...] = rounded

    sum_ref[0] = sums


def norm1_back_a_call(grad_proj, weight, got, fields, grad_field1, modul, gain):
    columns, width = grad_proj.shape[1], weight.shape[0]
    block, marks = (CHUNK, width), (16, width)
    row = lambda g: (g, 0)
    return call(
        norm1_back_a_kernel,
        "norm1_back_a",
        (2,),
        [
            (grad_proj, (CHUNK, columns), row),
            (weight, weight.shape, still(0, 0)),
            (got, block, row),
        ]
        + [(field, block, still(0, 0)) for field in fields]
        + [(field, marks, still(CHUNK // 16, 0)) for field in fields]
        + [
            (grad_field1, block, row),
            (modul, (1, 6, width), still(0, 0, 0)),
            (gain, (1, width), still(0, 0)),
        ],
        [(block, BF, block, still(0, 0))] * 2
        + [((2, 8, width), FL, (1, 8, width), lambda g: (g, 0, 0))],
        4 * CHUNK * columns * width,
        24,
    )


def norm1_back_b_kernel(own_ref, got_ref, field_ref, mask_ref, g_ref, mod_ref, gain_ref, out_ref, sum_ref):
    grad = own_ref[...] + got_ref[...].astype(FL)
    rounded, sums = norm1_back(grad, field_ref[...], g_ref[...], mask_ref[...], mod_ref, gain_ref)
    out_ref[...] = rounded
    sum_ref[0] = sums


def norm1_back_b_call(own, got, field, grad_field1, modul, gain):
    width = own.shape[1]
    block = (CHUNK, width)
    return call(
        norm1_back_b_kernel,
        "norm1_back_b",
        (1,),
        [
            (own, block, still(0, 0)),
            (got, block, still(0, 0)),
            (field, block, still(0, 0)),
            (field, (16, width), still(CHUNK // 16, 0)),
            (grad_field1, block, still(0, 0)),
            (modul, (1, 6, width), still(1, 0, 0)),
            (gain, (1, width), still(0, 0)),
        ],
        [(block, BF, block, still(0, 0)), ((1, 8, width), FL, (1, 8, width), still(0, 0, 0))],
        30 * CHUNK * width,
        16,
    )


def bits_of(axis):
    return (lax.axis_size(axis) - 1).bit_length()


def partner(axis, bit):
    return [(at, at ^ (1 << bit)) for at in range(lax.axis_size(axis))]


def one_of(array, at, axis):
    return lax.dynamic_index_in_dim(array, at, axis, keepdims=False)


def after(value, *others):
    return lax.optimization_barrier((value, *others))[0]


def scatter_batch(parts):
    bits = bits_of("batch")
    place, core = lax.axis_index("batch"), lax.axis_index("mp")
    parts = [part.reshape((lax.axis_size("batch"), -1) + part.shape[1:]) for part in parts]
    for bit in reversed(range(2, bits)):
        mine = (place >> bit) & 1
        halves = [part.reshape((2, -1) + part.shape[1:]) for part in parts]
        sent = [one_of(half, 1 - mine, 0).astype(BF) for half in halves]
        got = [lax.ppermute(part, "batch", partner("batch", bit)) for part in sent]
        parts = [one_of(half, mine, 0) + part.astype(FL) for half, part in zip(halves, got)]
    x, y = place & 1, (place >> 1) & 1

    def crossing(first):
        pairs = []
        for at in range(lax.axis_size("batch")):
            for side in range(2):
                pairs.append((2 * at + side, 2 * (at ^ (1 << (side if first else 1 - side))) + side))
        return pairs

    def chosen(part, low, high):
        return jnp.stack([one_of(part, low, 0), one_of(part, high, 0)])

    along = core == 0
    sent = [
        chosen(part, jnp.where(along, 1 - x, 2 - 2 * y), jnp.where(along, 3 - x, 3 - 2 * y)) for part in parts
    ]
    kept = [chosen(part, jnp.where(along, x, 2 * y), jnp.where(along, 2 + x, 2 * y + 1)) for part in parts]
    sent = jnp.concatenate([part.astype(BF) for part in sent], axis=1)
    got = lax.ppermute(sent, ("batch", "mp"), crossing(True))
    sizes = [part.shape[1] for part in parts]
    starts = [sum(sizes[:at]) for at in range(len(sizes))]
    which = jnp.where(along, y, x)
    left = one_of(got, 1 - which, 0)
    sent = jnp.concatenate(
        [
            (one_of(part, 1 - which, 0) + left[start : start + size].astype(FL)).astype(BF)
            for part, start, size in zip(kept, starts, sizes)
        ],
        axis=0,
    )
    last = lax.ppermute(sent, ("batch", "mp"), crossing(False))
    right = one_of(got, which, 0)
    return [
        one_of(part, which, 0)
        + right[start : start + size].astype(FL)
        + last[start : start + size].astype(FL)
        for part, start, size in zip(kept, starts, sizes)
    ]


def scatter_seq(parts):
    length = lax.axis_size("seq")
    parts = [part.astype(BF).reshape((length, -1) + part.shape[1:]) for part in parts]
    sizes = [part.shape[1] for part in parts]
    starts = [sum(sizes[:at]) for at in range(len(sizes))]
    got = lax.all_to_all(jnp.concatenate(parts, axis=1), "seq", 0, 0, tiled=True)
    return [
        jnp.sum(got[:, start : start + size].astype(FL), axis=0) for start, size in zip(starts, sizes)
    ]


def routes(second, turned):
    pairs = []
    for q in range(4):
        for c in range(2):
            group = 1 - c if second else c
            chip = 2 * group + (q // 2 + turned) % 2
            pairs.append((q * 2 + c, chip * 2 + q % 2))
    return pairs


def send(block, second, turned):
    return lax.ppermute(block, ("seq", "mp"), routes(second, turned))


def send_home(block, second, turned):
    return lax.ppermute(block, ("seq", "mp"), [(to, at) for at, to in routes(second, turned)])


def swap(array):
    return lax.ppermute(array, "mp", SWAP)


def per_device(
    tokens_in,
    prefix,
    mask_bits,
    timestep,
    mask_embed,
    w_ada,
    b_ada,
    gain1,
    query_key_value_weight,
    attention_out_weight,
    gain2,
    first_up_weight,
    first_hidden_bias,
    second_down_weight,
    second_output_bias,
    cotangent,
):
    seqs, span, width = tokens_in.shape
    own = width // 2
    z, c = lax.axis_index("seq"), lax.axis_index("mp")
    upper, side = z // 2, z % 2
    devices = lax.axis_size("batch") * lax.axis_size("seq") * lax.axis_size("mp")

    places = jnp.arange(span, dtype=jnp.int32) + z * span
    masked = (places[None, :] >= prefix[:, None]) & (mask_bits == 1)

    def block_of(at):
        marks = one_of(masked, at, 0)
        block = jnp.where(marks[:, None], mask_embed, one_of(tokens_in, at, 0))
        return block, jnp.pad(marks.astype(BF)[None, :], ((0, 15), (0, width - span)))

    def marked(at):
        return jnp.concatenate(block_of(at), axis=0)

    block_a0 = send(marked(upper), False, 0)
    block_a1 = send(marked(1 - upper), False, 1)
    block_b0 = send(marked(2), True, 0)
    block_b1 = send(block_of(2)[0], True, 1)

    def back_home(blocks):
        first = send_home(blocks[0], False, 0)
        second = send_home(blocks[1], False, 1)
        third = send_home(blocks[2], True, 0)
        low, high = jnp.where(upper == 0, first, second), jnp.where(upper == 0, second, first)
        return jnp.stack([low, high, third])

    other_time = swap(timestep)
    time_a = one_of(jnp.where(c == upper, timestep, other_time), side, 0)
    time_b = jnp.where(c == upper, other_time, timestep)[2]
    cond = jax.nn.silu(time_features(jnp.stack([time_a, time_b]), w_ada.shape[0])).astype(BF)
    modul = jnp.dot(cond, w_ada, preferred_element_type=FL) + b_ada.astype(FL)
    modul = modul.reshape(2, 6, width)
    gain_one, gain_two = gain1.astype(FL)[None, :], gain2.astype(FL)[None, :]

    w_heads = jnp.concatenate(
        [
            lax.dynamic_slice_in_dim(query_key_value_weight, at * width + c * own, own, 1)
            for at in range(3)
        ],
        axis=1,
    )
    w_out = jnp.concatenate(
        [
            lax.dynamic_slice_in_dim(attention_out_weight, c * own, own, 0),
            lax.dynamic_slice_in_dim(attention_out_weight, (1 - c) * own, own, 0),
        ],
        axis=0,
    )
    quarter = jnp.stack([2 * side + c, 2 * (1 - side) + c, 2 * side + 1 - c, 2 * (1 - side) + 1 - c])
    positions = (quarter[:, None] * span + jnp.arange(span)[None, :]).reshape(-1, 1).astype(FL)
    lane = jnp.arange(PAIR)
    half = HEAD // 2
    inverse = jnp.exp(-math.log(10000.0) * (lane % half).astype(FL) / half)
    angles = positions * inverse[None, :]
    cosine = jnp.cos(angles)
    sine = jnp.sin(angles) * jnp.where(lane % HEAD < half, -1.0, 1.0)[None, :]

    block_a0, block_a1, modul, w_heads, w_out, cosine, sine = lax.optimization_barrier(
        (block_a0, block_a1, modul, w_heads, w_out, cosine, sine)
    )
    normed_a = norm1_call(block_a0, block_a1, modul, gain_one, 0)
    other_a = swap(normed_a)
    first = qkv_call(normed_a, w_heads, cosine, sine, 0, None)
    normed_a, q_a, k_a, v_a = qkv_call(other_a, w_heads, cosine, sine, 1, first)
    normed_b = norm1_call(block_b0, block_b1, modul, gain_one, 1)
    other_b = swap(normed_b)
    first = qkv_call(normed_b, w_heads, cosine, sine, 0, None)
    normed_b, q_b, k_b, v_b = qkv_call(other_b, w_heads, cosine, sine, 1, first)
    own_a, away_a, lse_a = attend_call(q_a, k_a, v_a, 1)
    got_a = swap(away_a)
    own_b, away_b, lse_b = attend_call(q_b, k_b, v_b, 2)
    got_b = swap(away_b)

    late = after(cotangent, block_b1)
    grads_a = jnp.concatenate(
        [send(one_of(late, upper, 0), False, 0), send(one_of(late, 1 - upper, 0), False, 1)], axis=0
    )
    grads_b = send(late[2], True, 0)
    grads_other_a, grads_other_b = swap(grads_a), swap(grads_b)

    fields_a, fields_b = (block_a0, block_a1), (block_b0,)
    bias1 = first_hidden_bias.astype(FL)[None, :]
    bias2 = second_output_bias.astype(FL)[None, :]
    weights = (first_up_weight, bias1, second_down_weight)
    attended_a, result_a, normed2_a = out_call(own_a, got_a, fields_a, modul, gain_two, w_out, 0)
    other_a = swap(normed2_a)
    attended_b, result_b, normed2_b = out_call(own_b, got_b, fields_b, modul, gain_two, w_out, 1)
    other_b = swap(normed2_b)
    normed2_a, mlp_a, hidden_a, before_a, out_a, back_a, sent_a, sum_b1a, sum_b2a = mlp_call(
        normed2_a, other_a, grads_a, grads_other_a, modul, *weights, 0
    )
    got_a = swap(sent_a)
    normed2_b, mlp_b, hidden_b, before_b, out_b, back_b, sent_b, sum_b1b, sum_b2b = mlp_call(
        normed2_b, other_b, grads_b, grads_other_b, modul, *weights, 1
    )
    got_b = swap(sent_b)
    grad_w1 = mm_tn(normed2_a, before_a) + mm_tn(normed2_b, before_b)
    grad_w2 = mm_tn(mlp_a, hidden_a) + mm_tn(mlp_b, hidden_b)
    grad_b2 = (sum_b2a + sum_b2b)[0]
    grad_w1, grad_w2 = scatter_batch([grad_w1, grad_w2])

    m0, m1, field1_a, attn_a, back_own_a, back_away_a, sums2_a = norm2_back_call(
        out_a, back_a, got_a, result_a, fields_a, grads_a, modul, gain_two, bias2, w_out, 0
    )
    back_other_a = swap(back_away_a)
    m2, field1_b, attn_b, back_own_b, back_away_b, sums2_b = norm2_back_call(
        out_b, back_b, got_b, result_b, fields_b, grads_b, modul, gain_two, bias2, w_out, 1
    )
    back_other_b = swap(back_away_b)
    output = back_home((m0, m1, m2))
    grad_w_out = mm_tn(attended_a, attn_a) + mm_tn(attended_b, attn_b)
    grad_w_out = grad_w_out[:own] + swap(grad_w_out[own:].astype(BF)).astype(FL)

    chips = devices // 2
    grad_b1 = (sum_b1a + sum_b1b).reshape(-1, width).astype(BF)
    grad_w_out = jnp.concatenate(
        [
            grad_w_out.astype(BF).reshape(chips, -1, width),
            jnp.broadcast_to(grad_b1[None], (chips,) + grad_b1.shape),
        ],
        axis=1,
    )
    grad_w_out = lax.all_to_all(grad_w_out, ("batch", "seq"), 0, 0, tiled=True)
    grad_w_out = jnp.sum(grad_w_out.astype(FL), axis=0)
    grad_b1 = grad_w_out[own // chips :].reshape(-1)
    grad_w_out = grad_w_out[: own // chips]

    grad_att = (back_own_b, back_other_b)
    proj_b = attend_back_call(q_b, k_b, v_b, (own_b, away_b), grad_att, lse_b, cosine, sine, 2)
    got = swap(project_call(proj_b, w_heads))
    grad_att = (back_own_a, back_other_a)
    proj_a = attend_back_call(q_a, k_a, v_a, (own_a, away_a), grad_att, lse_a, cosine, sine, 1)
    normed1_b, beside = project_own_call(proj_b, w_heads, got)
    beside = lax.ppermute(beside, "seq", partner("seq", 0))
    got = swap(project_call(proj_a, w_heads))
    home_a0, home_a1, sums_a = norm1_back_a_call(
        proj_a, w_heads, got, fields_a, field1_a, modul, gain_one
    )
    home_b, sums_b = norm1_back_b_call(normed1_b, beside, block_b0, field1_b, modul, gain_one)
    grad_home = back_home((home_a0, home_a1, home_b)).astype(FL)
    grad_tokens = jnp.where(masked[:, :, None], 0.0, grad_home)

    (grad_w_qkv,) = scatter_batch([mm_tn(normed_b, proj_b) + mm_tn(normed_a, proj_a)])
    grad_w1, grad_w2 = scatter_seq([grad_w1, grad_w2])
    grad_w2 = grad_w2.T
    (grad_w_qkv,) = scatter_seq([grad_w_qkv])

    sums1 = jnp.stack([sums_a[0] + sums_a[1], sums_b[0]])
    sums2 = jnp.stack([sums2_a[0] + sums2_a[1], sums2_b[0]])
    grad_modul = jnp.stack(
        [
            sums1[:, 0],
            sums1[:, 1] * gain_one,
            sums2[:, 3],
            sums2[:, 1],
            sums2[:, 2] * gain_two,
            sums2[:, 0],
        ],
        axis=1,
    ).reshape(2, 6 * width)
    grad_embed = sums1[0, 2] + sums1[1, 2]
    grad_gain1 = jnp.sum(sums1[:, 1] * (1.0 + modul[:, 1]), axis=0)
    grad_gain2 = jnp.sum(sums2[:, 2] * (1.0 + modul[:, 4]), axis=0)
    ada = grad_modul.shape[1] // devices
    part = width // devices
    small = jnp.concatenate(
        [
            grad_modul.reshape(2, devices, ada).transpose(1, 0, 2).reshape(devices, 2 * ada),
            jnp.stack([grad_embed, grad_gain1, grad_gain2, grad_b2])
            .reshape(4, devices, part)
            .transpose(1, 0, 2)
            .reshape(devices, 4 * part),
            jnp.broadcast_to(cond.astype(FL).reshape(1, -1), (devices, cond.size)),
        ],
        axis=1,
    )
    small = lax.all_to_all(small, ("batch", "seq", "mp"), 0, 0, tiled=True)
    all_modul = small[:, : 2 * ada].reshape(2 * devices, ada)
    vectors = jnp.sum(small[:, 2 * ada : 2 * ada + 4 * part].reshape(devices, 4, part), axis=0)
    all_cond = small[:, 2 * ada + 4 * part :].reshape(2 * devices, -1)
    g_w_ada = lax.dot_general(
        all_cond, all_modul, (((0,), (0,)), ((), ())), precision=lax.Precision.HIGHEST
    )
    g_b_ada = jnp.sum(all_modul, axis=0)

    rows = grad_w_qkv.shape[0] // 2
    mine = lax.dynamic_slice_in_dim(grad_w_qkv, c * rows, rows, 0)
    other = lax.dynamic_slice_in_dim(grad_w_qkv, (1 - c) * rows, rows, 0)
    other = swap(other.astype(BF)).astype(FL)
    low = jnp.where(c == 0, mine, other).reshape(rows, 3, own)
    high = jnp.where(c == 0, other, mine).reshape(rows, 3, own)
    g_w_qkv = jnp.concatenate([low, high], axis=2).reshape(rows, 3 * width)
    moves = [(2 * at + core, chips * core + at) for at in range(chips) for core in range(2)]
    g_w_out = lax.ppermute(grad_w_out.astype(BF), ("batch", "seq", "mp"), moves).astype(FL)
    return (
        output,
        grad_tokens,
        vectors[0],
        g_w_ada,
        g_b_ada,
        vectors[1],
        g_w_qkv,
        g_w_out,
        vectors[2],
        grad_w1,
        grad_b1,
        grad_w2,
        vectors[3],
    )


def solution(mesh):
    in_specs = (
        P(("batch", "mp"), "seq", None),
        P(("batch", "mp")),
        P(("batch", "mp"), "seq"),
        P(("batch", "mp")),
        P(),
        P(),
        P(),
        P(),
        P(),
        P(),
        P(),
        P(None, "mp"),
        P("mp"),
        P("mp", None),
        P(),
        P(("batch", "mp"), "seq", None),
    )
    out_specs = (
        P(("batch", "mp"), "seq", None),
        P(("batch", "mp"), "seq", None),
        P(("batch", "seq", "mp")),
        P(None, ("batch", "seq", "mp")),
        P(("batch", "seq", "mp")),
        P(("batch", "seq", "mp")),
        P(("batch", "seq", "mp"), None),
        P(("batch", "seq", "mp"), None),
        P(("batch", "seq", "mp")),
        P(("batch", "seq"), "mp"),
        P("mp"),
        P("mp", ("batch", "seq")),
        P(("batch", "seq", "mp")),
    )
    return jax.shard_map(
        per_device, mesh=mesh, in_specs=in_specs, out_specs=out_specs, check_vma=False
    )
```

```python
import functools
import math

import jax
import jax.numpy as jnp
from jax import lax
from jax.experimental import pallas as pl
from jax.experimental.pallas import tpu as pltpu
from jax.sharding import PartitionSpec as P

HEAD = 64
PAIR = 2 * HEAD
CHUNK = 256
LOG2E = math.log2(math.e)
LN2 = math.log(2.0)
BF = jnp.bfloat16
FL = jnp.float32
SWAP = [(0, 1), (1, 0)]


def mm(left, right):
    return lax.dot_general(left, right, (((1,), (0,)), ((), ())), preferred_element_type=FL)


def mm_nt(left, right):
    return lax.dot_general(left, right, (((1,), (1,)), ((), ())), preferred_element_type=FL)


def mm_tn(left, right):
    return lax.dot_general(left, right, (((0,), (0,)), ((), ())), preferred_element_type=FL)


def time_features(timestep, width):
    half = width // 2
    freqs = jnp.exp(-math.log(10000.0) * jnp.arange(half, dtype=FL) / half)
    angles = timestep.astype(FL)[:, None] * freqs[None, :]
    return jnp.concatenate([jnp.cos(angles), jnp.sin(angles)], axis=-1)


def unit(field):
    center = field - jnp.mean(field, axis=-1, keepdims=True)
    scale = lax.rsqrt(jnp.mean(center * center, axis=-1, keepdims=True) + 1e-05)
    return center * scale, scale


def unit_back(grad, normal, scale):
    return scale * (
        grad
        - jnp.mean(grad, axis=-1, keepdims=True)
        - normal * jnp.mean(grad * normal, axis=-1, keepdims=True)
    )


def row_sum(array):
    return jnp.sum(array, axis=0, keepdims=True)


def call(kernel, name, grid, ins, outs, flops, megabytes, aliases=None, wait=()):
    given = len(ins)
    ins = list(ins) + [(array, None, None) for array in wait]
    arrays = [entry[0] for entry in ins]

    def body(*refs):
        kernel(*refs[:given], *refs[len(ins) :])

    in_specs = [
        pl.BlockSpec(memory_space=pl.ANY) if entry[1] is None else pl.BlockSpec(entry[1], entry[2])
        for entry in ins
    ]
    moved = sum(a.size * a.dtype.itemsize for a in arrays)
    moved += sum(math.prod(o[0]) * jnp.dtype(o[1]).itemsize for o in outs)
    return pl.pallas_call(
        body,
        grid=grid,
        in_specs=in_specs,
        out_specs=[pl.BlockSpec(o[2], o[3]) for o in outs],
        out_shape=[jax.ShapeDtypeStruct(o[0], o[1]) for o in outs],
        input_output_aliases=aliases or {},
        compiler_params=pltpu.CompilerParams(vmem_limit_bytes=megabytes * 1024 * 1024),
        cost_estimate=pl.CostEstimate(flops=flops * 20, bytes_accessed=moved * 20, transcendentals=0),
        name=name,
    )(*arrays)


def still(*indices):
    return lambda *grid: indices


def pick(values):
    step = pl.program_id(0)
    chosen = values[-1][...]
    for at in reversed(range(len(values) - 1)):
        chosen = jnp.where(step == at, values[at][...], chosen)
    return chosen


def norm1_kernel(x0_ref, x1_ref, mod_ref, gain_ref, out_ref):
    for at, ref in enumerate((x0_ref, x1_ref)):
        normal, _ = unit(ref[...].astype(FL))
        normed = normal * gain_ref[...] * (1.0 + mod_ref[0, 1:2]) + mod_ref[0, 0:1]
        out_ref[at * CHUNK : (at + 1) * CHUNK] = normed.astype(BF)


def norm1_call(x0, x1, modul, gain, seq, wait):
    width = gain.shape[1]
    block = (CHUNK, width)
    return call(
        norm1_kernel,
        "norm1",
        (1,),
        [
            (x0, block, still(0, 0)),
            (x1, block, still(0, 0)),
            (modul, (1, 6, width), still(seq, 0, 0)),
            (gain, (1, width), still(0, 0)),
        ],
        [((2 * CHUNK, width), BF, (2 * CHUNK, width), still(0, 0))],
        10 * 2 * CHUNK * width,
        8,
        wait=wait,
    )[0]


def turn(tile, cosine, sine):
    lane = lax.broadcasted_iota(jnp.int32, tile.shape, 1)
    ahead = pltpu.roll(tile, PAIR - HEAD // 2, 1)
    behind = pltpu.roll(tile, HEAD // 2, 1)
    other = jnp.where(lane % HEAD < HEAD // 2, ahead, behind)
    return tile * cosine + other * sine


def qkv_kernel(x_ref, w_ref, cos_ref, sin_ref, *refs):
    copy_ref, q_ref, k_ref, v_ref = refs[-4:]
    x = x_ref[...]
    copy_ref[...] = x
    out = mm(x, w_ref[...])
    cosine, sine = cos_ref[...], sin_ref[...]
    own = q_ref.shape[1]
    for at in range(0, own, PAIR):
        here = slice(at, at + PAIR)
        q_ref[:, here] = (turn(out[:, here], cosine, sine) * (LOG2E * HEAD ** (-0.5))).astype(BF)
        k_ref[:, here] = turn(out[:, own + at : own + at + PAIR], cosine, sine).astype(BF)
    v_ref[...] = out[:, 2 * own :].astype(BF)


def qkv_call(x, weight, cosine, sine, part, earlier):
    rows, width = x.shape
    own = weight.shape[1] // 3
    steps = rows // CHUNK
    place = lambda g: (g + part * steps, 0)
    extra = [] if earlier is None else list(earlier)
    return call(
        qkv_kernel,
        "qkv",
        (steps,),
        [
            (x, (CHUNK, width), lambda g: (g, 0)),
            (weight, weight.shape, still(0, 0)),
            (cosine, (CHUNK, PAIR), place),
            (sine, (CHUNK, PAIR), place),
        ]
        + [(array, None, None) for array in extra],
        [((2 * rows, width), BF, (CHUNK, width), place)]
        + [((2 * rows, own), BF, (CHUNK, own), place)] * 3,
        2 * rows * width * 3 * own,
        14,
        {4 + i: i for i in range(len(extra))},
    )


def head_lanes(shape, head):
    lane = lax.broadcasted_iota(jnp.int32, shape, 1)
    return (lane >= head * HEAD) & (lane < (head + 1) * HEAD)


def taken(ref, stride):
    chunks = [ref[at : at + CHUNK] for at in range(0, ref.shape[0], stride * CHUNK)]
    return jnp.concatenate(chunks, axis=0)


def attend_kernel(stride, q_ref, k_ref, v_ref, own_ref, other_ref, lse_ref):
    queries = taken(q_ref, stride)
    keys = k_ref[...]
    turned = v_ref[...].astype(FL).T.astype(BF)
    ones = jnp.ones((16, turned.shape[1]), BF)
    results = []
    for head in range(2):
        mine = jnp.where(head_lanes(queries.shape, head), queries, jnp.zeros_like(queries))
        scores = mm_nt(keys, mine)
        top = jnp.max(scores, axis=0, keepdims=True)
        raised = jnp.exp2(scores - top).astype(BF)
        values = jnp.concatenate([turned[head * HEAD : (head + 1) * HEAD], ones], axis=0)
        both = mm(values, raised)
        total = both[HEAD : HEAD + 1]
        results.append(both[:HEAD] / total)
        lse_ref[0, head : head + 1, :] = top + jnp.log2(total)
    out = jnp.concatenate(results, axis=0).T.astype(BF)
    rows = own_ref.shape[0]
    own_ref[...] = out[:rows]
    other_ref[...] = out[rows:]


def attend_call(q, k, v, stride, wait):
    length, width = k.shape
    rows = length // stride
    pairs = width // PAIR
    whole = ((length, PAIR), lambda p: (0, p))
    return call(
        functools.partial(attend_kernel, stride),
        "attend",
        (pairs,),
        [(q, *whole), (k, *whole), (v, *whole)],
        [((rows // 2, width), BF, (rows // 2, PAIR), lambda p: (0, p))] * 2
        + [((pairs, 8, rows), FL, (1, 8, rows), lambda p: (p, 0, 0))],
        8 * rows * length * width,
        24,
        wait=wait,
    )


def out_kernel(own_ref, got_ref, *refs):
    fields, (mod_ref, gain_ref, w_ref, att_ref, res_ref, normed_ref) = refs[:-6], refs[-6:]
    attended = jnp.concatenate([own_ref[...], got_ref[...]], axis=1)
    att_ref[...] = attended
    result = mm(attended, w_ref[...])
    res_ref[...] = result
    field = pick(fields).astype(FL) + mod_ref[0, 2:3] * result
    normal, _ = unit(field)
    normed = normal * gain_ref[...] * (1.0 + mod_ref[0, 4:5]) + mod_ref[0, 3:4]
    normed_ref[...] = normed.astype(BF)


def out_call(own, got, fields, modul, gain, weight, seq):
    rows, width = own.shape[0], gain.shape[1]
    part = (CHUNK, width // 2)
    block = (CHUNK, width)
    row = lambda g: (g, 0)
    return call(
        out_kernel,
        "out_norm2",
        (rows // CHUNK,),
        [(own, part, row), (got, part, row)]
        + [(field, block, still(0, 0)) for field in fields]
        + [
            (modul, (1, 6, width), still(seq, 0, 0)),
            (gain, (1, width), still(0, 0)),
            (weight, weight.shape, still(0, 0)),
        ],
        [((rows, width), BF, block, row), ((rows, width), FL, block, row), ((rows, width), BF, block, row)],
        2 * rows * width * width,
        14,
    )


def mlp_kernel(
    x_ref, xo_ref, c_ref, co_ref, mod_ref, w1_ref, b1_ref, w2_ref,
    copy_ref, grad_ref, hidden_ref, before_ref, out_ref, back_ref, away_ref, bsum_ref, gsum_ref,
):
    step = pl.program_id(0)
    first = step == 0
    owns = step < pl.num_programs(0) // 2
    x = jnp.where(owns, x_ref[...], xo_ref[...])
    copy_ref[...] = x
    grad = jnp.where(owns, c_ref[...], co_ref[...])
    grad = (mod_ref[0, 5:6] * grad.astype(FL)).astype(BF)
    grad_ref[...] = grad
    units = w1_ref.shape[1]
    size = units // 3
    root = math.sqrt(2.0 / math.pi)
    total, back = None, None
    for at in range(0, units, size):
        here = slice(at, at + size)
        before = mm(x, w1_ref[:, here]) + b1_ref[:, here]
        square = before * before
        inner = jnp.tanh(before * (root + (root * 0.044715) * square))
        half = 0.5 * (1.0 + inner)
        hidden = (before * half).astype(BF)
        slope = half + (0.5 * before) * (1.0 - inner * inner) * (root + (3.0 * root * 0.044715) * square)
        grad_before = (mm_nt(grad, w2_ref[here]) * slope).astype(BF)
        hidden_ref[:, here] = hidden
        before_ref[:, here] = grad_before
        add = row_sum(grad_before.astype(FL))
        bsum_ref[:, here] = jnp.where(first, add, bsum_ref[:, here] + add)
        term = mm(hidden, w2_ref[here])
        total = term if total is None else total + term
        term = mm_nt(grad_before, w1_ref[:, here])
        back = term if back is None else back + term

    @pl.when(owns)
    def _():
        out_ref[...] = total
        back_ref[...] = back
        add = row_sum(grad.astype(FL))
        gsum_ref[...] = jnp.where(first, add, gsum_ref[...] + add)

    @pl.when(jnp.logical_not(owns))
    def _():
        away_ref[0] = total.astype(BF)
        away_ref[1] = back.astype(BF)


def mlp_call(x, x_other, grads, grads_other, modul, w1, b1, w2, seq, wait):
    rows, width = x.shape
    units = w1.shape[1]
    steps = rows // CHUNK
    block = (CHUNK, width)
    row = lambda g: (g, 0)
    early = lambda g: (jnp.minimum(g, steps - 1), 0)
    late = lambda g: (jnp.maximum(g - steps, 0), 0)
    return call(
        mlp_kernel,
        "mlp",
        (2 * steps,),
        [
            (x, block, early),
            (x_other, block, late),
            (grads, block, early),
            (grads_other, block, late),
            (modul, (1, 6, width), still(seq, 0, 0)),
            (w1, w1.shape, still(0, 0)),
            (b1, b1.shape, still(0, 0)),
            (w2, w2.shape, still(0, 0)),
        ],
        [((2 * rows, width), BF, block, row)] * 2
        + [((2 * rows, units), BF, (CHUNK, units), row)] * 2
        + [((rows, width), FL, block, early)] * 2
        + [((2, rows, width), BF, (2, CHUNK, width), lambda g: (0, jnp.maximum(g - steps, 0), 0))]
        + [((1, units), FL, (1, units), still(0, 0)), ((1, width), FL, (1, width), still(0, 0))],
        16 * rows * width * units,
        28,
        wait=wait,
    )


def norm2_back_kernel(own_ref, got_ref, bown_ref, bgot_ref, res_ref, c_ref, *refs):
    blocks = (len(refs) - 9) // 2
    fields, refs = refs[:blocks], refs[blocks:]
    mod_ref, gain_ref, b2_ref, w_ref = refs[:4]
    outs, (field_ref, attn_ref, mine_ref, other_ref, sum_ref) = refs[4:-5], refs[-5:]
    step = pl.program_id(0)
    mod = lambda at: mod_ref[0, at : at + 1]
    grad_out = c_ref[...].astype(FL)
    result = res_ref[...]
    field = pick(fields).astype(FL) + mod(2) * result
    out = own_ref[...] + got_ref[0].astype(FL) + b2_ref[...]
    mixed = (field + mod(5) * out).astype(BF)
    for at, ref in enumerate(outs):

        @pl.when(step == at)
        def _():
            ref[...] = mixed

    grad = bown_ref[...] + bgot_ref[0].astype(FL)
    normal, scale = unit(field)
    grad_field = grad_out + unit_back(grad * (1.0 + mod(4)) * gain_ref[...], normal, scale)
    field_ref[...] = grad_field
    grad_attn = (mod(2) * grad_field).astype(BF)
    attn_ref[...] = grad_attn
    back = mm_nt(grad_attn, w_ref[...]).astype(BF)
    own = mine_ref.shape[1]
    mine_ref[...] = back[:, :own]
    other_ref[...] = back[:, own:]
    sums = [grad_out * out, grad, grad * normal, grad_field * result]
    sums = [row_sum(array) for array in sums] + [jnp.zeros((4, grad.shape[1]), FL)]
    sum_ref[0] = jnp.concatenate(sums, axis=0)


def norm2_back_call(own, back_own, got, result, fields, grads, modul, gain, bias, weight, seq, wait):
    rows, width = result.shape
    steps = rows // CHUNK
    block, half = (CHUNK, width), (CHUNK, width // 2)
    row = lambda g: (g, 0)
    return call(
        norm2_back_kernel,
        "norm2_back",
        (steps,),
        [
            (own, block, row),
            (got, (1, CHUNK, width), lambda g: (0, g, 0)),
            (back_own, block, row),
            (got, (1, CHUNK, width), lambda g: (1, g, 0)),
            (result, block, row),
            (grads, block, row),
        ]
        + [(array, block, still(0, 0)) for array in fields]
        + [
            (modul, (1, 6, width), still(seq, 0, 0)),
            (gain, (1, width), still(0, 0)),
            (bias, (1, width), still(0, 0)),
            (weight, weight.shape, still(0, 0)),
        ],
        [(block, BF, block, still(0, 0))] * steps
        + [((rows, width), FL, block, row), ((rows, width), BF, block, row)]
        + [((rows, width // 2), BF, half, row)] * 2
        + [((steps, 8, width), FL, (1, 8, width), lambda g: (g, 0, 0))],
        2 * rows * width * width,
        20,
        wait=wait,
    )


def attend_back_kernel(
    stride, q_ref, k_ref, v_ref, own_ref, other_ref, gown_ref, gother_ref, lse_ref, cos_ref, sin_ref, *refs
):
    out_ref = refs[-1]
    queries, keys, values = taken(q_ref, stride), k_ref[...], v_ref[...]
    att = jnp.concatenate([own_ref[...], other_ref[...]], axis=0)
    grads = jnp.concatenate([gown_ref[...], gother_ref[...]], axis=0)
    turned = keys.astype(FL).T.astype(BF)
    product = (att.astype(FL) * grads.astype(FL)).T
    parts, dk, dv = [], None, None
    for head in range(2):
        lanes = head_lanes(queries.shape, head)
        mine = jnp.where(lanes, queries, jnp.zeros_like(queries))
        grad = jnp.where(lanes, grads, jnp.zeros_like(grads))
        delta = jnp.sum(product[head * HEAD : (head + 1) * HEAD], axis=0, keepdims=True)
        probs = jnp.exp2(mm_nt(keys, mine) - lse_ref[0, head : head + 1, :])
        term = mm(probs.astype(BF), grad)
        dv = term if dv is None else dv + term
        scores = (probs * (mm_nt(values, grad) - delta)).astype(BF)
        term = mm(scores, mine)
        dk = term if dk is None else dk + term
        parts.append(mm(turned[head * HEAD : (head + 1) * HEAD], scores))
    dq = jnp.concatenate(parts, axis=0).T * (HEAD ** (-0.5))
    cosine, sine = cos_ref[...], -sin_ref[...]
    turned = turn(dq, taken(cos_ref, stride), -taken(sin_ref, stride)).astype(BF)
    for at in range(dq.shape[0] // CHUNK):
        start = at * stride * CHUNK
        out_ref[start : start + CHUNK, :PAIR] = turned[at * CHUNK : (at + 1) * CHUNK]
        if stride > 1:
            empty = jnp.zeros(((stride - 1) * CHUNK, PAIR), BF)
            out_ref[start + CHUNK : start + stride * CHUNK, :PAIR] = empty
    out_ref[:, PAIR : 2 * PAIR] = turn(dk * LN2, cosine, sine).astype(BF)
    out_ref[:, 2 * PAIR :] = dv.astype(BF)


def attend_back_call(q, k, v, att, grads, lse, cosine, sine, stride, first, pairs, earlier, wait):
    length, width = k.shape
    rows = length // stride
    column = lambda p: (0, first + p)
    whole = ((length, PAIR), column)
    fixed = ((length, PAIR), still(0, 0))
    ins = [(q, *whole), (k, *whole), (v, *whole)]
    ins += [(array, (rows // 2, PAIR), column) for array in (*att, *grads)]
    ins += [(lse, (1, 8, rows), lambda p: (first + p, 0, 0)), (cosine, *fixed), (sine, *fixed)]
    aliases = {}
    if earlier is not None:
        aliases = {len(ins): 0}
        ins.append((earlier, None, None))
    return call(
        functools.partial(attend_back_kernel, stride),
        "attend_back",
        (pairs,),
        ins,
        [((length, 3 * width), BF, (length, 3 * PAIR), column)],
        20 * rows * length * PAIR * pairs,
        34,
        aliases,
        wait,
    )[0]


def project_back(grad_ref, w_ref):
    own, result = w_ref.shape[1] // 3, None
    for at in range(0, own, PAIR):
        weight = jnp.concatenate([w_ref[:, start + at : start + at + PAIR] for start in (0, own, 2 * own)], axis=1)
        term = mm_nt(grad_ref[:, 3 * at : 3 * (at + PAIR)], weight)
        result = term if result is None else result + term
    return result


def project_kernel(grad_ref, w_ref, out_ref):
    out_ref[...] = project_back(grad_ref, w_ref).astype(BF)


def project_call(grad, weight):
    length = grad.shape[0]
    rows, width = length // 2, weight.shape[0]
    return call(
        project_kernel,
        "project_other",
        (2,),
        [(grad, (CHUNK, grad.shape[1]), lambda g: (g + 2, 0)), (weight, weight.shape, still(0, 0))],
        [((rows, width), BF, (CHUNK, width), lambda g: (g, 0))],
        2 * rows * weight.size,
        14,
    )[0]


def project_own_kernel(grad_ref, w_ref, got_ref, own_ref, beside_ref):
    out = project_back(grad_ref, w_ref) + got_ref[...].astype(FL)
    own_ref[...] = out[:CHUNK]
    beside_ref[...] = out[CHUNK:].astype(BF)


def project_own_call(grad, weight, got):
    width = weight.shape[0]
    block = (CHUNK, width)
    return call(
        project_own_kernel,
        "project_own",
        (1,),
        [
            (grad, (2 * CHUNK, grad.shape[1]), still(0, 0)),
            (weight, weight.shape, still(0, 0)),
            (got, (2 * CHUNK, width), still(0, 0)),
        ],
        [(block, FL, block, still(0, 0)), (block, BF, block, still(0, 0))],
        4 * CHUNK * weight.size,
        16,
    )


def norm1_back(grad, field, grad_field1, mask, mod_ref, gain_ref):
    normal, scale = unit(field.astype(FL))
    grad_field = grad_field1 + unit_back(
        grad * (1.0 + mod_ref[0, 1:2]) * gain_ref[...], normal, scale
    )
    rounded = grad_field.astype(BF)
    embed = mm(mask[:, :CHUNK], rounded)
    sums = jnp.concatenate(
        [row_sum(grad), row_sum(grad * normal), embed[:1], jnp.zeros((5, grad.shape[1]), FL)], axis=0
    )
    return rounded, sums


def norm1_back_a_kernel(
    grad_ref, w_ref, got_ref, f0, f1, k0, k1, g_ref, mod_ref, gain_ref, o0, o1, sum_ref
):
    step = pl.program_id(0)
    grad = project_back(grad_ref, w_ref) + got_ref[...].astype(FL)
    rounded, sums = norm1_back(grad, pick((f0, f1)), g_ref[...], pick((k0, k1)), mod_ref, gain_ref)
    for at, ref in enumerate((o0, o1)):

        @pl.when(step == at)
        def _():
            ref[...] = rounded

    sum_ref[0] = sums


def norm1_back_a_call(grad_proj, weight, got, fields, grad_field1, modul, gain, wait):
    width = weight.shape[0]
    block, marks = (CHUNK, width), (16, width)
    row = lambda g: (g, 0)
    return call(
        norm1_back_a_kernel,
        "norm1_back_a",
        (2,),
        [
            (grad_proj, (CHUNK, grad_proj.shape[1]), row),
            (weight, weight.shape, still(0, 0)),
            (got, block, row),
        ]
        + [(field, block, still(0, 0)) for field in fields]
        + [(field, marks, still(CHUNK // 16, 0)) for field in fields]
        + [
            (grad_field1, block, row),
            (modul, (1, 6, width), still(0, 0, 0)),
            (gain, (1, width), still(0, 0)),
        ],
        [(block, BF, block, still(0, 0))] * 2
        + [((2, 8, width), FL, (1, 8, width), lambda g: (g, 0, 0))],
        4 * CHUNK * weight.size,
        20,
        wait=wait,
    )


def norm1_back_b_kernel(own_ref, got_ref, field_ref, mask_ref, g_ref, mod_ref, gain_ref, out_ref, sum_ref):
    grad = own_ref[...] + got_ref[...].astype(FL)
    rounded, sums = norm1_back(grad, field_ref[...], g_ref[...], mask_ref[...], mod_ref, gain_ref)
    out_ref[...] = rounded
    sum_ref[0] = sums


def norm1_back_b_call(own, got, field, grad_field1, modul, gain):
    width = own.shape[1]
    block = (CHUNK, width)
    return call(
        norm1_back_b_kernel,
        "norm1_back_b",
        (1,),
        [
            (own, block, still(0, 0)),
            (got, block, still(0, 0)),
            (field, block, still(0, 0)),
            (field, (16, width), still(CHUNK // 16, 0)),
            (grad_field1, block, still(0, 0)),
            (modul, (1, 6, width), still(1, 0, 0)),
            (gain, (1, width), still(0, 0)),
        ],
        [(block, BF, block, still(0, 0)), ((1, 8, width), FL, (1, 8, width), still(0, 0, 0))],
        30 * CHUNK * width,
        10,
    )


def bits_of(axis):
    return (lax.axis_size(axis) - 1).bit_length()


def partner(axis, bit):
    return [(at, at ^ (1 << bit)) for at in range(lax.axis_size(axis))]


def one_of(array, at, axis):
    return lax.dynamic_index_in_dim(array, at, axis, keepdims=False)


def after(value, *others):
    if not others:
        return value
    return lax.optimization_barrier((value, *others))[0]


def first_send(part):
    place, core = lax.axis_index("batch") & 3, lax.axis_index("mp")
    x, y = place & 1, place >> 1
    along = core == 0
    low, high = jnp.where(along, 1 - x, 2 - 2 * y), jnp.where(along, 3 - x, 3 - 2 * y)
    sent = jnp.stack([one_of(part, low, 0), one_of(part, high, 0)]).astype(BF)
    again = jnp.where(along, x + 2 - 2 * y, 2 * y + 1 - x)
    return sent, again, 2 * y + x, jnp.where(along, y, x)


def crossing(first):
    pairs = []
    for at in range(lax.axis_size("batch")):
        for side in range(2):
            pairs.append((2 * at + side, 2 * (at ^ (1 << (side if first else 1 - side))) + side))
    return pairs


def total(terms):
    result = terms[0].astype(FL)
    for term in terms[1:]:
        result = result + term.astype(FL)
    return result


def scatter_steps(parts):
    batch, seq = lax.axis_size("batch"), lax.axis_size("seq")
    place, z = lax.axis_index("batch"), lax.axis_index("seq")
    parts = [part.reshape((batch, seq, -1) + part.shape[1:]) for part in parts]
    for bit in reversed(range(2, bits_of("batch"))):
        mine = (place >> bit) & 1
        halves = [part.reshape((2, -1) + part.shape[1:]) for part in parts]
        got = [lax.ppermute(one_of(half, 1 - mine, 0).astype(BF), "batch", partner("batch", bit)) for half in halves]
        parts = [one_of(half, mine, 0) + part.astype(FL) for half, part in zip(halves, got)]
    sent, again, stays, which = zip(*[first_send(part) for part in parts])
    again, stays, which = again[0], stays[0], which[0]
    sent = jnp.stack(sent, axis=1)
    gates = yield sent
    got = after(lax.ppermute(sent, ("batch", "mp"), crossing(True)), *gates)
    left, right = one_of(got, 1 - which, 0), one_of(got, which, 0)
    sent = jnp.stack([total([one_of(part, again, 0), left[at]]).astype(BF) for at, part in enumerate(parts)])
    gates = yield sent
    last = after(lax.ppermute(sent, ("batch", "mp"), crossing(False)), *gates)
    terms = [[one_of(part, stays, 0), right[at], last[at]] for at, part in enumerate(parts)]
    low, high = z % 2, z // 2
    chosen = [[jnp.stack([one_of(t, 1 - low, 0), one_of(t, 3 - low, 0)]) for t in part] for part in terms]
    sent = jnp.stack([total(part).astype(BF) for part in chosen])
    gates = yield sent
    near = after(lax.ppermute(sent, "seq", partner("seq", 0)), *gates)
    chosen = [
        [one_of(t, 2 * (1 - high) + low, 0) for t in part] + [one_of(near[at], 1 - high, 0)]
        for at, part in enumerate(terms)
    ]
    sent = jnp.stack([total(part).astype(BF) for part in chosen])
    gates = yield sent
    far = after(lax.ppermute(sent, "seq", partner("seq", 1)), *gates)
    yield [
        total([one_of(t, z, 0) for t in part] + [one_of(near[at], high, 0), far[at]])
        for at, part in enumerate(terms)
    ]


def routes(second, turned):
    pairs = []
    for q in range(4):
        for c in range(2):
            group = 1 - c if second else c
            chip = 2 * group + (q // 2 + turned) % 2
            pairs.append((q * 2 + c, chip * 2 + q % 2))
    return pairs


def send(block, second, turned):
    return lax.ppermute(block, ("seq", "mp"), routes(second, turned))


def send_home(block, second, turned):
    return lax.ppermute(block, ("seq", "mp"), [(to, at) for at, to in routes(second, turned)])


def swap(array):
    return lax.ppermute(array, "mp", SWAP)


def per_device(
    tokens_in,
    prefix,
    mask_bits,
    timestep,
    mask_embed,
    w_ada,
    b_ada,
    gain1,
    query_key_value_weight,
    attention_out_weight,
    gain2,
    first_up_weight,
    first_hidden_bias,
    second_down_weight,
    second_output_bias,
    cotangent,
):
    seqs, span, width = tokens_in.shape
    own = width // 2
    z, c = lax.axis_index("seq"), lax.axis_index("mp")
    upper, side = z // 2, z % 2
    devices = lax.axis_size("batch") * lax.axis_size("seq") * lax.axis_size("mp")

    places = jnp.arange(span, dtype=jnp.int32) + z * span
    masked = (places[None, :] >= prefix[:, None]) & (mask_bits == 1)

    def marked(tokens, at):
        marks = one_of(masked, at, 0)
        block = jnp.where(marks[:, None], mask_embed, one_of(tokens, at, 0))
        return jnp.concatenate([block, jnp.pad(marks.astype(BF)[None, :], ((0, 15), (0, width - span)))], axis=0)

    block_a0, block_a1 = marked(tokens_in, upper), marked(tokens_in, 1 - upper)
    def arrange(first, second, third):
        low, high = jnp.where(upper == 0, first, second), jnp.where(upper == 0, second, first)
        return jnp.stack([low, high, third])

    def back_home(blocks, *others):
        first = send_home(blocks[0], False, 0)
        second = send_home(blocks[1], False, 1)
        third = send_home(blocks[2], True, 0)
        return arrange(*lax.optimization_barrier((first, second, third, *others))[:3])

    other_time = swap(timestep)
    time_a = one_of(jnp.where(c == upper, timestep, other_time), side, 0)
    time_b = jnp.where(c == upper, other_time, timestep)[2]
    cond = jax.nn.silu(time_features(jnp.stack([time_a, time_b]), w_ada.shape[0])).astype(BF)
    modul = jnp.dot(cond, w_ada, preferred_element_type=FL) + b_ada.astype(FL)
    modul = modul.reshape(2, 6, width)
    gain_one, gain_two = gain1.astype(FL)[None, :], gain2.astype(FL)[None, :]

    pairs = own // PAIR
    pairs = own // PAIR

    w_heads = jnp.concatenate(
        [
            lax.dynamic_slice_in_dim(query_key_value_weight, at * width + c * own, own, 1)
            for at in range(3)
        ],
        axis=1,
    )
    w_out = jnp.concatenate([attention_out_weight[own:], attention_out_weight[:own]], axis=0)
    w_out = jnp.where(c == 0, attention_out_weight, w_out)
    quarter = jnp.stack([2 * side + c, 2 * (1 - side) + c, 2 * side + 1 - c, 2 * (1 - side) + 1 - c])
    positions = (quarter[:, None] * span + jnp.arange(span)[None, :]).reshape(-1, 1).astype(FL)
    lane = jnp.arange(PAIR)
    half = HEAD // 2
    inverse = jnp.exp(-math.log(10000.0) * (lane % half).astype(FL) / half)
    angles = positions * inverse[None, :]
    cosine = jnp.cos(angles)
    sine = jnp.sin(angles) * jnp.where(lane % HEAD < half, -1.0, 1.0)[None, :]

    block_b = marked(after(tokens_in, block_a0, block_a1), 2)
    block_a0, block_a1 = send(block_a0, False, 0), send(block_a1, False, 1)
    block_b0, block_b1 = send(block_b, True, 0), send(block_b, True, 1)

    block_a0, block_a1, modul, w_heads, w_out, cosine, sine = lax.optimization_barrier(
        (block_a0, block_a1, modul, w_heads, w_out, cosine, sine)
    )
    normed_a = norm1_call(block_a0, block_a1, modul, gain_one, 0, [block_b])
    other_a = swap(normed_a)
    first = qkv_call(normed_a, w_heads, cosine, sine, 0, None)
    normed_a, q_a, k_a, v_a = qkv_call(other_a, w_heads, cosine, sine, 1, first)
    normed_own_b = norm1_call(block_b0, block_b1, modul, gain_one, 1, [q_a])
    other_b, late = swap(normed_own_b), after(cotangent, normed_own_b)
    late = one_of(late, upper, 0), one_of(late, 1 - upper, 0), late[2]
    first = qkv_call(normed_own_b, w_heads, cosine, sine, 0, None)
    normed_b, q_b, k_b, v_b = qkv_call(other_b, w_heads, cosine, sine, 1, first)
    own_a, away_a, lse_a = attend_call(q_a, k_a, v_a, 1, [normed_own_b, *late])
    got_a = swap(away_a)
    own_b, away_b, lse_b = attend_call(q_b, k_b, v_b, 2, [])
    got_b = swap(away_b)

    grads_b = send(late[2], True, 0)
    grads_a = jnp.concatenate([send(late[0], False, 0), send(late[1], False, 1)], axis=0)
    grads_other_a, grads_other_b = swap(grads_a), swap(grads_b)

    fields_a, fields_b = (block_a0, block_a1), (block_b0,)
    bias1 = first_hidden_bias.astype(FL)[None, :]
    bias2 = second_output_bias.astype(FL)[None, :]
    weights = (first_up_weight, bias1, second_down_weight)
    attended_a, result_a, normed2_a = out_call(own_a, got_a, fields_a, modul, gain_two, w_out, 0)
    other_a = swap(normed2_a)
    attended_b, result_b, normed2_b = out_call(own_b, got_b, fields_b, modul, gain_two, w_out, 1)
    other_b = swap(normed2_b)
    normed2_b, mlp_b, hidden_b, before_b, out_b, back_b, sent_b, sum_b1b, sum_b2b = mlp_call(
        normed2_b, other_b, grads_b, grads_other_b, modul, *weights, 1, []
    )
    got_b = swap(sent_b)
    normed2_a, mlp_a, hidden_a, before_a, out_a, back_a, sent_a, sum_b1a, sum_b2a = mlp_call(
        normed2_a, other_a, grads_a, grads_other_a, modul, *weights, 0, [sent_b]
    )
    got_a = swap(sent_a)
    grad_w1 = (mm_tn(normed2_b, before_b) + mm_tn(normed2_a, before_a)).astype(BF)
    grad_w2 = (mm_tn(mlp_b, hidden_b) + mm_tn(mlp_a, hidden_a)).astype(BF)
    grad_b2 = (sum_b2a + sum_b2b)[0]
    gather_w = scatter_steps([grad_w1, grad_w2])
    sent_w = next(gather_w)

    m2, field1_b, attn_b, back_own_b, back_away_b, sums2_b = norm2_back_call(
        out_b, back_b, got_b, result_b, fields_b, grads_b, modul, gain_two, bias2, w_out, 1, [sent_w]
    )
    back_other_b = swap(back_away_b)
    m0, m1, field1_a, attn_a, back_own_a, back_away_a, sums2_a = norm2_back_call(
        out_a, back_a, got_a, result_a, fields_a, grads_a, modul, gain_two, bias2, w_out, 0, [back_away_b]
    )
    back_other_a = swap(back_away_a)
    grad_w_out = mm_tn(attended_a, attn_a) + mm_tn(attended_b, attn_b)
    out_away = grad_w_out[own:].astype(BF)
    grad_w_out = grad_w_out[:own] + swap(out_away).astype(FL)

    chips = devices // 2
    grad_b1 = (sum_b1a + sum_b1b).reshape(-1, width).astype(BF)
    grad_w_out = jnp.concatenate(
        [
            grad_w_out.astype(BF).reshape(chips, -1, width),
            jnp.broadcast_to(grad_b1[None], (chips,) + grad_b1.shape),
        ],
        axis=1,
    )
    out_sent = grad_w_out
    grad_w_out = lax.all_to_all(grad_w_out, ("batch", "seq"), 0, 0, tiled=True)

    proj_b = attend_back_call(
        q_b, k_b, v_b, (own_b, away_b), (back_own_b, back_other_b), lse_b, cosine, sine, 2, 0, pairs, None,
        [back_other_a, out_sent],
    )
    away_b = project_call(proj_b, w_heads)
    got = swap(away_b)
    qkv_b = mm_tn(normed_b, after(proj_b, away_b))
    sent_w = gather_w.send([away_b])
    normed1_b, beside = project_own_call(proj_b, w_heads, got)
    got = lax.ppermute(beside, "seq", partner("seq", 0))

    grad_w_out = jnp.sum(grad_w_out.astype(FL), axis=0)
    grad_b1 = grad_w_out[own // chips :].reshape(-1)
    grad_w_out = grad_w_out[: own // chips]

    def attention_back_a(first, count, earlier, wait):
        return attend_back_call(
            q_a, k_a, v_a, (own_a, away_a), (back_own_a, back_other_a), lse_a, cosine, sine, 1, first, count,
            earlier, wait,
        )

    proj_a = attention_back_a(0, pairs - 1, None, [beside, sent_w, qkv_b])
    sent_w = gather_w.send([proj_a])
    home_b, sums_b = norm1_back_b_call(normed1_b, after(got, proj_a), block_b0, field1_b, modul, gain_one)
    output = back_home((m0, m1, m2), proj_a)
    home_b = send_home(home_b, True, 0)
    proj_a = attention_back_a(pairs - 1, 1, proj_a, [sums_b, sent_w, output, grad_w_out])
    sent_w = gather_w.send([proj_a])
    away = project_call(after(proj_a, sent_w), w_heads)
    got = swap(away)
    gather_qkv = scatter_steps([(qkv_b + mm_tn(normed_a, after(proj_a, away))).astype(BF)])
    sent_qkv = next(gather_qkv)
    home_a0, home_a1, sums_a = norm1_back_a_call(
        proj_a, w_heads, got, fields_a, field1_a, modul, gain_one, [sent_qkv]
    )
    home_a0, home_a1 = send_home(home_a0, False, 0), send_home(home_a1, False, 1)
    grad_home = arrange(home_a0, home_a1, home_b).astype(FL)
    grad_w1, grad_w2 = gather_w.send([sums_a])
    sent_qkv = gather_qkv.send([sums_a, grad_w1, grad_w2])
    grad_w2 = grad_w2.T
    sums_a = after(sums_a, sent_qkv)
    sent_qkv = gather_qkv.send([sums_a])
    sent_qkv = gather_qkv.send([sums_a])
    last_sent = sent_qkv
    (grad_w_qkv,) = gather_qkv.send([sums_a])
    grad_tokens = jnp.where(masked[:, :, None], 0.0, grad_home)

    sums1 = jnp.stack([sums_a[0] + sums_a[1], sums_b[0]])
    sums2 = jnp.stack([sums2_a[0] + sums2_a[1], sums2_b[0]])
    grad_modul = jnp.stack(
        [
            sums1[:, 0],
            sums1[:, 1] * gain_one,
            sums2[:, 3],
            sums2[:, 1],
            sums2[:, 2] * gain_two,
            sums2[:, 0],
        ],
        axis=1,
    ).reshape(2, 6 * width)
    grad_embed = sums1[0, 2] + sums1[1, 2]
    grad_gain1 = jnp.sum(sums1[:, 1] * (1.0 + modul[:, 1]), axis=0)
    grad_gain2 = jnp.sum(sums2[:, 2] * (1.0 + modul[:, 4]), axis=0)
    ada = grad_modul.shape[1] // devices
    part = width // devices
    small = jnp.concatenate(
        [
            grad_modul.reshape(2, devices, ada).transpose(1, 0, 2).reshape(devices, 2 * ada),
            jnp.stack([grad_embed, grad_gain1, grad_gain2, grad_b2])
            .reshape(4, devices, part)
            .transpose(1, 0, 2)
            .reshape(devices, 4 * part),
            jnp.broadcast_to(cond.astype(FL).reshape(1, -1), (devices, cond.size)),
        ],
        axis=1,
    )
    small = after(lax.all_to_all(small, ("batch", "seq", "mp"), 0, 0, tiled=True), last_sent)
    all_modul = small[:, : 2 * ada].reshape(2 * devices, ada)
    vectors = jnp.sum(small[:, 2 * ada : 2 * ada + 4 * part].reshape(devices, 4, part), axis=0)
    all_cond = small[:, 2 * ada + 4 * part :].reshape(2 * devices, -1)
    g_w_ada = lax.dot_general(
        all_cond, all_modul, (((0,), (0,)), ((), ())), precision=lax.Precision.HIGHEST
    )
    g_b_ada = jnp.sum(all_modul, axis=0)

    rows = grad_w_qkv.shape[0] // 2
    mine = lax.dynamic_slice_in_dim(grad_w_qkv, c * rows, rows, 0)
    other = lax.dynamic_slice_in_dim(grad_w_qkv, (1 - c) * rows, rows, 0)
    other = swap(other.astype(BF)).astype(FL)
    low, high = jnp.where(c == 0, mine, other), jnp.where(c == 0, other, mine)
    g_w_qkv = jnp.concatenate(
        [
            half[:, (3 * pair + part) * PAIR : (3 * pair + part + 1) * PAIR]
            for part in range(3)
            for half in (low, high)
            for pair in range(pairs)
        ],
        axis=1,
    )
    moves = [(2 * at + core, chips * core + at) for at in range(chips) for core in range(2)]
    g_w_out = lax.ppermute(grad_w_out.astype(BF), ("batch", "seq", "mp"), moves).astype(FL)
    return (
        output,
        grad_tokens,
        vectors[0],
        g_w_ada,
        g_b_ada,
        vectors[1],
        g_w_qkv,
        g_w_out,
        vectors[2],
        grad_w1,
        grad_b1,
        grad_w2,
        vectors[3],
    )


def solution(mesh):
    in_specs = (
        P(("batch", "mp"), "seq", None),
        P(("batch", "mp")),
        P(("batch", "mp"), "seq"),
        P(("batch", "mp")),
        P(),
        P(),
        P(),
        P(),
        P(),
        P(),
        P(),
        P(None, "mp"),
        P("mp"),
        P("mp", None),
        P(),
        P(("batch", "mp"), "seq", None),
    )
    out_specs = (
        P(("batch", "mp"), "seq", None),
        P(("batch", "mp"), "seq", None),
        P(("batch", "seq", "mp")),
        P(None, ("batch", "seq", "mp")),
        P(("batch", "seq", "mp")),
        P(("batch", "seq", "mp")),
        P(("batch", "seq", "mp"), None),
        P(("batch", "seq", "mp"), None),
        P(("batch", "seq", "mp")),
        P(("batch", "seq"), "mp"),
        P("mp"),
        P("mp", ("batch", "seq")),
        P(("batch", "seq", "mp")),
    )
    return jax.shard_map(
        per_device, mesh=mesh, in_specs=in_specs, out_specs=out_specs, check_vma=False
    )
```

```python
import functools
import math

import jax
import jax.numpy as jnp
from jax import lax
from jax.experimental import pallas as pl
from jax.experimental.pallas import tpu as pltpu
from jax.sharding import PartitionSpec as P

HEAD = 64
PAIR = 2 * HEAD
CHUNK = 256
LOG2E = math.log2(math.e)
LN2 = math.log(2.0)
BF = jnp.bfloat16
FL = jnp.float32
SWAP = [(0, 1), (1, 0)]


def mm(left, right):
    return lax.dot_general(left, right, (((1,), (0,)), ((), ())), preferred_element_type=FL)


def mm_nt(left, right):
    return lax.dot_general(left, right, (((1,), (1,)), ((), ())), preferred_element_type=FL)


def mm_tn(left, right):
    return lax.dot_general(left, right, (((0,), (0,)), ((), ())), preferred_element_type=FL)


def time_features(timestep, width):
    half = width // 2
    freqs = jnp.exp(-math.log(10000.0) * jnp.arange(half, dtype=FL) / half)
    angles = timestep.astype(FL)[:, None] * freqs[None, :]
    return jnp.concatenate([jnp.cos(angles), jnp.sin(angles)], axis=-1)


def unit(field):
    center = field - jnp.mean(field, axis=-1, keepdims=True)
    scale = lax.rsqrt(jnp.mean(center * center, axis=-1, keepdims=True) + 1e-05)
    return center * scale, scale


def unit_back(grad, normal, scale):
    return scale * (
        grad
        - jnp.mean(grad, axis=-1, keepdims=True)
        - normal * jnp.mean(grad * normal, axis=-1, keepdims=True)
    )


def row_sum(array):
    return jnp.sum(array, axis=0, keepdims=True)


def call(kernel, name, grid, ins, outs, micros, megabytes, aliases=None, wait=()):
    given = len(ins)
    ins = list(ins) + [(array, None, None) for array in wait]
    arrays = [entry[0] for entry in ins]

    def body(*refs):
        kernel(*refs[:given], *refs[len(ins) :])

    in_specs = [
        pl.BlockSpec(memory_space=pl.ANY) if entry[1] is None else pl.BlockSpec(entry[1], entry[2])
        for entry in ins
    ]
    return pl.pallas_call(
        body,
        grid=grid,
        in_specs=in_specs,
        out_specs=[pl.BlockSpec(o[2], o[3]) for o in outs],
        out_shape=[jax.ShapeDtypeStruct(o[0], o[1]) for o in outs],
        input_output_aliases=aliases or {},
        compiler_params=pltpu.CompilerParams(vmem_limit_bytes=megabytes * 1024 * 1024),
        cost_estimate=pl.CostEstimate(flops=int(micros * 2e9), bytes_accessed=0, transcendentals=0),
        name=name,
    )(*arrays)


def still(*indices):
    return lambda *grid: indices


def pick(values):
    step = pl.program_id(0)
    chosen = values[-1][...]
    for at in reversed(range(len(values) - 1)):
        chosen = jnp.where(step == at, values[at][...], chosen)
    return chosen


def norm1_kernel(x0_ref, x1_ref, mod_ref, gain_ref, out_ref):
    for at, ref in enumerate((x0_ref, x1_ref)):
        normal, _ = unit(ref[...].astype(FL))
        normed = normal * gain_ref[...] * (1.0 + mod_ref[0, 1:2]) + mod_ref[0, 0:1]
        out_ref[at * CHUNK : (at + 1) * CHUNK] = normed.astype(BF)


def norm1_call(x0, x1, modul, gain, seq, wait):
    width = gain.shape[1]
    block = (CHUNK, width)
    return call(
        norm1_kernel,
        "norm1",
        (1,),
        [
            (x0, block, still(0, 0)),
            (x1, block, still(0, 0)),
            (modul, (1, 6, width), still(seq, 0, 0)),
            (gain, (1, width), still(0, 0)),
        ],
        [((2 * CHUNK, width), BF, (2 * CHUNK, width), still(0, 0))],
        1.5,
        8,
        wait=wait,
    )[0]


def turn(tile, cosine, sine):
    lane = lax.broadcasted_iota(jnp.int32, tile.shape, 1)
    ahead = pltpu.roll(tile, PAIR - HEAD // 2, 1)
    behind = pltpu.roll(tile, HEAD // 2, 1)
    other = jnp.where(lane % HEAD < HEAD // 2, ahead, behind)
    return tile * cosine + other * sine


def qkv_kernel(x_ref, w_ref, cos_ref, sin_ref, *refs):
    copy_ref, q_ref, k_ref, v_ref = refs[-4:]
    x = x_ref[...]
    copy_ref[...] = x
    out = mm(x, w_ref[...])
    cosine, sine = cos_ref[...], sin_ref[...]
    own = q_ref.shape[1]
    for at in range(0, own, PAIR):
        here = slice(at, at + PAIR)
        q_ref[:, here] = (turn(out[:, here], cosine, sine) * (LOG2E * HEAD ** (-0.5))).astype(BF)
        k_ref[:, here] = turn(out[:, own + at : own + at + PAIR], cosine, sine).astype(BF)
    v_ref[...] = out[:, 2 * own :].astype(BF)


def qkv_call(x, weight, cosine, sine, part, earlier):
    rows, width = x.shape
    own = weight.shape[1] // 3
    steps = rows // CHUNK
    place = lambda g: (g + part * steps, 0)
    extra = [] if earlier is None else list(earlier)
    return call(
        qkv_kernel,
        "qkv",
        (steps,),
        [
            (x, (CHUNK, width), lambda g: (g, 0)),
            (weight, weight.shape, still(0, 0)),
            (cosine, (CHUNK, PAIR), place),
            (sine, (CHUNK, PAIR), place),
        ]
        + [(array, None, None) for array in extra],
        [((2 * rows, width), BF, (CHUNK, width), place)]
        + [((2 * rows, own), BF, (CHUNK, own), place)] * 3,
        1.6,
        14,
        {4 + i: i for i in range(len(extra))},
    )


def head_lanes(shape, head):
    lane = lax.broadcasted_iota(jnp.int32, shape, 1)
    return (lane >= head * HEAD) & (lane < (head + 1) * HEAD)


def taken(ref, stride):
    chunks = [ref[at : at + CHUNK] for at in range(0, ref.shape[0], stride * CHUNK)]
    return jnp.concatenate(chunks, axis=0)


def attend_kernel(stride, q_ref, k_ref, v_ref, own_ref, other_ref, lse_ref):
    queries = taken(q_ref, stride)
    keys = k_ref[...]
    turned = v_ref[...].astype(FL).T.astype(BF)
    ones = jnp.ones((16, turned.shape[1]), BF)
    results = []
    for head in range(2):
        mine = jnp.where(head_lanes(queries.shape, head), queries, jnp.zeros_like(queries))
        scores = mm_nt(keys, mine)
        top = jnp.max(scores, axis=0, keepdims=True)
        raised = jnp.exp2(scores - top).astype(BF)
        values = jnp.concatenate([turned[head * HEAD : (head + 1) * HEAD], ones], axis=0)
        both = mm(values, raised)
        total = both[HEAD : HEAD + 1]
        results.append(both[:HEAD] / total)
        lse_ref[0, head : head + 1, :] = top + jnp.log2(total)
    out = jnp.concatenate(results, axis=0).T.astype(BF)
    rows = own_ref.shape[0]
    own_ref[...] = out[:rows]
    other_ref[...] = out[rows:]


def attend_call(q, k, v, stride, wait):
    length, width = k.shape
    rows = length // stride
    pairs = width // PAIR
    whole = ((length, PAIR), lambda p: (0, p))
    return call(
        functools.partial(attend_kernel, stride),
        "attend",
        (pairs,),
        [(q, *whole), (k, *whole), (v, *whole)],
        [((rows // 2, width), BF, (rows // 2, PAIR), lambda p: (0, p))] * 2
        + [((pairs, 8, rows), FL, (1, 8, rows), lambda p: (p, 0, 0))],
        3.5 + 6.2 * rows / length,
        24,
        wait=wait,
    )


def out_kernel(own_ref, got_ref, *refs):
    fields, (mod_ref, gain_ref, w_ref, att_ref, res_ref, normed_ref) = refs[:-6], refs[-6:]
    attended = jnp.concatenate([own_ref[...], got_ref[...]], axis=1)
    att_ref[...] = attended
    result = mm(attended, w_ref[...])
    res_ref[...] = result
    field = pick(fields).astype(FL) + mod_ref[0, 2:3] * result
    normal, _ = unit(field)
    normed = normal * gain_ref[...] * (1.0 + mod_ref[0, 4:5]) + mod_ref[0, 3:4]
    normed_ref[...] = normed.astype(BF)


def out_call(own, got, fields, modul, gain, weight, seq):
    rows, width = own.shape[0], gain.shape[1]
    part = (CHUNK, width // 2)
    block = (CHUNK, width)
    row = lambda g: (g, 0)
    return call(
        out_kernel,
        "out_norm2",
        (rows // CHUNK,),
        [(own, part, row), (got, part, row)]
        + [(field, block, still(0, 0)) for field in fields]
        + [
            (modul, (1, 6, width), still(seq, 0, 0)),
            (gain, (1, width), still(0, 0)),
            (weight, weight.shape, still(0, 0)),
        ],
        [((rows, width), BF, block, row), ((rows, width), FL, block, row), ((rows, width), BF, block, row)],
        1.7 * rows / CHUNK,
        14,
    )


def mlp_kernel(
    x_ref, xo_ref, c_ref, co_ref, mod_ref, w1_ref, b1_ref, w2_ref,
    copy_ref, grad_ref, hidden_ref, before_ref, out_ref, back_ref, away_ref, bsum_ref, gsum_ref,
):
    step = pl.program_id(0)
    first = step == 0
    owns = step < pl.num_programs(0) // 2
    x = jnp.where(owns, x_ref[...], xo_ref[...])
    copy_ref[...] = x
    grad = jnp.where(owns, c_ref[...], co_ref[...])
    grad = (mod_ref[0, 5:6] * grad.astype(FL)).astype(BF)
    grad_ref[...] = grad
    units = w1_ref.shape[1]
    size = units // 3
    root = math.sqrt(2.0 / math.pi)
    total, back = None, None
    for at in range(0, units, size):
        here = slice(at, at + size)
        before = mm(x, w1_ref[:, here]) + b1_ref[:, here]
        square = before * before
        inner = jnp.tanh(before * (root + (root * 0.044715) * square))
        half = 0.5 * (1.0 + inner)
        hidden = (before * half).astype(BF)
        slope = half + (0.5 * before) * (1.0 - inner * inner) * (root + (3.0 * root * 0.044715) * square)
        grad_before = (mm_nt(grad, w2_ref[here]) * slope).astype(BF)
        hidden_ref[:, here] = hidden
        before_ref[:, here] = grad_before
        add = row_sum(grad_before.astype(FL))
        bsum_ref[:, here] = jnp.where(first, add, bsum_ref[:, here] + add)
        term = mm(hidden, w2_ref[here])
        total = term if total is None else total + term
        term = mm_nt(grad_before, w1_ref[:, here])
        back = term if back is None else back + term

    @pl.when(owns)
    def _():
        out_ref[...] = total
        back_ref[...] = back
        add = row_sum(grad.astype(FL))
        gsum_ref[...] = jnp.where(first, add, gsum_ref[...] + add)

    @pl.when(jnp.logical_not(owns))
    def _():
        away_ref[0] = total.astype(BF)
        away_ref[1] = back.astype(BF)


def mlp_call(x, x_other, grads, grads_other, modul, w1, b1, w2, seq, wait):
    rows, width = x.shape
    units = w1.shape[1]
    steps = rows // CHUNK
    block = (CHUNK, width)
    row = lambda g: (g, 0)
    early = lambda g: (jnp.minimum(g, steps - 1), 0)
    late = lambda g: (jnp.maximum(g - steps, 0), 0)
    return call(
        mlp_kernel,
        "mlp",
        (2 * steps,),
        [
            (x, block, early),
            (x_other, block, late),
            (grads, block, early),
            (grads_other, block, late),
            (modul, (1, 6, width), still(seq, 0, 0)),
            (w1, w1.shape, still(0, 0)),
            (b1, b1.shape, still(0, 0)),
            (w2, w2.shape, still(0, 0)),
        ],
        [((2 * rows, width), BF, block, row)] * 2
        + [((2 * rows, units), BF, (CHUNK, units), row)] * 2
        + [((rows, width), FL, block, early)] * 2
        + [((2, rows, width), BF, (2, CHUNK, width), lambda g: (0, jnp.maximum(g - steps, 0), 0))]
        + [((1, units), FL, (1, units), still(0, 0)), ((1, width), FL, (1, width), still(0, 0))],
        8.0 * rows / CHUNK,
        28,
        wait=wait,
    )


def norm2_back_kernel(own_ref, got_ref, bown_ref, bgot_ref, res_ref, c_ref, *refs):
    blocks = (len(refs) - 9) // 2
    fields, refs = refs[:blocks], refs[blocks:]
    mod_ref, gain_ref, b2_ref, w_ref = refs[:4]
    outs, (field_ref, attn_ref, mine_ref, other_ref, sum_ref) = refs[4:-5], refs[-5:]
    step = pl.program_id(0)
    mod = lambda at: mod_ref[0, at : at + 1]
    grad_out = c_ref[...].astype(FL)
    result = res_ref[...]
    field = pick(fields).astype(FL) + mod(2) * result
    out = own_ref[...] + got_ref[0].astype(FL) + b2_ref[...]
    mixed = (field + mod(5) * out).astype(BF)
    for at, ref in enumerate(outs):

        @pl.when(step == at)
        def _():
            ref[...] = mixed

    grad = bown_ref[...] + bgot_ref[0].astype(FL)
    normal, scale = unit(field)
    grad_field = grad_out + unit_back(grad * (1.0 + mod(4)) * gain_ref[...], normal, scale)
    field_ref[...] = grad_field
    grad_attn = (mod(2) * grad_field).astype(BF)
    attn_ref[...] = grad_attn
    back = mm_nt(grad_attn, w_ref[...]).astype(BF)
    own = mine_ref.shape[1]
    mine_ref[...] = back[:, :own]
    other_ref[...] = back[:, own:]
    sums = [grad_out * out, grad, grad * normal, grad_field * result]
    sums = [row_sum(array) for array in sums] + [jnp.zeros((4, grad.shape[1]), FL)]
    sum_ref[0] = jnp.concatenate(sums, axis=0)


def norm2_back_call(own, back_own, got, result, fields, grads, modul, gain, bias, weight, seq, wait):
    rows, width = result.shape
    steps = rows // CHUNK
    block, half = (CHUNK, width), (CHUNK, width // 2)
    row = lambda g: (g, 0)
    return call(
        norm2_back_kernel,
        "norm2_back",
        (steps,),
        [
            (own, block, row),
            (got, (1, CHUNK, width), lambda g: (0, g, 0)),
            (back_own, block, row),
            (got, (1, CHUNK, width), lambda g: (1, g, 0)),
            (result, block, row),
            (grads, block, row),
        ]
        + [(array, block, still(0, 0)) for array in fields]
        + [
            (modul, (1, 6, width), still(seq, 0, 0)),
            (gain, (1, width), still(0, 0)),
            (bias, (1, width), still(0, 0)),
            (weight, weight.shape, still(0, 0)),
        ],
        [(block, BF, block, still(0, 0))] * steps
        + [((rows, width), FL, block, row), ((rows, width), BF, block, row)]
        + [((rows, width // 2), BF, half, row)] * 2
        + [((steps, 8, width), FL, (1, 8, width), lambda g: (g, 0, 0))],
        3.0 * rows / CHUNK,
        20,
        wait=wait,
    )


def attend_back_kernel(
    stride, q_ref, k_ref, v_ref, own_ref, other_ref, gown_ref, gother_ref, lse_ref, cos_ref, sin_ref, *refs
):
    out_ref = refs[-1]
    queries, keys, values = taken(q_ref, stride), k_ref[...], v_ref[...]
    att = jnp.concatenate([own_ref[...], other_ref[...]], axis=0)
    grads = jnp.concatenate([gown_ref[...], gother_ref[...]], axis=0)
    turned = keys.astype(FL).T.astype(BF)
    product = (att.astype(FL) * grads.astype(FL)).T
    parts, dk, dv = [], None, None
    for head in range(2):
        lanes = head_lanes(queries.shape, head)
        mine = jnp.where(lanes, queries, jnp.zeros_like(queries))
        grad = jnp.where(lanes, grads, jnp.zeros_like(grads))
        delta = jnp.sum(product[head * HEAD : (head + 1) * HEAD], axis=0, keepdims=True)
        probs = jnp.exp2(mm_nt(keys, mine) - lse_ref[0, head : head + 1, :])
        term = mm(probs.astype(BF), grad)
        dv = term if dv is None else dv + term
        scores = (probs * (mm_nt(values, grad) - delta)).astype(BF)
        term = mm(scores, mine)
        dk = term if dk is None else dk + term
        parts.append(mm(turned[head * HEAD : (head + 1) * HEAD], scores))
    dq = jnp.concatenate(parts, axis=0).T * (HEAD ** (-0.5))
    cosine, sine = cos_ref[...], -sin_ref[...]
    turned = turn(dq, taken(cos_ref, stride), -taken(sin_ref, stride)).astype(BF)
    for at in range(dq.shape[0] // CHUNK):
        start = at * stride * CHUNK
        out_ref[start : start + CHUNK, :PAIR] = turned[at * CHUNK : (at + 1) * CHUNK]
        if stride > 1:
            empty = jnp.zeros(((stride - 1) * CHUNK, PAIR), BF)
            out_ref[start + CHUNK : start + stride * CHUNK, :PAIR] = empty
    out_ref[:, PAIR : 2 * PAIR] = turn(dk * LN2, cosine, sine).astype(BF)
    out_ref[:, 2 * PAIR :] = dv.astype(BF)


def attend_back_call(q, k, v, att, grads, lse, cosine, sine, stride, first, pairs, earlier, wait):
    length, width = k.shape
    rows = length // stride
    column = lambda p: (0, first + p)
    whole = ((length, PAIR), column)
    fixed = ((length, PAIR), still(0, 0))
    ins = [(q, *whole), (k, *whole), (v, *whole)]
    ins += [(array, (rows // 2, PAIR), column) for array in (*att, *grads)]
    ins += [(lse, (1, 8, rows), lambda p: (first + p, 0, 0)), (cosine, *fixed), (sine, *fixed)]
    aliases = {}
    if earlier is not None:
        aliases = {len(ins): 0}
        ins.append((earlier, None, None))
    return call(
        functools.partial(attend_back_kernel, stride),
        "attend_back",
        (pairs,),
        ins,
        [((length, 3 * width), BF, (length, 3 * PAIR), column)],
        (1.0 + 5.0 * rows / length) * pairs,
        34,
        aliases,
        wait,
    )[0]


def project_back(grad_ref, w_ref):
    own, result = w_ref.shape[1] // 3, None
    for at in range(0, own, PAIR):
        weight = jnp.concatenate([w_ref[:, start + at : start + at + PAIR] for start in (0, own, 2 * own)], axis=1)
        term = mm_nt(grad_ref[:, 3 * at : 3 * (at + PAIR)], weight)
        result = term if result is None else result + term
    return result


def project_kernel(grad_ref, w_ref, out_ref):
    out_ref[...] = project_back(grad_ref, w_ref).astype(BF)


def project_call(grad, weight):
    length = grad.shape[0]
    rows, width = length // 2, weight.shape[0]
    return call(
        project_kernel,
        "project_other",
        (2,),
        [(grad, (CHUNK, grad.shape[1]), lambda g: (g + 2, 0)), (weight, weight.shape, still(0, 0))],
        [((rows, width), BF, (CHUNK, width), lambda g: (g, 0))],
        1.8,
        14,
    )[0]


def project_own_kernel(grad_ref, w_ref, got_ref, own_ref, beside_ref):
    out = project_back(grad_ref, w_ref) + got_ref[...].astype(FL)
    own_ref[...] = out[:CHUNK]
    beside_ref[...] = out[CHUNK:].astype(BF)


def project_own_call(grad, weight, got):
    width = weight.shape[0]
    block = (CHUNK, width)
    return call(
        project_own_kernel,
        "project_own",
        (1,),
        [
            (grad, (2 * CHUNK, grad.shape[1]), still(0, 0)),
            (weight, weight.shape, still(0, 0)),
            (got, (2 * CHUNK, width), still(0, 0)),
        ],
        [(block, FL, block, still(0, 0)), (block, BF, block, still(0, 0))],
        1.8,
        16,
    )


def norm1_back(grad, field, grad_field1, mask, mod_ref, gain_ref):
    normal, scale = unit(field.astype(FL))
    grad_field = grad_field1 + unit_back(
        grad * (1.0 + mod_ref[0, 1:2]) * gain_ref[...], normal, scale
    )
    rounded = grad_field.astype(BF)
    embed = mm(mask[:, :CHUNK], rounded)
    sums = jnp.concatenate(
        [row_sum(grad), row_sum(grad * normal), embed[:1], jnp.zeros((5, grad.shape[1]), FL)], axis=0
    )
    return rounded, sums


def norm1_back_a_kernel(
    grad_ref, w_ref, got_ref, f0, f1, k0, k1, g_ref, mod_ref, gain_ref, o0, o1, sum_ref
):
    step = pl.program_id(0)
    grad = project_back(grad_ref, w_ref) + got_ref[...].astype(FL)
    rounded, sums = norm1_back(grad, pick((f0, f1)), g_ref[...], pick((k0, k1)), mod_ref, gain_ref)
    for at, ref in enumerate((o0, o1)):

        @pl.when(step == at)
        def _():
            ref[...] = rounded

    sum_ref[0] = sums


def norm1_back_a_call(grad_proj, weight, got, fields, grad_field1, modul, gain, wait):
    width = weight.shape[0]
    block, marks = (CHUNK, width), (16, width)
    row = lambda g: (g, 0)
    return call(
        norm1_back_a_kernel,
        "norm1_back_a",
        (2,),
        [
            (grad_proj, (CHUNK, grad_proj.shape[1]), row),
            (weight, weight.shape, still(0, 0)),
            (got, block, row),
        ]
        + [(field, block, still(0, 0)) for field in fields]
        + [(field, marks, still(CHUNK // 16, 0)) for field in fields]
        + [
            (grad_field1, block, row),
            (modul, (1, 6, width), still(0, 0, 0)),
            (gain, (1, width), still(0, 0)),
        ],
        [(block, BF, block, still(0, 0))] * 2
        + [((2, 8, width), FL, (1, 8, width), lambda g: (g, 0, 0))],
        4.0,
        20,
        wait=wait,
    )


def norm1_back_b_kernel(own_ref, got_ref, field_ref, mask_ref, g_ref, mod_ref, gain_ref, out_ref, sum_ref):
    grad = own_ref[...] + got_ref[...].astype(FL)
    rounded, sums = norm1_back(grad, field_ref[...], g_ref[...], mask_ref[...], mod_ref, gain_ref)
    out_ref[...] = rounded
    sum_ref[0] = sums


def norm1_back_b_call(own, got, field, grad_field1, modul, gain):
    width = own.shape[1]
    block = (CHUNK, width)
    return call(
        norm1_back_b_kernel,
        "norm1_back_b",
        (1,),
        [
            (own, block, still(0, 0)),
            (got, block, still(0, 0)),
            (field, block, still(0, 0)),
            (field, (16, width), still(CHUNK // 16, 0)),
            (grad_field1, block, still(0, 0)),
            (modul, (1, 6, width), still(1, 0, 0)),
            (gain, (1, width), still(0, 0)),
        ],
        [(block, BF, block, still(0, 0)), ((1, 8, width), FL, (1, 8, width), still(0, 0, 0))],
        1.2,
        10,
    )


def bits_of(axis):
    return (lax.axis_size(axis) - 1).bit_length()


def partner(axis, bit):
    return [(at, at ^ (1 << bit)) for at in range(lax.axis_size(axis))]


def one_of(array, at, axis):
    return lax.dynamic_index_in_dim(array, at, axis, keepdims=False)


def after(value, *others):
    if not others:
        return value
    return lax.optimization_barrier((value, *others))[0]


def first_send(part):
    place, core = lax.axis_index("batch") & 3, lax.axis_index("mp")
    x, y = place & 1, place >> 1
    along = core == 0
    low, high = jnp.where(along, 1 - x, 2 - 2 * y), jnp.where(along, 3 - x, 3 - 2 * y)
    sent = jnp.stack([one_of(part, low, 0), one_of(part, high, 0)]).astype(BF)
    again = jnp.where(along, x + 2 - 2 * y, 2 * y + 1 - x)
    return sent, again, 2 * y + x, jnp.where(along, y, x)


def crossing(first):
    pairs = []
    for at in range(lax.axis_size("batch")):
        for side in range(2):
            pairs.append((2 * at + side, 2 * (at ^ (1 << (side if first else 1 - side))) + side))
    return pairs


def total(terms):
    result = terms[0].astype(FL)
    for term in terms[1:]:
        result = result + term.astype(FL)
    return result


def scatter_steps(parts):
    batch, seq = lax.axis_size("batch"), lax.axis_size("seq")
    place, z = lax.axis_index("batch"), lax.axis_index("seq")
    parts = [part.reshape((batch, seq, -1) + part.shape[1:]) for part in parts]
    for bit in reversed(range(2, bits_of("batch"))):
        mine = (place >> bit) & 1
        halves = [part.reshape((2, -1) + part.shape[1:]) for part in parts]
        got = [lax.ppermute(one_of(half, 1 - mine, 0).astype(BF), "batch", partner("batch", bit)) for half in halves]
        parts = [one_of(half, mine, 0) + part.astype(FL) for half, part in zip(halves, got)]
    sent, again, stays, which = zip(*[first_send(part) for part in parts])
    again, stays, which = again[0], stays[0], which[0]
    sent = jnp.stack(sent, axis=1)
    gates = yield sent
    got = after(lax.ppermute(sent, ("batch", "mp"), crossing(True)), *gates)
    left, right = one_of(got, 1 - which, 0), one_of(got, which, 0)
    sent = jnp.stack([total([one_of(part, again, 0), left[at]]).astype(BF) for at, part in enumerate(parts)])
    gates = yield sent
    last = after(lax.ppermute(sent, ("batch", "mp"), crossing(False)), *gates)
    terms = [[one_of(part, stays, 0), right[at], last[at]] for at, part in enumerate(parts)]
    low, high = z % 2, z // 2
    chosen = [[jnp.stack([one_of(t, 1 - low, 0), one_of(t, 3 - low, 0)]) for t in part] for part in terms]
    sent = jnp.stack([total(part).astype(BF) for part in chosen])
    gates = yield sent
    near = after(lax.ppermute(sent, "seq", partner("seq", 0)), *gates)
    chosen = [
        [one_of(t, 2 * (1 - high) + low, 0) for t in part] + [one_of(near[at], 1 - high, 0)]
        for at, part in enumerate(terms)
    ]
    sent = jnp.stack([total(part).astype(BF) for part in chosen])
    gates = yield sent
    far = after(lax.ppermute(sent, "seq", partner("seq", 1)), *gates)
    yield [
        total([one_of(t, z, 0) for t in part] + [one_of(near[at], high, 0), far[at]])
        for at, part in enumerate(terms)
    ]


def routes(second, turned):
    pairs = []
    for q in range(4):
        for c in range(2):
            group = 1 - c if second else c
            chip = 2 * group + (q // 2 + turned) % 2
            pairs.append((q * 2 + c, chip * 2 + q % 2))
    return pairs


def send(block, second, turned):
    return lax.ppermute(block, ("seq", "mp"), routes(second, turned))


def send_home(block, second, turned):
    return lax.ppermute(block, ("seq", "mp"), [(to, at) for at, to in routes(second, turned)])


def swap(array):
    return lax.ppermute(array, "mp", SWAP)


def per_device(
    tokens_in,
    prefix,
    mask_bits,
    timestep,
    mask_embed,
    w_ada,
    b_ada,
    gain1,
    query_key_value_weight,
    attention_out_weight,
    gain2,
    first_up_weight,
    first_hidden_bias,
    second_down_weight,
    second_output_bias,
    cotangent,
):
    seqs, span, width = tokens_in.shape
    own = width // 2
    z, c = lax.axis_index("seq"), lax.axis_index("mp")
    upper, side = z // 2, z % 2
    devices = lax.axis_size("batch") * lax.axis_size("seq") * lax.axis_size("mp")

    places = jnp.arange(span, dtype=jnp.int32) + z * span
    masked = (places[None, :] >= prefix[:, None]) & (mask_bits == 1)

    def marked(tokens, at):
        marks = one_of(masked, at, 0)
        block = jnp.where(marks[:, None], mask_embed, one_of(tokens, at, 0))
        return jnp.concatenate([block, jnp.pad(marks.astype(BF)[None, :], ((0, 15), (0, width - span)))], axis=0)

    block_a0, block_a1 = marked(tokens_in, upper), marked(tokens_in, 1 - upper)
    def arrange(first, second, third):
        low, high = jnp.where(upper == 0, first, second), jnp.where(upper == 0, second, first)
        return jnp.stack([low, high, third])

    def back_home(blocks, *others):
        first = send_home(blocks[0], False, 0)
        second = send_home(blocks[1], False, 1)
        third = send_home(blocks[2], True, 0)
        return arrange(*lax.optimization_barrier((first, second, third, *others))[:3])

    other_time = swap(timestep)
    time_a = one_of(jnp.where(c == upper, timestep, other_time), side, 0)
    time_b = jnp.where(c == upper, other_time, timestep)[2]
    cond = jax.nn.silu(time_features(jnp.stack([time_a, time_b]), w_ada.shape[0])).astype(BF)
    modul = jnp.dot(cond, w_ada, preferred_element_type=FL) + b_ada.astype(FL)
    modul = modul.reshape(2, 6, width)
    gain_one, gain_two = gain1.astype(FL)[None, :], gain2.astype(FL)[None, :]

    pairs = own // PAIR
    pairs = own // PAIR

    w_heads = jnp.concatenate(
        [
            lax.dynamic_slice_in_dim(query_key_value_weight, at * width + c * own, own, 1)
            for at in range(3)
        ],
        axis=1,
    )
    w_out = jnp.concatenate([attention_out_weight[own:], attention_out_weight[:own]], axis=0)
    w_out = jnp.where(c == 0, attention_out_weight, w_out)
    quarter = jnp.stack([2 * side + c, 2 * (1 - side) + c, 2 * side + 1 - c, 2 * (1 - side) + 1 - c])
    positions = (quarter[:, None] * span + jnp.arange(span)[None, :]).reshape(-1, 1).astype(FL)
    lane = jnp.arange(PAIR)
    half = HEAD // 2
    inverse = jnp.exp(-math.log(10000.0) * (lane % half).astype(FL) / half)
    angles = positions * inverse[None, :]
    cosine = jnp.cos(angles)
    sine = jnp.sin(angles) * jnp.where(lane % HEAD < half, -1.0, 1.0)[None, :]

    block_b = marked(after(tokens_in, block_a0, block_a1), 2)
    block_a0, block_a1 = send(block_a0, False, 0), send(block_a1, False, 1)
    block_b0, block_b1 = send(block_b, True, 0), send(block_b, True, 1)

    block_a0, block_a1, modul, w_heads, w_out, cosine, sine = lax.optimization_barrier(
        (block_a0, block_a1, modul, w_heads, w_out, cosine, sine)
    )
    normed_a = norm1_call(block_a0, block_a1, modul, gain_one, 0, [block_b])
    other_a = swap(normed_a)
    first = qkv_call(normed_a, w_heads, cosine, sine, 0, None)
    normed_a, q_a, k_a, v_a = qkv_call(other_a, w_heads, cosine, sine, 1, first)
    normed_own_b = norm1_call(block_b0, block_b1, modul, gain_one, 1, [q_a])
    other_b, late = swap(normed_own_b), after(cotangent, normed_own_b)
    late = one_of(late, upper, 0), one_of(late, 1 - upper, 0), late[2]
    first = qkv_call(normed_own_b, w_heads, cosine, sine, 0, None)
    normed_b, q_b, k_b, v_b = qkv_call(other_b, w_heads, cosine, sine, 1, first)
    own_a, away_a, lse_a = attend_call(q_a, k_a, v_a, 1, [normed_own_b, *late])
    got_a = swap(away_a)
    own_b, away_b, lse_b = attend_call(q_b, k_b, v_b, 2, [])
    got_b = swap(away_b)

    grads_b = send(late[2], True, 0)
    grads_a = jnp.concatenate([send(late[0], False, 0), send(late[1], False, 1)], axis=0)
    grads_other_a, grads_other_b = swap(grads_a), swap(grads_b)

    fields_a, fields_b = (block_a0, block_a1), (block_b0,)
    bias1 = first_hidden_bias.astype(FL)[None, :]
    bias2 = second_output_bias.astype(FL)[None, :]
    weights = (first_up_weight, bias1, second_down_weight)
    attended_a, result_a, normed2_a = out_call(own_a, got_a, fields_a, modul, gain_two, w_out, 0)
    other_a = swap(normed2_a)
    attended_b, result_b, normed2_b = out_call(own_b, got_b, fields_b, modul, gain_two, w_out, 1)
    other_b = swap(normed2_b)
    normed2_b, mlp_b, hidden_b, before_b, out_b, back_b, sent_b, sum_b1b, sum_b2b = mlp_call(
        normed2_b, other_b, grads_b, grads_other_b, modul, *weights, 1, []
    )
    got_b = swap(sent_b)
    normed2_a, mlp_a, hidden_a, before_a, out_a, back_a, sent_a, sum_b1a, sum_b2a = mlp_call(
        normed2_a, other_a, grads_a, grads_other_a, modul, *weights, 0, [sent_b]
    )
    got_a = swap(sent_a)
    m2, field1_b, attn_b, back_own_b, back_away_b, sums2_b = norm2_back_call(
        out_b, back_b, got_b, result_b, fields_b, grads_b, modul, gain_two, bias2, w_out, 1, [sent_a]
    )
    back_other_b = swap(back_away_b)
    before_a, hidden_a = lax.optimization_barrier((before_a, hidden_a, back_away_b))[:2]
    grad_w1 = (mm_tn(normed2_b, before_b) + mm_tn(normed2_a, before_a)).astype(BF)
    grad_w2 = (mm_tn(mlp_b, hidden_b) + mm_tn(mlp_a, hidden_a)).astype(BF)
    grad_b2 = (sum_b2a + sum_b2b)[0]
    gather_w = scatter_steps([grad_w1, grad_w2])
    sent_w = next(gather_w)

    m0, m1, field1_a, attn_a, back_own_a, back_away_a, sums2_a = norm2_back_call(
        out_a, back_a, got_a, result_a, fields_a, grads_a, modul, gain_two, bias2, w_out, 0, [sent_w]
    )
    back_other_a = swap(back_away_a)
    grad_w_out = mm_tn(attended_a, attn_a) + mm_tn(attended_b, attn_b)
    out_away = grad_w_out[own:].astype(BF)
    grad_w_out = grad_w_out[:own] + swap(out_away).astype(FL)

    chips = devices // 2
    grad_b1 = (sum_b1a + sum_b1b).reshape(-1, width).astype(BF)
    grad_w_out = jnp.concatenate(
        [
            grad_w_out.astype(BF).reshape(chips, -1, width),
            jnp.broadcast_to(grad_b1[None], (chips,) + grad_b1.shape),
        ],
        axis=1,
    )
    out_sent = grad_w_out
    grad_w_out = lax.all_to_all(grad_w_out, ("batch", "seq"), 0, 0, tiled=True)

    proj_b = attend_back_call(
        q_b, k_b, v_b, (own_b, away_b), (back_own_b, back_other_b), lse_b, cosine, sine, 2, 0, pairs, None,
        [back_other_a, out_sent],
    )
    away_b = project_call(proj_b, w_heads)
    got = swap(away_b)
    qkv_b = mm_tn(normed_b, after(proj_b, away_b))
    sent_w = gather_w.send([away_b])
    normed1_b, beside = project_own_call(proj_b, w_heads, got)
    got = lax.ppermute(beside, "seq", partner("seq", 0))

    def attention_back_a(first, count, earlier, wait):
        return attend_back_call(
            q_a, k_a, v_a, (own_a, away_a), (back_own_a, back_other_a), lse_a, cosine, sine, 1, first, count,
            earlier, wait,
        )

    proj_a = attention_back_a(0, pairs - 1, None, [beside, sent_w, qkv_b])
    sent_w = gather_w.send([proj_a])
    home_b, sums_b = norm1_back_b_call(normed1_b, after(got, sent_w), block_b0, field1_b, modul, gain_one)
    output = back_home((m0, m1, m2), sums_b)
    home_b = send_home(home_b, True, 0)
    proj_a = attention_back_a(pairs - 1, 1, proj_a, [sums_b, sent_w, output])
    away = project_call(proj_a, w_heads)
    got = swap(away)
    gather_qkv = scatter_steps([(qkv_b + mm_tn(normed_a, after(proj_a, away))).astype(BF)])
    sent_qkv = next(gather_qkv)
    sent_w = gather_w.send([sent_qkv])
    home_a0, home_a1, sums_a = norm1_back_a_call(
        proj_a, w_heads, got, fields_a, field1_a, modul, gain_one, [sent_qkv, sent_w, home_b]
    )
    home_a0, home_a1 = send_home(home_a0, False, 0), send_home(home_a1, False, 1)
    sent_qkv = gather_qkv.send([sums_a])
    grad_w1, grad_w2 = gather_w.send([sent_qkv])
    sent_qkv = gather_qkv.send([sums_a, grad_w1, grad_w2])
    sums_a = after(sums_a, sent_qkv)
    sent_qkv = gather_qkv.send([sums_a])
    grad_home = arrange(*lax.optimization_barrier((home_a0, home_a1, home_b, sent_qkv))[:3]).astype(FL)
    (grad_w_qkv,) = gather_qkv.send([])
    grad_w2 = grad_w2.T
    last_sent = grad_w_qkv
    grad_w_out = after(grad_w_out, sums_a)
    grad_w_out = jnp.sum(grad_w_out.astype(FL), axis=0)
    grad_b1 = grad_w_out[own // chips :].reshape(-1)
    grad_w_out = grad_w_out[: own // chips]
    grad_tokens = jnp.where(masked[:, :, None], 0.0, grad_home)

    sums1 = jnp.stack([sums_a[0] + sums_a[1], sums_b[0]])
    sums2 = jnp.stack([sums2_a[0] + sums2_a[1], sums2_b[0]])
    grad_modul = jnp.stack(
        [
            sums1[:, 0],
            sums1[:, 1] * gain_one,
            sums2[:, 3],
            sums2[:, 1],
            sums2[:, 2] * gain_two,
            sums2[:, 0],
        ],
        axis=1,
    ).reshape(2, 6 * width)
    grad_embed = sums1[0, 2] + sums1[1, 2]
    grad_gain1 = jnp.sum(sums1[:, 1] * (1.0 + modul[:, 1]), axis=0)
    grad_gain2 = jnp.sum(sums2[:, 2] * (1.0 + modul[:, 4]), axis=0)
    ada = grad_modul.shape[1] // devices
    part = width // devices
    small = jnp.concatenate(
        [
            grad_modul.reshape(2, devices, ada).transpose(1, 0, 2).reshape(devices, 2 * ada),
            jnp.stack([grad_embed, grad_gain1, grad_gain2, grad_b2])
            .reshape(4, devices, part)
            .transpose(1, 0, 2)
            .reshape(devices, 4 * part),
            jnp.broadcast_to(cond.astype(FL).reshape(1, -1), (devices, cond.size)),
        ],
        axis=1,
    )
    small = after(lax.all_to_all(small, ("batch", "seq", "mp"), 0, 0, tiled=True), last_sent)
    all_modul = small[:, : 2 * ada].reshape(2 * devices, ada)
    vectors = jnp.sum(small[:, 2 * ada : 2 * ada + 4 * part].reshape(devices, 4, part), axis=0)
    all_cond = small[:, 2 * ada + 4 * part :].reshape(2 * devices, -1)
    g_w_ada = lax.dot_general(
        all_cond, all_modul, (((0,), (0,)), ((), ())), precision=lax.Precision.HIGHEST
    )
    g_b_ada = jnp.sum(all_modul, axis=0)

    rows = grad_w_qkv.shape[0] // 2
    mine = lax.dynamic_slice_in_dim(grad_w_qkv, c * rows, rows, 0)
    other = lax.dynamic_slice_in_dim(grad_w_qkv, (1 - c) * rows, rows, 0)
    other = swap(other.astype(BF)).astype(FL)
    low, high = jnp.where(c == 0, mine, other), jnp.where(c == 0, other, mine)
    g_w_qkv = jnp.concatenate(
        [
            half[:, (3 * pair + part) * PAIR : (3 * pair + part + 1) * PAIR]
            for part in range(3)
            for half in (low, high)
            for pair in range(pairs)
        ],
        axis=1,
    )
    moves = [(2 * at + core, chips * core + at) for at in range(chips) for core in range(2)]
    g_w_out = lax.ppermute(grad_w_out.astype(BF), ("batch", "seq", "mp"), moves).astype(FL)
    return (
        output,
        grad_tokens,
        vectors[0],
        g_w_ada,
        g_b_ada,
        vectors[1],
        g_w_qkv,
        g_w_out,
        vectors[2],
        grad_w1,
        grad_b1,
        grad_w2,
        vectors[3],
    )


def solution(mesh):
    in_specs = (
        P(("batch", "mp"), "seq", None),
        P(("batch", "mp")),
        P(("batch", "mp"), "seq"),
        P(("batch", "mp")),
        P(),
        P(),
        P(),
        P(),
        P(),
        P(),
        P(),
        P(None, "mp"),
        P("mp"),
        P("mp", None),
        P(),
        P(("batch", "mp"), "seq", None),
    )
    out_specs = (
        P(("batch", "mp"), "seq", None),
        P(("batch", "mp"), "seq", None),
        P(("batch", "seq", "mp")),
        P(None, ("batch", "seq", "mp")),
        P(("batch", "seq", "mp")),
        P(("batch", "seq", "mp")),
        P(("batch", "seq", "mp"), None),
        P(("batch", "seq", "mp"), None),
        P(("batch", "seq", "mp")),
        P(("batch", "seq"), "mp"),
        P("mp"),
        P("mp", ("batch", "seq")),
        P(("batch", "seq", "mp")),
    )
    return jax.shard_map(
        per_device, mesh=mesh, in_specs=in_specs, out_specs=out_specs, check_vma=False
    )
```

```python
import functools
import math

import jax
import jax.numpy as jnp
from jax import lax
from jax.experimental import pallas as pl
from jax.experimental.pallas import tpu as pltpu
from jax.sharding import PartitionSpec as P

HEAD = 64
PAIR = 2 * HEAD
CHUNK = 256
LOG2E = math.log2(math.e)
LN2 = math.log(2.0)
BF = jnp.bfloat16
FL = jnp.float32
SWAP = [(0, 1), (1, 0)]


def mm(left, right):
    return lax.dot_general(left, right, (((1,), (0,)), ((), ())), preferred_element_type=FL)


def mm_nt(left, right):
    return lax.dot_general(left, right, (((1,), (1,)), ((), ())), preferred_element_type=FL)


def mm_tn(left, right):
    return lax.dot_general(left, right, (((0,), (0,)), ((), ())), preferred_element_type=FL)


def time_features(timestep, width):
    half = width // 2
    freqs = jnp.exp(-math.log(10000.0) * jnp.arange(half, dtype=FL) / half)
    angles = timestep.astype(FL)[:, None] * freqs[None, :]
    return jnp.concatenate([jnp.cos(angles), jnp.sin(angles)], axis=-1)


def unit(field):
    center = field - jnp.mean(field, axis=-1, keepdims=True)
    scale = lax.rsqrt(jnp.mean(center * center, axis=-1, keepdims=True) + 1e-05)
    return center * scale, scale


def unit_back(grad, normal, scale):
    return scale * (
        grad
        - jnp.mean(grad, axis=-1, keepdims=True)
        - normal * jnp.mean(grad * normal, axis=-1, keepdims=True)
    )


def row_sum(array):
    return jnp.sum(array, axis=0, keepdims=True)


def call(kernel, name, grid, ins, outs, micros, megabytes, aliases=None, wait=()):
    given = len(ins)
    ins = list(ins) + [(array, None, None) for array in wait]
    arrays = [entry[0] for entry in ins]

    def body(*refs):
        kernel(*refs[:given], *refs[len(ins) :])

    in_specs = [
        pl.BlockSpec(memory_space=pl.ANY) if entry[1] is None else pl.BlockSpec(entry[1], entry[2])
        for entry in ins
    ]
    return pl.pallas_call(
        body,
        grid=grid,
        in_specs=in_specs,
        out_specs=[pl.BlockSpec(o[2], o[3]) for o in outs],
        out_shape=[jax.ShapeDtypeStruct(o[0], o[1]) for o in outs],
        input_output_aliases=aliases or {},
        compiler_params=pltpu.CompilerParams(vmem_limit_bytes=megabytes * 1024 * 1024),
        cost_estimate=pl.CostEstimate(flops=int(micros * 2e9), bytes_accessed=0, transcendentals=0),
        name=name,
    )(*arrays)


def still(*indices):
    return lambda *grid: indices


def pick(values):
    step = pl.program_id(0)
    chosen = values[-1][...]
    for at in reversed(range(len(values) - 1)):
        chosen = jnp.where(step == at, values[at][...], chosen)
    return chosen


def norm1_kernel(x0_ref, x1_ref, mod_ref, gain_ref, out_ref):
    for at, ref in enumerate((x0_ref, x1_ref)):
        normal, _ = unit(ref[...].astype(FL))
        normed = normal * gain_ref[...] * (1.0 + mod_ref[0, 1:2]) + mod_ref[0, 0:1]
        out_ref[at * CHUNK : (at + 1) * CHUNK] = normed.astype(BF)


def norm1_call(x0, x1, modul, gain, seq, wait):
    width = gain.shape[1]
    block = (CHUNK, width)
    return call(
        norm1_kernel,
        "norm1",
        (1,),
        [
            (x0, block, still(0, 0)),
            (x1, block, still(0, 0)),
            (modul, (1, 6, width), still(seq, 0, 0)),
            (gain, (1, width), still(0, 0)),
        ],
        [((2 * CHUNK, width), BF, (2 * CHUNK, width), still(0, 0))],
        1.5,
        8,
        wait=wait,
    )[0]


def turn(tile, cosine, sine):
    lane = lax.broadcasted_iota(jnp.int32, tile.shape, 1)
    ahead = pltpu.roll(tile, PAIR - HEAD // 2, 1)
    behind = pltpu.roll(tile, HEAD // 2, 1)
    other = jnp.where(lane % HEAD < HEAD // 2, ahead, behind)
    return tile * cosine + other * sine


def qkv_kernel(x_ref, w_ref, cos_ref, sin_ref, *refs):
    copy_ref, q_ref, k_ref, v_ref = refs[-4:]
    x = x_ref[...]
    copy_ref[...] = x
    out = mm(x, w_ref[...])
    cosine, sine = cos_ref[...], sin_ref[...]
    own = q_ref.shape[1]
    for at in range(0, own, PAIR):
        here = slice(at, at + PAIR)
        q_ref[:, here] = (turn(out[:, here], cosine, sine) * (LOG2E * HEAD ** (-0.5))).astype(BF)
        k_ref[:, here] = turn(out[:, own + at : own + at + PAIR], cosine, sine).astype(BF)
    v_ref[...] = out[:, 2 * own :].astype(BF)


def qkv_call(x, weight, cosine, sine, part, earlier):
    rows, width = x.shape
    own = weight.shape[1] // 3
    steps = rows // CHUNK
    place = lambda g: (g + part * steps, 0)
    extra = [] if earlier is None else list(earlier)
    return call(
        qkv_kernel,
        "qkv",
        (steps,),
        [
            (x, (CHUNK, width), lambda g: (g, 0)),
            (weight, weight.shape, still(0, 0)),
            (cosine, (CHUNK, PAIR), place),
            (sine, (CHUNK, PAIR), place),
        ]
        + [(array, None, None) for array in extra],
        [((2 * rows, width), BF, (CHUNK, width), place)]
        + [((2 * rows, own), BF, (CHUNK, own), place)] * 3,
        1.6,
        14,
        {4 + i: i for i in range(len(extra))},
    )


def head_lanes(shape, head):
    lane = lax.broadcasted_iota(jnp.int32, shape, 1)
    return (lane >= head * HEAD) & (lane < (head + 1) * HEAD)


def taken(ref, stride):
    chunks = [ref[at : at + CHUNK] for at in range(0, ref.shape[0], stride * CHUNK)]
    return jnp.concatenate(chunks, axis=0)


def attend_kernel(stride, q_ref, k_ref, v_ref, own_ref, other_ref, lse_ref):
    queries = taken(q_ref, stride)
    keys = k_ref[...]
    turned = v_ref[...].astype(FL).T.astype(BF)
    ones = jnp.ones((16, turned.shape[1]), BF)
    results = []
    for head in range(2):
        mine = jnp.where(head_lanes(queries.shape, head), queries, jnp.zeros_like(queries))
        scores = mm_nt(keys, mine)
        top = jnp.max(scores, axis=0, keepdims=True)
        raised = jnp.exp2(scores - top).astype(BF)
        values = jnp.concatenate([turned[head * HEAD : (head + 1) * HEAD], ones], axis=0)
        both = mm(values, raised)
        total = both[HEAD : HEAD + 1]
        results.append(both[:HEAD] / total)
        lse_ref[0, head : head + 1, :] = top + jnp.log2(total)
    out = jnp.concatenate(results, axis=0).T.astype(BF)
    rows = own_ref.shape[0]
    own_ref[...] = out[:rows]
    other_ref[...] = out[rows:]


def attend_call(q, k, v, stride, wait):
    length, width = k.shape
    rows = length // stride
    pairs = width // PAIR
    whole = ((length, PAIR), lambda p: (0, p))
    return call(
        functools.partial(attend_kernel, stride),
        "attend",
        (pairs,),
        [(q, *whole), (k, *whole), (v, *whole)],
        [((rows // 2, width), BF, (rows // 2, PAIR), lambda p: (0, p))] * 2
        + [((pairs, 8, rows), FL, (1, 8, rows), lambda p: (p, 0, 0))],
        3.5 + 6.2 * rows / length,
        16,
        wait=wait,
    )


def out_kernel(own_ref, got_ref, *refs):
    fields, (mod_ref, gain_ref, w_ref, att_ref, res_ref, normed_ref) = refs[:-6], refs[-6:]
    attended = jnp.concatenate([own_ref[...], got_ref[...]], axis=1)
    att_ref[...] = attended
    result = mm(attended, w_ref[...])
    res_ref[...] = result
    field = pick(fields).astype(FL) + mod_ref[0, 2:3] * result
    normal, _ = unit(field)
    normed = normal * gain_ref[...] * (1.0 + mod_ref[0, 4:5]) + mod_ref[0, 3:4]
    normed_ref[...] = normed.astype(BF)


def out_call(own, got, fields, modul, gain, weight, seq):
    rows, width = own.shape[0], gain.shape[1]
    part = (CHUNK, width // 2)
    block = (CHUNK, width)
    row = lambda g: (g, 0)
    return call(
        out_kernel,
        "out_norm2",
        (rows // CHUNK,),
        [(own, part, row), (got, part, row)]
        + [(field, block, still(0, 0)) for field in fields]
        + [
            (modul, (1, 6, width), still(seq, 0, 0)),
            (gain, (1, width), still(0, 0)),
            (weight, weight.shape, still(0, 0)),
        ],
        [((rows, width), BF, block, row), ((rows, width), FL, block, row), ((rows, width), BF, block, row)],
        1.7 * rows / CHUNK,
        14,
    )


def mlp_kernel(
    x_ref, xo_ref, c_ref, co_ref, mod_ref, w1_ref, b1_ref, w2_ref,
    copy_ref, grad_ref, hidden_ref, before_ref, out_ref, back_ref, away_ref, bsum_ref, gsum_ref,
):
    step = pl.program_id(0)
    first = step == 0
    owns = step < pl.num_programs(0) // 2
    x = jnp.where(owns, x_ref[...], xo_ref[...])
    copy_ref[...] = x
    grad = jnp.where(owns, c_ref[...], co_ref[...])
    grad = (mod_ref[0, 5:6] * grad.astype(FL)).astype(BF)
    grad_ref[...] = grad
    units = w1_ref.shape[1]
    size = units // 3
    root = math.sqrt(2.0 / math.pi)
    total, back = None, None
    for at in range(0, units, size):
        here = slice(at, at + size)
        before = mm(x, w1_ref[:, here]) + b1_ref[:, here]
        square = before * before
        inner = jnp.tanh(before * (root + (root * 0.044715) * square))
        half = 0.5 * (1.0 + inner)
        hidden = (before * half).astype(BF)
        slope = half + (0.5 * before) * (1.0 - inner * inner) * (root + (3.0 * root * 0.044715) * square)
        grad_before = (mm_nt(grad, w2_ref[here]) * slope).astype(BF)
        hidden_ref[:, here] = hidden
        before_ref[:, here] = grad_before
        add = row_sum(grad_before.astype(FL))
        bsum_ref[:, here] = jnp.where(first, add, bsum_ref[:, here] + add)
        term = mm(hidden, w2_ref[here])
        total = term if total is None else total + term
        term = mm_nt(grad_before, w1_ref[:, here])
        back = term if back is None else back + term

    @pl.when(owns)
    def _():
        out_ref[...] = total
        back_ref[...] = back
        add = row_sum(grad.astype(FL))
        gsum_ref[...] = jnp.where(first, add, gsum_ref[...] + add)

    @pl.when(jnp.logical_not(owns))
    def _():
        away_ref[0] = total.astype(BF)
        away_ref[1] = back.astype(BF)


def mlp_call(x, x_other, grads, grads_other, modul, w1, b1, w2, seq, wait):
    rows, width = x.shape
    units = w1.shape[1]
    steps = rows // CHUNK
    block = (CHUNK, width)
    row = lambda g: (g, 0)
    early = lambda g: (jnp.minimum(g, steps - 1), 0)
    late = lambda g: (jnp.maximum(g - steps, 0), 0)
    return call(
        mlp_kernel,
        "mlp",
        (2 * steps,),
        [
            (x, block, early),
            (x_other, block, late),
            (grads, block, early),
            (grads_other, block, late),
            (modul, (1, 6, width), still(seq, 0, 0)),
            (w1, w1.shape, still(0, 0)),
            (b1, b1.shape, still(0, 0)),
            (w2, w2.shape, still(0, 0)),
        ],
        [((2 * rows, width), BF, block, row)] * 2
        + [((2 * rows, units), BF, (CHUNK, units), row)] * 2
        + [((rows, width), FL, block, early)] * 2
        + [((2, rows, width), BF, (2, CHUNK, width), lambda g: (0, jnp.maximum(g - steps, 0), 0))]
        + [((1, units), FL, (1, units), still(0, 0)), ((1, width), FL, (1, width), still(0, 0))],
        8.0 * rows / CHUNK,
        20,
        wait=wait,
    )


def norm2_back_kernel(own_ref, got_ref, bown_ref, bgot_ref, res_ref, c_ref, *refs):
    blocks = (len(refs) - 9) // 2
    fields, refs = refs[:blocks], refs[blocks:]
    mod_ref, gain_ref, b2_ref, w_ref = refs[:4]
    outs, (field_ref, attn_ref, mine_ref, other_ref, sum_ref) = refs[4:-5], refs[-5:]
    step = pl.program_id(0)
    mod = lambda at: mod_ref[0, at : at + 1]
    grad_out = c_ref[...].astype(FL)
    result = res_ref[...]
    field = pick(fields).astype(FL) + mod(2) * result
    out = own_ref[...] + got_ref[0].astype(FL) + b2_ref[...]
    mixed = (field + mod(5) * out).astype(BF)
    for at, ref in enumerate(outs):

        @pl.when(step == at)
        def _():
            ref[...] = mixed

    grad = bown_ref[...] + bgot_ref[0].astype(FL)
    normal, scale = unit(field)
    grad_field = grad_out + unit_back(grad * (1.0 + mod(4)) * gain_ref[...], normal, scale)
    field_ref[...] = grad_field
    grad_attn = (mod(2) * grad_field).astype(BF)
    attn_ref[...] = grad_attn
    back = mm_nt(grad_attn, w_ref[...]).astype(BF)
    own = mine_ref.shape[1]
    mine_ref[...] = back[:, :own]
    other_ref[...] = back[:, own:]
    sums = [grad_out * out, grad, grad * normal, grad_field * result]
    sums = [row_sum(array) for array in sums] + [jnp.zeros((4, grad.shape[1]), FL)]
    sum_ref[0] = jnp.concatenate(sums, axis=0)


def norm2_back_call(own, back_own, got, result, fields, grads, modul, gain, bias, weight, seq, wait):
    rows, width = result.shape
    steps = rows // CHUNK
    block, half = (CHUNK, width), (CHUNK, width // 2)
    row = lambda g: (g, 0)
    return call(
        norm2_back_kernel,
        "norm2_back",
        (steps,),
        [
            (own, block, row),
            (got, (1, CHUNK, width), lambda g: (0, g, 0)),
            (back_own, block, row),
            (got, (1, CHUNK, width), lambda g: (1, g, 0)),
            (result, block, row),
            (grads, block, row),
        ]
        + [(array, block, still(0, 0)) for array in fields]
        + [
            (modul, (1, 6, width), still(seq, 0, 0)),
            (gain, (1, width), still(0, 0)),
            (bias, (1, width), still(0, 0)),
            (weight, weight.shape, still(0, 0)),
        ],
        [(block, BF, block, still(0, 0))] * steps
        + [((rows, width), FL, block, row), ((rows, width), BF, block, row)]
        + [((rows, width // 2), BF, half, row)] * 2
        + [((steps, 8, width), FL, (1, 8, width), lambda g: (g, 0, 0))],
        3.0 * rows / CHUNK,
        14,
        wait=wait,
    )


def attend_back_kernel(
    stride, q_ref, k_ref, v_ref, own_ref, other_ref, gown_ref, gother_ref, lse_ref, cos_ref, sin_ref, *refs
):
    out_ref = refs[-1]
    queries, keys, values = taken(q_ref, stride), k_ref[...], v_ref[...]
    att = jnp.concatenate([own_ref[...], other_ref[...]], axis=0)
    grads = jnp.concatenate([gown_ref[...], gother_ref[...]], axis=0)
    turned = keys.astype(FL).T.astype(BF)
    product = (att.astype(FL) * grads.astype(FL)).T
    parts, dk, dv = [], None, None
    for head in range(2):
        lanes = head_lanes(queries.shape, head)
        mine = jnp.where(lanes, queries, jnp.zeros_like(queries))
        grad = jnp.where(lanes, grads, jnp.zeros_like(grads))
        delta = jnp.sum(product[head * HEAD : (head + 1) * HEAD], axis=0, keepdims=True)
        probs = jnp.exp2(mm_nt(keys, mine) - lse_ref[0, head : head + 1, :])
        term = mm(probs.astype(BF), grad)
        dv = term if dv is None else dv + term
        scores = (probs * (mm_nt(values, grad) - delta)).astype(BF)
        term = mm(scores, mine)
        dk = term if dk is None else dk + term
        parts.append(mm(turned[head * HEAD : (head + 1) * HEAD], scores))
    dq = jnp.concatenate(parts, axis=0).T * (HEAD ** (-0.5))
    cosine, sine = cos_ref[...], -sin_ref[...]
    turned = turn(dq, taken(cos_ref, stride), -taken(sin_ref, stride)).astype(BF)
    for at in range(dq.shape[0] // CHUNK):
        start = at * stride * CHUNK
        out_ref[start : start + CHUNK, :PAIR] = turned[at * CHUNK : (at + 1) * CHUNK]
        if stride > 1:
            empty = jnp.zeros(((stride - 1) * CHUNK, PAIR), BF)
            out_ref[start + CHUNK : start + stride * CHUNK, :PAIR] = empty
    out_ref[:, PAIR : 2 * PAIR] = turn(dk * LN2, cosine, sine).astype(BF)
    out_ref[:, 2 * PAIR :] = dv.astype(BF)


def attend_back_call(q, k, v, att, grads, lse, cosine, sine, stride, first, pairs, earlier, wait):
    length, width = k.shape
    rows = length // stride
    column = lambda p: (0, first + p)
    whole = ((length, PAIR), column)
    fixed = ((length, PAIR), still(0, 0))
    ins = [(q, *whole), (k, *whole), (v, *whole)]
    ins += [(array, (rows // 2, PAIR), column) for array in (*att, *grads)]
    ins += [(lse, (1, 8, rows), lambda p: (first + p, 0, 0)), (cosine, *fixed), (sine, *fixed)]
    aliases = {}
    if earlier is not None:
        aliases = {len(ins): 0}
        ins.append((earlier, None, None))
    return call(
        functools.partial(attend_back_kernel, stride),
        "attend_back",
        (pairs,),
        ins,
        [((length, 3 * width), BF, (length, 3 * PAIR), column)],
        (1.0 + 5.0 * rows / length) * pairs,
        26,
        aliases,
        wait,
    )[0]


def project_back(grad_ref, w_ref):
    own, result = w_ref.shape[1] // 3, None
    for at in range(0, own, PAIR):
        weight = jnp.concatenate([w_ref[:, start + at : start + at + PAIR] for start in (0, own, 2 * own)], axis=1)
        term = mm_nt(grad_ref[:, 3 * at : 3 * (at + PAIR)], weight)
        result = term if result is None else result + term
    return result


def project_kernel(grad_ref, w_ref, out_ref):
    out_ref[...] = project_back(grad_ref, w_ref).astype(BF)


def project_call(grad, weight):
    length = grad.shape[0]
    rows, width = length // 2, weight.shape[0]
    return call(
        project_kernel,
        "project_other",
        (2,),
        [(grad, (CHUNK, grad.shape[1]), lambda g: (g + 2, 0)), (weight, weight.shape, still(0, 0))],
        [((rows, width), BF, (CHUNK, width), lambda g: (g, 0))],
        1.8,
        14,
    )[0]


def project_own_kernel(grad_ref, w_ref, got_ref, own_ref, beside_ref):
    out = project_back(grad_ref, w_ref) + got_ref[...].astype(FL)
    own_ref[...] = out[:CHUNK]
    beside_ref[...] = out[CHUNK:].astype(BF)


def project_own_call(grad, weight, got):
    width = weight.shape[0]
    block = (CHUNK, width)
    return call(
        project_own_kernel,
        "project_own",
        (1,),
        [
            (grad, (2 * CHUNK, grad.shape[1]), still(0, 0)),
            (weight, weight.shape, still(0, 0)),
            (got, (2 * CHUNK, width), still(0, 0)),
        ],
        [(block, FL, block, still(0, 0)), (block, BF, block, still(0, 0))],
        1.8,
        16,
    )


def norm1_back(grad, field, grad_field1, mask, mod_ref, gain_ref):
    normal, scale = unit(field.astype(FL))
    grad_field = grad_field1 + unit_back(
        grad * (1.0 + mod_ref[0, 1:2]) * gain_ref[...], normal, scale
    )
    rounded = grad_field.astype(BF)
    embed = mm(mask[:, :CHUNK], rounded)
    sums = jnp.concatenate(
        [row_sum(grad), row_sum(grad * normal), embed[:1], jnp.zeros((5, grad.shape[1]), FL)], axis=0
    )
    return rounded, sums


def norm1_back_a_kernel(
    grad_ref, w_ref, got_ref, f0, f1, k0, k1, g_ref, mod_ref, gain_ref, o0, o1, sum_ref
):
    step = pl.program_id(0)
    grad = project_back(grad_ref, w_ref) + got_ref[...].astype(FL)
    rounded, sums = norm1_back(grad, pick((f0, f1)), g_ref[...], pick((k0, k1)), mod_ref, gain_ref)
    for at, ref in enumerate((o0, o1)):

        @pl.when(step == at)
        def _():
            ref[...] = rounded

    sum_ref[0] = sums


def norm1_back_a_call(grad_proj, weight, got, fields, grad_field1, modul, gain, wait):
    width = weight.shape[0]
    block, marks = (CHUNK, width), (16, width)
    row = lambda g: (g, 0)
    return call(
        norm1_back_a_kernel,
        "norm1_back_a",
        (2,),
        [
            (grad_proj, (CHUNK, grad_proj.shape[1]), row),
            (weight, weight.shape, still(0, 0)),
            (got, block, row),
        ]
        + [(field, block, still(0, 0)) for field in fields]
        + [(field, marks, still(CHUNK // 16, 0)) for field in fields]
        + [
            (grad_field1, block, row),
            (modul, (1, 6, width), still(0, 0, 0)),
            (gain, (1, width), still(0, 0)),
        ],
        [(block, BF, block, still(0, 0))] * 2
        + [((2, 8, width), FL, (1, 8, width), lambda g: (g, 0, 0))],
        4.0,
        20,
        wait=wait,
    )


def norm1_back_b_kernel(own_ref, got_ref, field_ref, mask_ref, g_ref, mod_ref, gain_ref, out_ref, sum_ref):
    grad = own_ref[...] + got_ref[...].astype(FL)
    rounded, sums = norm1_back(grad, field_ref[...], g_ref[...], mask_ref[...], mod_ref, gain_ref)
    out_ref[...] = rounded
    sum_ref[0] = sums


def norm1_back_b_call(own, got, field, grad_field1, modul, gain):
    width = own.shape[1]
    block = (CHUNK, width)
    return call(
        norm1_back_b_kernel,
        "norm1_back_b",
        (1,),
        [
            (own, block, still(0, 0)),
            (got, block, still(0, 0)),
            (field, block, still(0, 0)),
            (field, (16, width), still(CHUNK // 16, 0)),
            (grad_field1, block, still(0, 0)),
            (modul, (1, 6, width), still(1, 0, 0)),
            (gain, (1, width), still(0, 0)),
        ],
        [(block, BF, block, still(0, 0)), ((1, 8, width), FL, (1, 8, width), still(0, 0, 0))],
        1.2,
        10,
    )


def bits_of(axis):
    return (lax.axis_size(axis) - 1).bit_length()


def partner(axis, bit):
    return [(at, at ^ (1 << bit)) for at in range(lax.axis_size(axis))]


def one_of(array, at, axis):
    return lax.dynamic_index_in_dim(array, at, axis, keepdims=False)


def after(value, *others):
    if not others:
        return value
    return lax.optimization_barrier((value, *others))[0]


def first_send(part):
    place, core = lax.axis_index("batch") & 3, lax.axis_index("mp")
    x, y = place & 1, place >> 1
    along = core == 0
    low, high = jnp.where(along, 1 - x, 2 - 2 * y), jnp.where(along, 3 - x, 3 - 2 * y)
    sent = jnp.stack([one_of(part, low, 0), one_of(part, high, 0)]).astype(BF)
    again = jnp.where(along, x + 2 - 2 * y, 2 * y + 1 - x)
    return sent, again, 2 * y + x, jnp.where(along, y, x)


def crossing(first):
    pairs = []
    for at in range(lax.axis_size("batch")):
        for side in range(2):
            pairs.append((2 * at + side, 2 * (at ^ (1 << (side if first else 1 - side))) + side))
    return pairs


def total(terms):
    result = terms[0].astype(FL)
    for term in terms[1:]:
        result = result + term.astype(FL)
    return result


def scatter_steps(parts):
    batch, seq = lax.axis_size("batch"), lax.axis_size("seq")
    place, z = lax.axis_index("batch"), lax.axis_index("seq")
    parts = [part.reshape((batch, seq, -1) + part.shape[1:]) for part in parts]
    for bit in reversed(range(2, bits_of("batch"))):
        mine = (place >> bit) & 1
        halves = [part.reshape((2, -1) + part.shape[1:]) for part in parts]
        got = [lax.ppermute(one_of(half, 1 - mine, 0).astype(BF), "batch", partner("batch", bit)) for half in halves]
        parts = [one_of(half, mine, 0) + part.astype(FL) for half, part in zip(halves, got)]
    sent, again, stays, which = zip(*[first_send(part) for part in parts])
    again, stays, which = again[0], stays[0], which[0]
    sent = jnp.stack(sent, axis=1)
    gates = yield sent
    got = after(lax.ppermute(sent, ("batch", "mp"), crossing(True)), *gates)
    left, right = one_of(got, 1 - which, 0), one_of(got, which, 0)
    sent = jnp.stack([total([one_of(part, again, 0), left[at]]).astype(BF) for at, part in enumerate(parts)])
    gates = yield sent
    last = after(lax.ppermute(sent, ("batch", "mp"), crossing(False)), *gates)
    terms = [[one_of(part, stays, 0), right[at], last[at]] for at, part in enumerate(parts)]
    low, high = z % 2, z // 2
    chosen = [[jnp.stack([one_of(t, 1 - low, 0), one_of(t, 3 - low, 0)]) for t in part] for part in terms]
    sent = jnp.stack([total(part).astype(BF) for part in chosen])
    gates = yield sent
    near = after(lax.ppermute(sent, "seq", partner("seq", 0)), *gates)
    chosen = [
        [one_of(t, 2 * (1 - high) + low, 0) for t in part] + [one_of(near[at], 1 - high, 0)]
        for at, part in enumerate(terms)
    ]
    sent = jnp.stack([total(part).astype(BF) for part in chosen])
    gates = yield sent
    far = after(lax.ppermute(sent, "seq", partner("seq", 1)), *gates)
    yield [
        total([one_of(t, z, 0) for t in part] + [one_of(near[at], high, 0), far[at]])
        for at, part in enumerate(terms)
    ]


def routes(second, turned):
    pairs = []
    for q in range(4):
        for c in range(2):
            group = 1 - c if second else c
            chip = 2 * group + (q // 2 + turned) % 2
            pairs.append((q * 2 + c, chip * 2 + q % 2))
    return pairs


def send(block, second, turned):
    return lax.ppermute(block, ("seq", "mp"), routes(second, turned))


def send_home(block, second, turned):
    return lax.ppermute(block, ("seq", "mp"), [(to, at) for at, to in routes(second, turned)])


def swap(array):
    return lax.ppermute(array, "mp", SWAP)


def per_device(
    tokens_in,
    prefix,
    mask_bits,
    timestep,
    mask_embed,
    w_ada,
    b_ada,
    gain1,
    query_key_value_weight,
    attention_out_weight,
    gain2,
    first_up_weight,
    first_hidden_bias,
    second_down_weight,
    second_output_bias,
    cotangent,
):
    seqs, span, width = tokens_in.shape
    own = width // 2
    z, c = lax.axis_index("seq"), lax.axis_index("mp")
    upper, side = z // 2, z % 2
    devices = lax.axis_size("batch") * lax.axis_size("seq") * lax.axis_size("mp")

    places = jnp.arange(span, dtype=jnp.int32) + z * span
    masked = (places[None, :] >= prefix[:, None]) & (mask_bits == 1)

    def marked(tokens, at):
        marks = one_of(masked, at, 0)
        block = jnp.where(marks[:, None], mask_embed, one_of(tokens, at, 0))
        return jnp.concatenate([block, jnp.pad(marks.astype(BF)[None, :], ((0, 15), (0, width - span)))], axis=0)

    block_a0, block_a1 = marked(tokens_in, upper), marked(tokens_in, 1 - upper)
    def arrange(first, second, third):
        low, high = jnp.where(upper == 0, first, second), jnp.where(upper == 0, second, first)
        return jnp.stack([low, high, third])

    def back_home(blocks, *others):
        first = send_home(blocks[0], False, 0)
        second = send_home(blocks[1], False, 1)
        third = send_home(blocks[2], True, 0)
        return arrange(*lax.optimization_barrier((first, second, third, *others))[:3])

    other_time = swap(timestep)
    time_a = one_of(jnp.where(c == upper, timestep, other_time), side, 0)
    time_b = jnp.where(c == upper, other_time, timestep)[2]
    cond = jax.nn.silu(time_features(jnp.stack([time_a, time_b]), w_ada.shape[0])).astype(BF)
    modul = jnp.dot(cond, w_ada, preferred_element_type=FL) + b_ada.astype(FL)
    modul = modul.reshape(2, 6, width)
    gain_one, gain_two = gain1.astype(FL)[None, :], gain2.astype(FL)[None, :]

    pairs = own // PAIR
    pairs = own // PAIR

    w_heads = jnp.concatenate(
        [
            lax.dynamic_slice_in_dim(query_key_value_weight, at * width + c * own, own, 1)
            for at in range(3)
        ],
        axis=1,
    )
    w_out = jnp.concatenate([attention_out_weight[own:], attention_out_weight[:own]], axis=0)
    w_out = jnp.where(c == 0, attention_out_weight, w_out)
    quarter = jnp.stack([2 * side + c, 2 * (1 - side) + c, 2 * side + 1 - c, 2 * (1 - side) + 1 - c])
    positions = (quarter[:, None] * span + jnp.arange(span)[None, :]).reshape(-1, 1).astype(FL)
    lane = jnp.arange(PAIR)
    half = HEAD // 2
    inverse = jnp.exp(-math.log(10000.0) * (lane % half).astype(FL) / half)
    angles = positions * inverse[None, :]
    cosine = jnp.cos(angles)
    sine = jnp.sin(angles) * jnp.where(lane % HEAD < half, -1.0, 1.0)[None, :]

    block_b = marked(after(tokens_in, block_a0, block_a1), 2)
    block_a0, block_a1 = send(block_a0, False, 0), send(block_a1, False, 1)
    block_b0, block_b1 = send(block_b, True, 0), send(block_b, True, 1)

    block_a0, block_a1, modul, w_heads, w_out, cosine, sine = lax.optimization_barrier(
        (block_a0, block_a1, modul, w_heads, w_out, cosine, sine)
    )
    normed_a = norm1_call(block_a0, block_a1, modul, gain_one, 0, [block_b])
    other_a = swap(normed_a)
    first = qkv_call(normed_a, w_heads, cosine, sine, 0, None)
    normed_a, q_a, k_a, v_a = qkv_call(other_a, w_heads, cosine, sine, 1, first)
    own_a, away_a, lse_a = attend_call(q_a, k_a, v_a, 1, [])
    got_a = swap(away_a)
    late = after(cotangent, own_a)
    late = one_of(late, upper, 0), one_of(late, 1 - upper, 0), late[2]
    normed_own_b = norm1_call(block_b0, block_b1, modul, gain_one, 1, [own_a])
    other_b = swap(normed_own_b)
    first = qkv_call(normed_own_b, w_heads, cosine, sine, 0, None)
    normed_b, q_b, k_b, v_b = qkv_call(other_b, w_heads, cosine, sine, 1, first)
    own_b, away_b, lse_b = attend_call(q_b, k_b, v_b, 2, [])
    got_b = swap(away_b)

    grads_b = send(late[2], True, 0)
    grads_a = jnp.concatenate([send(late[0], False, 0), send(late[1], False, 1)], axis=0)
    grads_other_a, grads_other_b = swap(grads_a), swap(grads_b)

    fields_a, fields_b = (block_a0, block_a1), (block_b0,)
    bias1 = first_hidden_bias.astype(FL)[None, :]
    bias2 = second_output_bias.astype(FL)[None, :]
    weights = (first_up_weight, bias1, second_down_weight)
    attended_a, result_a, normed2_a = out_call(own_a, got_a, fields_a, modul, gain_two, w_out, 0)
    other_a = swap(normed2_a)
    attended_b, result_b, normed2_b = out_call(own_b, got_b, fields_b, modul, gain_two, w_out, 1)
    other_b = swap(normed2_b)
    normed2_b, mlp_b, hidden_b, before_b, out_b, back_b, sent_b, sum_b1b, sum_b2b = mlp_call(
        normed2_b, other_b, grads_b, grads_other_b, modul, *weights, 1, []
    )
    got_b = swap(sent_b)
    normed2_a, mlp_a, hidden_a, before_a, out_a, back_a, sent_a, sum_b1a, sum_b2a = mlp_call(
        normed2_a, other_a, grads_a, grads_other_a, modul, *weights, 0, [sent_b]
    )
    got_a = swap(sent_a)
    m2, field1_b, attn_b, back_own_b, back_away_b, sums2_b = norm2_back_call(
        out_b, back_b, got_b, result_b, fields_b, grads_b, modul, gain_two, bias2, w_out, 1, [sent_a]
    )
    back_other_b = swap(back_away_b)
    before_a, hidden_a = lax.optimization_barrier((before_a, hidden_a, back_away_b))[:2]
    grad_w1 = (mm_tn(normed2_b, before_b) + mm_tn(normed2_a, before_a)).astype(BF)
    grad_w2 = (mm_tn(mlp_b, hidden_b) + mm_tn(mlp_a, hidden_a)).astype(BF)
    grad_b2 = (sum_b2a + sum_b2b)[0]
    gather_w = scatter_steps([grad_w1, grad_w2])
    sent_w = next(gather_w)

    m0, m1, field1_a, attn_a, back_own_a, back_away_a, sums2_a = norm2_back_call(
        out_a, back_a, got_a, result_a, fields_a, grads_a, modul, gain_two, bias2, w_out, 0, [sent_w]
    )
    back_other_a = swap(back_away_a)
    grad_w_out = mm_tn(attended_a, attn_a) + mm_tn(attended_b, attn_b)
    out_away = grad_w_out[own:].astype(BF)
    grad_w_out = grad_w_out[:own] + swap(out_away).astype(FL)

    chips = devices // 2
    grad_b1 = (sum_b1a + sum_b1b).reshape(-1, width).astype(BF)
    grad_w_out = jnp.concatenate(
        [
            grad_w_out.astype(BF).reshape(chips, -1, width),
            jnp.broadcast_to(grad_b1[None], (chips,) + grad_b1.shape),
        ],
        axis=1,
    )
    out_sent = grad_w_out
    grad_w_out = lax.all_to_all(grad_w_out, ("batch", "seq"), 0, 0, tiled=True)

    proj_b = attend_back_call(
        q_b, k_b, v_b, (own_b, away_b), (back_own_b, back_other_b), lse_b, cosine, sine, 2, 0, pairs, None,
        [back_other_a, out_sent],
    )
    away_b = project_call(proj_b, w_heads)
    got = swap(away_b)
    qkv_b = mm_tn(normed_b, after(proj_b, away_b))
    sent_w = gather_w.send([away_b])
    normed1_b, beside = project_own_call(proj_b, w_heads, got)
    got = lax.ppermute(beside, "seq", partner("seq", 0))

    def attention_back_a(first, count, earlier, wait):
        return attend_back_call(
            q_a, k_a, v_a, (own_a, away_a), (back_own_a, back_other_a), lse_a, cosine, sine, 1, first, count,
            earlier, wait,
        )

    proj_a = attention_back_a(0, pairs - 1, None, [beside, sent_w, qkv_b])
    sent_w = gather_w.send([proj_a])
    home_b, sums_b = norm1_back_b_call(normed1_b, after(got, sent_w), block_b0, field1_b, modul, gain_one)
    output = back_home((m0, m1, m2), sums_b)
    home_b = send_home(home_b, True, 0)
    proj_a = attention_back_a(pairs - 1, 1, proj_a, [sums_b, sent_w, output])
    away = project_call(proj_a, w_heads)
    got = swap(away)
    gather_qkv = scatter_steps([(qkv_b + mm_tn(normed_a, after(proj_a, away))).astype(BF)])
    sent_qkv = next(gather_qkv)
    sent_w = gather_w.send([sent_qkv])
    home_a0, home_a1, sums_a = norm1_back_a_call(
        proj_a, w_heads, got, fields_a, field1_a, modul, gain_one, [sent_qkv, sent_w, home_b]
    )
    home_a0, home_a1 = send_home(home_a0, False, 0), send_home(home_a1, False, 1)
    sent_qkv = gather_qkv.send([sums_a])
    grad_w1, grad_w2 = gather_w.send([sent_qkv])
    sent_qkv = gather_qkv.send([sums_a, grad_w1, grad_w2])
    sums_a = after(sums_a, sent_qkv)
    sent_qkv = gather_qkv.send([sums_a])
    grad_home = arrange(*lax.optimization_barrier((home_a0, home_a1, home_b, sent_qkv))[:3]).astype(FL)
    (grad_w_qkv,) = gather_qkv.send([])
    grad_w2 = grad_w2.T
    last_sent = grad_w_qkv
    grad_w_out = after(grad_w_out, sums_a)
    grad_w_out = jnp.sum(grad_w_out.astype(FL), axis=0)
    grad_b1 = grad_w_out[own // chips :].reshape(-1)
    grad_w_out = grad_w_out[: own // chips]
    grad_tokens = jnp.where(masked[:, :, None], 0.0, grad_home)

    sums1 = jnp.stack([sums_a[0] + sums_a[1], sums_b[0]])
    sums2 = jnp.stack([sums2_a[0] + sums2_a[1], sums2_b[0]])
    grad_modul = jnp.stack(
        [
            sums1[:, 0],
            sums1[:, 1] * gain_one,
            sums2[:, 3],
            sums2[:, 1],
            sums2[:, 2] * gain_two,
            sums2[:, 0],
        ],
        axis=1,
    ).reshape(2, 6 * width)
    grad_embed = sums1[0, 2] + sums1[1, 2]
    grad_gain1 = jnp.sum(sums1[:, 1] * (1.0 + modul[:, 1]), axis=0)
    grad_gain2 = jnp.sum(sums2[:, 2] * (1.0 + modul[:, 4]), axis=0)
    ada = grad_modul.shape[1] // devices
    part = width // devices
    small = jnp.concatenate(
        [
            grad_modul.reshape(2, devices, ada).transpose(1, 0, 2).reshape(devices, 2 * ada),
            jnp.stack([grad_embed, grad_gain1, grad_gain2, grad_b2])
            .reshape(4, devices, part)
            .transpose(1, 0, 2)
            .reshape(devices, 4 * part),
            jnp.broadcast_to(cond.astype(FL).reshape(1, -1), (devices, cond.size)),
        ],
        axis=1,
    )
    small = after(lax.all_to_all(small, ("batch", "seq", "mp"), 0, 0, tiled=True), last_sent)
    all_modul = small[:, : 2 * ada].reshape(2 * devices, ada)
    vectors = jnp.sum(small[:, 2 * ada : 2 * ada + 4 * part].reshape(devices, 4, part), axis=0)
    all_cond = small[:, 2 * ada + 4 * part :].reshape(2 * devices, -1)
    g_w_ada = lax.dot_general(
        all_cond, all_modul, (((0,), (0,)), ((), ())), precision=lax.Precision.HIGHEST
    )
    g_b_ada = jnp.sum(all_modul, axis=0)

    rows = grad_w_qkv.shape[0] // 2
    mine = lax.dynamic_slice_in_dim(grad_w_qkv, c * rows, rows, 0)
    other = lax.dynamic_slice_in_dim(grad_w_qkv, (1 - c) * rows, rows, 0)
    other = swap(other.astype(BF)).astype(FL)
    low, high = jnp.where(c == 0, mine, other), jnp.where(c == 0, other, mine)
    g_w_qkv = jnp.concatenate(
        [
            half[:, (3 * pair + part) * PAIR : (3 * pair + part + 1) * PAIR]
            for part in range(3)
            for half in (low, high)
            for pair in range(pairs)
        ],
        axis=1,
    )
    moves = [(2 * at + core, chips * core + at) for at in range(chips) for core in range(2)]
    g_w_out = lax.ppermute(grad_w_out.astype(BF), ("batch", "seq", "mp"), moves).astype(FL)
    return (
        output,
        grad_tokens,
        vectors[0],
        g_w_ada,
        g_b_ada,
        vectors[1],
        g_w_qkv,
        g_w_out,
        vectors[2],
        grad_w1,
        grad_b1,
        grad_w2,
        vectors[3],
    )


def solution(mesh):
    in_specs = (
        P(("batch", "mp"), "seq", None),
        P(("batch", "mp")),
        P(("batch", "mp"), "seq"),
        P(("batch", "mp")),
        P(),
        P(),
        P(),
        P(),
        P(),
        P(),
        P(),
        P(None, "mp"),
        P("mp"),
        P("mp", None),
        P(),
        P(("batch", "mp"), "seq", None),
    )
    out_specs = (
        P(("batch", "mp"), "seq", None),
        P(("batch", "mp"), "seq", None),
        P(("batch", "seq", "mp")),
        P(None, ("batch", "seq", "mp")),
        P(("batch", "seq", "mp")),
        P(("batch", "seq", "mp")),
        P(("batch", "seq", "mp"), None),
        P(("batch", "seq", "mp"), None),
        P(("batch", "seq", "mp")),
        P(("batch", "seq"), "mp"),
        P("mp"),
        P("mp", ("batch", "seq")),
        P(("batch", "seq", "mp")),
    )
    return jax.shard_map(
        per_device, mesh=mesh, in_specs=in_specs, out_specs=out_specs, check_vma=False
    )
```
